32 devices in a mesh: dp: 16 (over z, y, x), rep: 2 (over core).
Axes of the slice: x: 2, y: 2, z: 4, core: 2. Of those that a mesh axis runs over, the one named last changes fastest.
Arguments:
- mel: bfloat16 [64, 1024, 80], P('rep', 'dp'), may hold values from -6 to 6
- grad_post: bfloat16 [64, 1024, 80], P('rep', 'dp'), may hold values from -6 to 6
- lengths: int32 [64], replicated, may hold values from 256 to 1024, as said below
- regroup: int32 [2, 32], replicated, may hold values from 0 to 31, each once within a row
- w_first: bfloat16 [5, 512, 80], P(None, 'dp'), may hold values from -0.3125 to 0.3125
- w_mid: bfloat16 [3, 5, 512, 512], P(None, None, 'dp'), may hold values from -0.125 to 0.125
- w_last: bfloat16 [5, 512, 80], P(None, 'dp'), may hold values from -0.125 to 0.125
- gains: float32 [4, 512], replicated, may hold values from 0.1 to 1.9
- shifts: float32 [4, 512], replicated, may hold values from -3 to 3
- gain_last: float32 [80], replicated, may hold values from 0.1 to 1.9
- shift_last: float32 [80], replicated, may hold values from -3 to 3
Outputs:
- mel_post: bfloat16 [64, 1024, 80], P('rep', 'dp')
- grad_mel: bfloat16 [64, 1024, 80], P('rep', 'dp')
- grad_w_first: float32 [5, 512, 80], P(None, 'dp')
- grad_w_mid: float32 [3, 5, 512, 512], P(None, None, 'dp')
- grad_w_last: float32 [5, 512, 80], P(None, 'dp')
- grad_gains: float32 [4, 512], replicated
- grad_shifts: float32 [4, 512], replicated
- grad_gain_last: float32 [80], replicated
- grad_shift_last: float32 [80], replicated
The draws below stay inside these ranges and needn't reach their ends.
Inputs may be any that keep to these rules, and one draw needn't show every extreme that they name: `lengths`: every replica group's 32 utterances include one of exactly 1024 frames.
All inputs are finite; a program needn't handle non-finite values.
Results may differ from the reference program's by a relative error of at most 0.015.
Values may be sent and summed in bfloat16 or wider, within the bound.
A program may use at most 192 MiB of HBM per device.

```python
import jax
import jax.numpy as jnp
from jax import lax

MEL = 80
C = 512
KW = 5
MIDDLE = 3
LEN = 1024
MB = 2
UTT_MB = 1
UTT_DEV = 2
UTT_REP = 32
UTTS = 64
N_DP = 16
N_REP = 2


def draw_lengths(key, part):
    key = jax.random.fold_in(key, 7)
    first_key, second_key = jax.random.split(key)
    group_size = UTT_DEV * N_DP
    drawn = jax.random.randint(first_key, (N_REP, group_size), LEN // 4, LEN + 1)
    chosen = jax.random.randint(second_key, (N_REP, 1), 0, group_size)
    slots = jnp.arange(group_size, dtype=jnp.int32)[None, :]
    return jnp.where(slots == chosen, LEN, drawn).astype(jnp.int32).reshape(-1)


def block_scale(key, shape, cuts, smallest, largest):
    factor_of, own = 1.0, jax.random.fold_in(key, 6)
    for dim, parts in cuts:
        steps = jnp.exp(jax.random.uniform(jax.random.fold_in(own, dim), (parts,), jnp.float32, smallest / len(cuts), largest / len(cuts)))
        factor_of = factor_of * jnp.repeat(steps, shape[dim] // parts).reshape([-1 if axis == dim else 1 for axis in range(len(shape))])
    return factor_of


def bell_draw(stream_key, dims, scale, most, cuts=(), held_as=jnp.bfloat16):
    values = jax.random.normal(stream_key, dims, jnp.float32) * scale
    if len(cuts) > 0:
        values = block_scale(stream_key, dims, cuts, -0.22, 0.18) * values
    return jnp.clip(values, min=-most, max=most).astype(held_as)


def setup_inputs(seed: int = 0) -> dict:
    splits = jax.random.split(jax.random.key(seed), 12)
    mel = bell_draw(splits[0], (UTTS, LEN, MEL), 1.0, 6.0, ((0, 2), (1, 16)))
    grad_post = bell_draw(splits[1], (UTTS, LEN, MEL), 1.0, 6.0, ((0, 2), (1, 16)))
    lengths = draw_lengths(jax.random.fold_in(splits[11], 71), 0)
    regroup = jax.vmap(lambda own: jax.random.permutation(own, UTT_REP))(jax.random.split(splits[3], N_REP)).reshape((N_REP, UTT_REP)).astype(jnp.int32)
    w_first = bell_draw(splits[4], (KW, C, MEL), (KW * MEL) ** -0.5, 0.3125, ((1, 16),))
    w_mid = bell_draw(splits[5], (MIDDLE, KW, C, C), (KW * C) ** -0.5, 0.125, ((2, 16),))
    w_last = bell_draw(splits[6], (KW, C, MEL), (KW * C) ** -0.5, 0.125, ((1, 16),))
    gains = jnp.clip(1.0 + 0.18 * jax.random.normal(splits[7], (MIDDLE + 1, C), jnp.float32), 0.1, 1.9)
    shifts = bell_draw(splits[8], (MIDDLE + 1, C), 0.5, 3.0, (), jnp.float32)
    gain_last = jnp.clip(1.0 + 0.18 * jax.random.normal(splits[9], (MEL,), jnp.float32), 0.1, 1.9)
    shift_last = bell_draw(splits[10], (MEL,), 0.5, 3.0, (), jnp.float32)
    return dict(mel=mel, grad_post=grad_post, lengths=lengths, regroup=regroup, w_first=w_first, w_mid=w_mid, w_last=w_last, gains=gains, shifts=shifts, gain_last=gain_last, shift_last=shift_last)


@jax.custom_vjp
def low(v):
    return lax.optimization_barrier(v.astype(jnp.bfloat16)).astype(jnp.float32)

@jax.custom_vjp
def low_back(v):
    return v

def low_keep(v):
    return (low(v), None)

def low_pass(kept, grad):
    return (grad,)

def back_keep(v):
    return (v, None)

def back_low(kept, grad):
    return (low(grad),)
low.defvjp(low_keep, low_pass)
low_back.defvjp(back_keep, back_low)

def conv_same(hidden, weight):
    taps = weight.shape[0]
    centre = taps // 2
    frames = hidden.shape[1]
    padded = jnp.pad(hidden, ((0, 0), (centre, centre), (0, 0)))
    running = jnp.zeros(hidden.shape[:2] + (weight.shape[2],), jnp.float32)
    for tap_index in range(taps):
        running = running + jnp.einsum('blc,cd->bld', padded[:, tap_index:tap_index + frames], weight[tap_index], precision=lax.Precision.HIGHEST)
    return running

def batch_norm(values, frame_mask, frame_count, gain, shift):
    first_sum = lax.optimization_barrier(jnp.sum(values * frame_mask, axis=(0, 1)))
    second_sum = lax.optimization_barrier(jnp.sum(values * values * frame_mask, axis=(0, 1)))
    centre = first_sum / frame_count
    spread = second_sum / frame_count - centre * centre
    return gain * (values - centre) * lax.rsqrt(spread + 1e-05) + shift

def postnet(mel_b, frame_mask, frame_count, w_first, w_mid, w_last, gains, shifts, gain_last, shift_last):
    hidden = mel_b * frame_mask
    values = low_back(conv_same(hidden, jnp.swapaxes(w_first, 1, 2)))
    hidden = low(frame_mask * jnp.tanh(batch_norm(values, frame_mask, frame_count, gains[0], shifts[0])))
    for layer in range(w_mid.shape[0]):
        values = low_back(conv_same(hidden, w_mid[layer]))
        hidden = low(frame_mask * jnp.tanh(batch_norm(values, frame_mask, frame_count, gains[layer + 1], shifts[layer + 1])))
    values = low_back(conv_same(hidden, w_last))
    return mel_b + frame_mask * batch_norm(values, frame_mask, frame_count, gain_last, shift_last)

def reference(mel, grad_post, lengths, regroup, w_first, w_mid, w_last, gains, shifts, gain_last, shift_last):
    group_size = UTT_DEV * N_DP
    everyone = N_REP * group_size
    offsets = (jnp.arange(N_REP, dtype=jnp.int32) * group_size)[:, None]
    order = (regroup.astype(jnp.int32) + offsets).reshape(-1).astype(jnp.int32)
    inverse = jnp.zeros((everyone,), jnp.int32).at[order].set(jnp.arange(everyone, dtype=jnp.int32))
    frames = jnp.arange(LEN, dtype=jnp.int32)
    valid = (frames[None, :] < lengths[:, None]).astype(jnp.float32)[:, :, None]

    def arrange(values):
        shaped = values[order].reshape(N_REP, N_DP, MB, UTT_MB, LEN, values.shape[-1])
        return jnp.moveaxis(shaped, 2, 0).reshape(MB, N_REP * N_DP * UTT_MB, LEN, values.shape[-1])

    def restore(values):
        shaped = values.reshape(MB, N_REP, N_DP, UTT_MB, LEN, values.shape[-1])
        shaped = jnp.moveaxis(shaped, 0, 2).reshape(everyone, LEN, values.shape[-1])
        return shaped[inverse]
    masks = arrange(valid)
    counts = lax.optimization_barrier(jnp.sum(masks, axis=(1, 2, 3)))

    def forward(mel_f, w_first_f, w_mid_f, w_last_f, gains_f, shifts_f, gain_last_f, shift_last_f):

        def step(carry, inputs):
            mel_b, mask_b, count_b = inputs
            return (carry, postnet(mel_b, mask_b, count_b, w_first_f, w_mid_f, w_last_f, gains_f, shifts_f, gain_last_f, shift_last_f))
        unused, outputs = lax.scan(jax.checkpoint(step), jnp.zeros((), jnp.float32), (arrange(mel_f), masks, counts))
        return restore(outputs)
    result, pullback = jax.vjp(forward, mel.astype(jnp.float32), w_first.astype(jnp.float32), w_mid.astype(jnp.float32), w_last.astype(jnp.float32), gains, shifts, gain_last, shift_last)
    grads = pullback(grad_post.astype(jnp.float32))
    return (result.astype(jnp.bfloat16), grads[0].astype(jnp.bfloat16), grads[1], grads[2], grads[3], grads[4], grads[5], grads[6], grads[7])
```

```python
import functools

import jax
import jax.numpy as jnp
from jax import lax
from jax.experimental import pallas as pl
from jax.experimental.pallas import tpu as pltpu
from jax.sharding import PartitionSpec as P

MB = 2
PLANE = 4
CORES = 2
SUB = 16
LANES = 128
MESH = pl.DeviceIdType.MESH
bf16 = jnp.bfloat16
f32 = jnp.float32
EPS = 1e-05


def nn(a, b):
    return jnp.dot(a, b, preferred_element_type=f32)


def nt(a, b):
    return lax.dot_general(a, b, (((1,), (1,)), ((), ())), preferred_element_type=f32)


def tn(a, b):
    return lax.dot_general(a, b, (((0,), (0,)), ((), ())), preferred_element_type=f32)


def kernel(
    n_dp, utts, frames, chans, mels, taps, middle,
    len_s, reg_s, mel, gpost, wf, wm, wl, gains, shifts, gl, sl,
    o_mel, o_grad, o_wf, o_wm, o_wl, o_gains, o_shifts, o_gl, o_sl,
    mel_s, grd_s, bak_s, bak2_s, mel_r, grd_r, bak_r, bak2_r,
    mel_p, grd_p, mask, h0, h, xh, xl, z, zl, gz, gzl,
    W, WF, WL, rbufs,
    ar_s, ar_r, ar_t, a1, a2, invs, glp, slp, lens,
    ars_sem, arr_sem, a2a_s, a2a_r, gz_s, gz_r, gp_s, gp_r, gq_s, gq_r, gb_s, gb_r,
    r0_s, r0_r, r1_s, r1_r, r2_s, r2_r, r3_s, r3_r, ro_s, ro_r,
):
    nz = n_dp // PLANE
    total = n_dp * CORES
    T = n_dp * frames
    HALO = 2 * SUB
    MT = T // 2
    CL = chans // LANES
    ctile = 32
    dp = lax.axis_index("dp")
    rep = lax.axis_index("rep")
    zc = lax.div(dp, PLANE)
    s = lax.rem(dp, PLANE)
    sx = s + 1 - 2 * lax.rem(s, 2)
    sy = s + 2 - 4 * lax.div(s, 2)
    s1 = sx + rep * (sy - sx)
    s2 = sy + rep * (sx - sy)
    sd = 3 - s
    lin = dp * CORES + rep
    other = 1 - rep
    sib = (dp, other)
    peer1 = (zc * PLANE + s1, rep)
    peer2 = (zc * PLANE + s2, rep)

    def send(src, dst, ss, rs, to):
        pltpu.make_async_remote_copy(
            src_ref=src, dst_ref=dst, send_sem=ss, recv_sem=rs, device_id=to, device_id_type=MESH
        ).start()

    def wait(ref, sem):
        pltpu.make_async_copy(ref, ref, sem).wait()

    W[:, :, zc, s] = wm[...]
    WF[:, zc, s] = jnp.zeros((taps, CORES) + WF.shape[4:], bf16)
    WL[:, zc, s] = jnp.zeros((taps, CORES) + WL.shape[4:], bf16)
    WF[:, zc, s, :, :, 0:mels] = wf[...]
    WL[:, zc, s, :, :, 0:mels] = wl[...]

    barrier = pltpu.get_barrier_semaphore()
    for i in range(1, total):
        to = lax.rem(lin + i, total)
        pl.semaphore_signal(
            barrier, inc=1, device_id=(lax.div(to, CORES), lax.rem(to, CORES)), device_id_type=MESH
        )

    mel_s[...] = jnp.zeros(mel_s.shape, bf16)
    grd_s[...] = jnp.zeros(grd_s.shape, bf16)

    @pl.loop(0, utts)
    def _(k):
        u = reg_s[rep, k]
        mel_s[k, :, 0:mels] = mel[u]
        grd_s[k, :, 0:mels] = gpost[u]

    pl.semaphore_wait(barrier, total - 1)

    def chunk(c):
        if c == 0:
            return WF
        if c == middle + 1:
            return WL
        return W.at[c - 1]

    def g0(c):
        w = chunk(c)
        for i in range(1, nz):
            to = lax.rem(zc + i, nz) * PLANE + s
            piece = w.at[:, zc, s, rep]
            send(piece, piece, gz_s.at[c], gz_r.at[c], (to, rep))

    def three(w):
        return w.at[:, pl.ds(0, nz - 1), 0, 0]

    def g1(c):
        w = chunk(c)
        wait(three(w), gz_r.at[c])
        col = w.at[:, :, s, rep]
        send(col, col, gp_s.at[c], gp_r.at[c], peer1)
        send(col, col, gq_s.at[c], gq_r.at[c], peer2)
        send(col, col, gb_s.at[c], gb_r.at[c], sib)

    def g2(c):
        w = chunk(c)
        wait(w.at[:, :, 0, 0], gp_r.at[c])
        col = w.at[:, :, s1, rep]
        send(col, col, gq_s.at[c], gq_r.at[c], peer2)
        send(col, col, gb_s.at[c], gb_r.at[c], sib)

    def g3(c):
        w = chunk(c)
        wait(w.at[:, :, pl.ds(0, 2), 0], gq_r.at[c])
        for q in (s2, sd):
            col = w.at[:, :, q, rep]
            send(col, col, gb_s.at[c], gb_r.at[c], sib)

    def g4(c):
        wait(chunk(c).at[:, :, :, 0], gb_r.at[c])

    def gdrain(c):
        w = chunk(c)
        wait(three(w), gz_s.at[c])
        wait(w.at[:, :, 0, 0], gp_s.at[c])
        wait(w.at[:, :, pl.ds(0, 2), 0], gq_s.at[c])
        wait(w.at[:, :, :, 0], gb_s.at[c])

    def deal(src, dst, which):
        for i in range(1, n_dp):
            to = lax.rem(dp + i, n_dp)
            send(
                src.at[pl.ds(to * MB, MB)], dst.at[dp], a2a_s.at[which], a2a_r.at[which], (to, rep)
            )
        dst[dp] = src[pl.ds(dp * MB, MB)]

    def dealt(dst, which):
        wait(dst.at[pl.ds(0, n_dp - 1)], a2a_r.at[which])

    def back(src, dst, which):
        for i in range(1, n_dp):
            to = lax.rem(dp + i, n_dp)
            send(
                src.at[to], dst.at[pl.ds(dp * MB, MB)], a2a_s.at[which], a2a_r.at[which], (to, rep)
            )
        dst[pl.ds(dp * MB, MB)] = src[dp]

    def backed(dst, which):
        wait(dst.at[pl.ds(0, utts - MB)], a2a_r.at[which])

    def ar_go(rd, v1, v2):
        n = v1.shape[1] // LANES
        for i in range(CL):
            for base, v in ((0, v1), (CL, v2)):
                if i < n:
                    row = v[:, i * LANES : (i + 1) * LANES]
                else:
                    row = jnp.zeros((1, LANES), f32)
                ar_s[rd, base + i : base + i + 1, :] = row
                ar_r[rd, lin, base + i : base + i + 1, :] = row
        for i in range(1, total):
            to = lax.rem(lin + i, total)
            send(
                ar_s.at[rd], ar_r.at[rd, lin], ars_sem.at[rd], arr_sem.at[rd],
                (lax.div(to, CORES), lax.rem(to, CORES)),
            )

    def ar_get(rd, n):
        wait(ar_r.at[rd, pl.ds(0, total - 1)], arr_sem.at[rd])
        acc = ar_r[rd, 0]
        for i in range(1, total):
            acc = acc + ar_r[rd, i]
        ar_t[...] = acc
        v1 = jnp.concatenate([ar_t[i : i + 1, :] for i in range(n)], axis=1)
        v2 = jnp.concatenate([ar_t[CL + i : CL + i + 1, :] for i in range(n)], axis=1)
        return v1, v2

    def fold(v):
        return jnp.sum(v.reshape(v.shape[0] // 8, 8, v.shape[1]), axis=0)

    def wide(mk, d):
        return jnp.concatenate([mk] * (d // LANES), axis=1) if d > LANES else mk

    def clear(d):
        a1[:, 0:d] = jnp.zeros((8, d), f32)
        a2[:, 0:d] = jnp.zeros((8, d), f32)

    def ar_acc(rd, d):
        ar_go(
            rd,
            jnp.sum(a1[:, 0:d], axis=0, keepdims=True),
            jnp.sum(a2[:, 0:d], axis=0, keepdims=True),
        )

    def halo(ref):
        d = ref.shape[1]
        row = lax.rem(lax.broadcasted_iota(jnp.int32, (HALO, d), 0), SUB)
        low = pltpu.roll(ref[T : T + HALO, :].astype(f32), 1, 0)
        ref[0:HALO, :] = jnp.where(row == 0, 0.0, low).astype(bf16)
        high = pltpu.roll(ref[HALO : 2 * HALO, :].astype(f32), HALO - 1, 0)
        ref[T + HALO : T + 2 * HALO, :] = jnp.where(row == SUB - 1, 0.0, high).astype(bf16)

    cnt = []
    own = []
    for m in range(MB):

        def body(j, c, m=m):
            for r in range(CORES):
                c = c + len_s[r * utts + reg_s[r, j * MB + m]]
            return c

        cnt.append(lax.fori_loop(0, n_dp, body, jnp.int32(0)).astype(f32))
        own.append(len_s[rep * utts + reg_s[rep, dp * MB + m]])

    last = middle + 1

    def mean_inv(rd, m, n):
        v1, v2 = ar_get(rd, n)
        mean = v1 / cnt[m]
        var = v2 / cnt[m] - mean * mean
        inv = lax.rsqrt(var + EPS)
        invs[rd, 0:1, 0 : n * LANES] = inv
        return mean, inv

    def conv(layer, m):
        rd = layer * MB + m
        d = LANES if layer == last else chans
        dst = zl if layer == last else z
        clear(d)

        @pl.loop(0, T // MT)
        def _(t):
            base = pl.multiple_of(t * MT, MT)
            acc = None
            for k in range(taps):
                rows = pl.ds(base + SUB * k, MT)
                if layer == 0:
                    part = nt(h0[m, rows, :], WF[k].reshape(chans, LANES))
                elif layer == last:
                    part = nn(h[layer - 1, m, rows, :], WL[k].reshape(chans, LANES))
                else:
                    part = nn(h[layer - 1, m, rows, :], W[layer - 1, k].reshape(chans, chans))
                acc = part if acc is None else acc + part
            dst[m, pl.ds(base, MT), :] = acc
            zm = acc * wide(mask[m, pl.ds(base, MT), :], d)
            a1[:, 0:d] += fold(zm)
            a2[:, 0:d] += fold(zm * acc)

        ar_acc(rd, d)

    def norm(layer, m):
        mean, inv = mean_inv(layer * MB + m, m, CL)
        g = gains[layer : layer + 1, :]
        b = shifts[layer : layer + 1, :]

        @pl.loop(0, T // ctile)
        def _(i):
            base = pl.multiple_of(i * ctile, ctile)
            rows = pl.ds(base, ctile)
            xv = (z[m, rows, :] - mean) * inv
            hv = wide(mask[m, rows, :], chans) * jnp.tanh(g * xv + b)
            xh[layer, m, rows, :] = xv.astype(bf16)
            h[layer, m, pl.ds(base + HALO, ctile), :] = hv.astype(bf16)

        halo(h.at[layer, m])

    def grad_tail(layer, m, base, acc):
        g = gains[layer : layer + 1, :]
        b = shifts[layer : layer + 1, :]
        rows = pl.ds(base, MT)
        xv = xh[layer, m, rows, :].astype(f32)
        th = jnp.tanh(g * xv + b)
        gy = wide(mask[m, rows, :], chans) * acc * (1.0 - th * th)
        z[m, rows, :] = gy
        a1[...] += fold(gy)
        a2[...] += fold(gy * xv)

    def bround(layer, m):
        return (last + 1 + layer) * MB + m

    def coefs(layer, m, n, g, og, os):
        v1, v2 = ar_get(bround(layer, m), n)
        if m == 0:
            og(v2, False)
            os(v1, False)
        else:
            og(v2, True)
            os(v1, True)
        a = g * invs[layer * MB + m, 0:1, 0 : n * LANES]
        return a, a * v1 / cnt[m], a * v2 / cnt[m]

    def grad_z(layer, m):
        def og(v, add):
            o_gains[layer : layer + 1, :] = v + o_gains[layer : layer + 1, :] if add else v

        def os(v, add):
            o_shifts[layer : layer + 1, :] = v + o_shifts[layer : layer + 1, :] if add else v

        a, c1, c2 = coefs(layer, m, CL, gains[layer : layer + 1, :], og, os)

        @pl.loop(0, T // ctile)
        def _(i):
            base = pl.multiple_of(i * ctile, ctile)
            rows = pl.ds(base, ctile)
            v = a * z[m, rows, :] - c1 - c2 * xh[layer, m, rows, :].astype(f32)
            gz[m, pl.ds(base + HALO, ctile), :] = (wide(mask[m, rows, :], chans) * v).astype(bf16)

        halo(gz.at[m])

    def grad_h(layer, m):
        clear(chans)

        @pl.loop(0, T // MT)
        def _(t):
            base = pl.multiple_of(t * MT, MT)
            acc = None
            for k in range(taps):
                rows = pl.ds(base + SUB * (taps - 1 - k), MT)
                if layer == last:
                    part = nt(gzl[m, rows, :], WL[k].reshape(chans, LANES))
                else:
                    part = nt(gz[m, rows, :], W[layer - 1, k].reshape(chans, chans))
                acc = part if acc is None else acc + part
            grad_tail(layer - 1, m, base, acc)

        ar_acc(bround(layer - 1, m), chans)

    def wgrad(layer):
        gdrain(layer)
        w = chunk(layer)

        @pl.loop(0, taps)
        def _(k):
            if layer == 0:
                rows = pl.ds(pl.multiple_of(SUB * k, SUB), T)
                acc = tn(gz[0, HALO : HALO + T, :], h0[0, rows, :])
                for m in range(1, MB):
                    acc = acc + tn(gz[m, HALO : HALO + T, :], h0[m, rows, :])
            else:
                g = gzl if layer == last else gz
                rows = pl.ds(pl.multiple_of(SUB * (taps - 1 - k), SUB), T)
                acc = tn(h[layer - 1, 0, HALO : HALO + T, :], g[0, rows, :])
                for m in range(1, MB):
                    acc = acc + tn(h[layer - 1, m, HALO : HALO + T, :], g[m, rows, :])
            w[k] = acc.astype(bf16).reshape(w.shape[1:])

        send(w.at[:, :, :, other], rbuf(layer)[0], r0_s.at[layer], r0_r.at[layer], sib)

    def rbuf(layer):
        return rbufs[layer]

    def total_of(a, b):
        return (a.astype(f32) + b.astype(f32)).astype(bf16)

    def ra(layer):
        w = chunk(layer)
        r0, r1 = rbuf(layer)[0:2]
        wait(r0, r0_r.at[layer])
        for k in range(taps):
            r0[k] = total_of(r0[k], w[k, :, :, rep])
        for slot, q in ((1, sd), (0, s2)):
            send(r0.at[:, :, q], r1.at[slot], r1_s.at[layer], r1_r.at[layer], peer2)

    def rb(layer):
        r0, r1, r2 = rbuf(layer)[0:3]
        wait(r1, r1_r.at[layer])
        for slot, q in ((1, s1), (0, s)):
            for k in range(taps):
                r1[slot, k] = total_of(r1[slot, k], r0[k, :, q])
        send(r1.at[1], r2, r2_s.at[layer], r2_r.at[layer], peer1)

    def rc(layer):
        r1, r2, r3 = rbuf(layer)[1:4]
        wait(r2, r2_r.at[layer])
        for k in range(taps):
            r2[k] = total_of(r2[k], r1[0, k])
        for i in range(1, nz):
            zt = lax.rem(zc + i, nz)
            send(
                r2.at[:, zt], r3.at[i - 1], r3_s.at[layer], r3_r.at[layer],
                (zt * PLANE + s, rep),
            )

    def outs(layer):
        return o_wf if layer == 0 else o_wl if layer == last else o_wm.at[layer - 1]

    def rd_(layer):
        r2, r3 = rbuf(layer)[2:4]
        fs, fr = rbuf(layer)[4:6]
        wait(r3, r3_r.at[layer])
        out = outs(layer)
        for k in range(taps):
            v = r2[k, zc].astype(f32)
            for i in range(nz - 1):
                v = v + r3[i, k].astype(f32)
            fs[k] = v
            out[k, rep] = v[:, 0 : out.shape[3]]
        send(fs, fr, ro_s.at[layer], ro_r.at[layer], sib)

    def rdrain(layer):
        r0, r1, r2, r3, fs, fr = rbuf(layer)
        out = outs(layer)
        wait(fr, ro_r.at[layer])
        for k in range(taps):
            out[k, other] = fr[k][:, 0 : out.shape[3]]
        wait(fs, ro_s.at[layer])
        wait(r0, r0_s.at[layer])
        wait(r1, r1_s.at[layer])
        wait(r2, r2_s.at[layer])
        wait(r3, r3_s.at[layer])

    g0(0)
    deal(mel_s, mel_r, 0)
    for c in range(1, last + 1):
        g0(c)
    glp[...] = jnp.zeros(glp.shape, f32)
    slp[...] = jnp.zeros(slp.shape, f32)
    glp[0:1, 0:mels] = gl[...]
    slp[0:1, 0:mels] = sl[...]
    for m in range(MB):

        @pl.loop(0, T // ctile)
        def _(i):
            base = pl.multiple_of(i * ctile, ctile)
            r = base + lax.broadcasted_iota(jnp.int32, (ctile, LANES), 0)
            t = lax.rem(r, SUB) * frames + lax.div(r, SUB)
            mask[m, pl.ds(base, ctile), :] = jnp.where(t < own[m], 1.0, 0.0)

    g1(0)
    g1(1)
    g2(0)
    g2(1)
    g3(0)
    dealt(mel_r, 0)
    for m in range(MB):
        for j in range(n_dp):
            mel_p.at[m][pl.ds(j, frames, stride=SUB), :] = mel_r[j, m].astype(f32)
        h0[m, HALO : HALO + T, :] = (mel_p[m] * mask[m]).astype(bf16)
        halo(h0.at[m])
    g1(2)
    g4(0)
    conv(0, 0)
    g3(1)
    conv(0, 1)
    g2(2)
    g4(1)
    for layer in range(1, last + 1):
        for m in range(MB):
            norm(layer - 1, m)
            conv(layer, m)
            if m == 0:
                if layer + 2 <= last:
                    g1(layer + 2)
            else:
                if layer == 1:
                    deal(grd_s, grd_r, 1)
                if layer + 1 <= last:
                    g3(layer + 1)
                    if layer + 2 <= last:
                        g2(layer + 2)
                    g4(layer + 1)

    dealt(grd_r, 1)
    g_last = glp[0:1, :]
    b_last = slp[0:1, :]
    for m in range(MB):
        for j in range(n_dp):
            grd_p.at[m][pl.ds(j, frames, stride=SUB), :] = grd_r[j, m].astype(f32)
        mean, inv = mean_inv(last * MB + m, m, 1)
        clear(LANES)
        ct = 64

        @pl.loop(0, T // ct)
        def _(i):
            rows = pl.ds(pl.multiple_of(i * ct, ct), ct)
            mk = mask[m, rows, :]
            xv = (zl[m, rows, :] - mean) * inv
            xl[m, rows, :] = xv
            mel_p[m, rows, :] = mel_p[m, rows, :] + mk * (g_last * xv + b_last)
            gy = mk * grd_p[m, rows, :]
            a1[:, 0:LANES] += fold(gy)
            a2[:, 0:LANES] += fold(gy * xv)

        ar_acc(bround(last, m), LANES)
    for m in range(MB):
        for j in range(n_dp):
            bak_s[j, m] = mel_p.at[m][pl.ds(j, frames, stride=SUB), :].astype(bf16)
    back(bak_s, bak_r, 2)
    for m in range(MB):

        def og(v, add):
            v = v[:, 0:mels]
            o_gl[...] = o_gl[...] + v if add else v

        def os(v, add):
            v = v[:, 0:mels]
            o_sl[...] = o_sl[...] + v if add else v

        a, c1, c2 = coefs(last, m, 1, g_last, og, os)
        ct = 64

        @pl.loop(0, T // ct)
        def _(i):
            base = pl.multiple_of(i * ct, ct)
            rows = pl.ds(base, ct)
            v = a * grd_p[m, rows, :] - c1 - c2 * xl[m, rows, :]
            gzl[m, pl.ds(base + HALO, ct), :] = (mask[m, rows, :] * v).astype(bf16)

        halo(gzl.at[m])
        grad_h(last, m)
    wgrad(last)
    for layer in range(middle, 0, -1):
        for m in range(MB):
            grad_z(layer, m)
            grad_h(layer, m)
            if m == 0:
                ra(layer + 1)
                if layer + 2 <= last:
                    rc(layer + 2)
            else:
                rb(layer + 1)
                if layer + 2 <= last:
                    rd_(layer + 2)
        wgrad(layer)
    for m in range(MB):
        grad_z(0, m)

        @pl.loop(0, T // MT)
        def _(t):
            base = pl.multiple_of(t * MT, MT)
            acc = None
            for k in range(taps):
                rows = pl.ds(base + SUB * (taps - 1 - k), MT)
                part = nn(gz[m, rows, :], WF[k].reshape(chans, LANES))
                acc = part if acc is None else acc + part
            rows = pl.ds(base, MT)
            grd_p[m, rows, :] = grd_p[m, rows, :] + mask[m, rows, :] * acc

        if m == 0:
            ra(1)
            rc(2)
        for j in range(n_dp):
            bak2_s[j, m] = grd_p.at[m][pl.ds(j, frames, stride=SUB), :].astype(bf16)
    back(bak2_s, bak2_r, 3)
    wgrad(0)
    rb(1)
    ra(0)
    rd_(2)

    @pl.loop(0, utts)
    def _(u):
        def body(k, c):
            return jnp.where(reg_s[rep, k] == u, k, c)

        lens[u] = lax.fori_loop(0, utts, body, jnp.int32(0))

    backed(bak_r, 2)

    @pl.loop(0, utts)
    def _(u):
        o_mel[u] = bak_r[lens[u], :, 0:mels]

    rc(1)
    rb(0)
    rd_(1)
    rc(0)
    backed(bak2_r, 3)

    @pl.loop(0, utts)
    def _(u):
        o_grad[u] = bak2_r[lens[u], :, 0:mels]

    rd_(0)
    for layer in range(last + 1):
        rdrain(layer)
    wait(mel_r.at[pl.ds(0, n_dp - 1)], a2a_s.at[0])
    wait(grd_r.at[pl.ds(0, n_dp - 1)], a2a_s.at[1])
    wait(bak_r.at[pl.ds(0, utts - MB)], a2a_s.at[2])
    wait(bak2_r.at[pl.ds(0, utts - MB)], a2a_s.at[3])

    @pl.loop(0, 2 * (last + 1) * MB)
    def _(r):
        wait(ar_r.at[r, pl.ds(0, total - 1)], ars_sem.at[r])


def local_kernel(
    mel, grad_post, lengths, regroup, w_first, w_mid, w_last, gains, shifts, gain_last, shift_last
):
    n_dp = lax.axis_size("dp")
    nz = n_dp // PLANE
    utts, frames, mels = mel.shape
    middle, taps, shard, chans = w_mid.shape
    depth = middle + 2
    T = n_dp * frames
    TH = T + 4 * SUB
    rows = shard // CORES
    total = n_dp * CORES
    rounds = 2 * depth * MB
    V = pltpu.VMEM
    D = pltpu.SemaphoreType.DMA
    S = jax.ShapeDtypeStruct
    out_shape = (
        S(mel.shape, bf16),
        S(mel.shape, bf16),
        S((taps, CORES, rows, mels), f32),
        S((middle, taps, CORES, rows, chans), f32),
        S((taps, CORES, rows, mels), f32),
        S(gains.shape, f32),
        S(gains.shape, f32),
        S((1, mels), f32),
        S((1, mels), f32),
    )
    frame_buf = V((utts, frames, LANES), bf16)
    frame_buf2 = V((n_dp, MB, frames, LANES), bf16)
    landing = [
        [
            V((taps, nz, PLANE, rows, d), bf16),
            V((2, taps, nz, rows, d), bf16),
            V((taps, nz, rows, d), bf16),
            V((nz - 1, taps, rows, d), bf16),
            V((taps, rows, d), f32),
            V((taps, rows, d), f32),
        ]
        for d in [LANES] + [chans] * middle + [LANES]
    ]
    scratch = [
        frame_buf, frame_buf, frame_buf2, frame_buf2, frame_buf2, frame_buf2, frame_buf, frame_buf,
        V((MB, T, LANES), f32), V((MB, T, LANES), f32), V((MB, T, LANES), f32),
        V((MB, TH, LANES), bf16), V((middle + 1, MB, TH, chans), bf16),
        V((middle + 1, MB, T, chans), bf16), V((MB, T, LANES), f32),
        V((MB, T, chans), f32), V((MB, T, LANES), f32),
        V((MB, TH, chans), bf16), V((MB, TH, LANES), bf16),
        V((middle, taps, nz, PLANE, CORES, rows, chans), bf16),
        V((taps, nz, PLANE, CORES, rows, LANES), bf16),
        V((taps, nz, PLANE, CORES, rows, LANES), bf16),
        landing,
        V((rounds, 8, LANES), f32), V((rounds, total, 8, LANES), f32), V((8, LANES), f32),
        V((8, chans), f32), V((8, chans), f32), V((depth * MB, 8, chans), f32),
        V((8, LANES), f32), V((8, LANES), f32), pltpu.SMEM((utts,), jnp.int32),
        D((rounds,)), D((rounds,)), D((4,)), D((4,)),
    ] + [D((depth,))] * 18
    body = functools.partial(kernel, n_dp, utts, frames, chans, mels, taps, middle)
    vmem = pl.BlockSpec(memory_space=pltpu.VMEM)
    smem = pl.BlockSpec(memory_space=pltpu.SMEM)
    out = pl.pallas_call(
        body,
        out_shape=out_shape,
        in_specs=[smem, smem] + [vmem] * 9,
        out_specs=(vmem,) * 9,
        scratch_shapes=scratch,
        compiler_params=pltpu.CompilerParams(
            collective_id=0, has_side_effects=True, vmem_limit_bytes=64 * 2**20
        ),
        name="postnet_step",
    )(
        lengths, regroup, mel, grad_post,
        w_first.reshape(taps, CORES, rows, mels),
        w_mid.reshape(middle, taps, CORES, rows, chans),
        w_last.reshape(taps, CORES, rows, mels),
        gains, shifts, gain_last[None, :], shift_last[None, :],
    )
    return (
        out[0], out[1],
        out[2].reshape(w_first.shape), out[3].reshape(w_mid.shape), out[4].reshape(w_last.shape),
        out[5], out[6], out[7][0], out[8][0],
    )


def shortened(value):

    def short(part):
        return part.astype(jnp.bfloat16) if part.dtype == jnp.float32 else part

    return jax.tree.map(short, value)


def shifted(hidden, offset):
    if offset == 0:
        return hidden
    frames = hidden.shape[1]
    reach = abs(offset)
    padded = jnp.pad(hidden, ((0, 0), (reach, reach), (0, 0)))
    return padded[:, reach + offset : reach + offset + frames]


def conv_forward(hidden, weight):
    centre = weight.shape[0] // 2
    running = jnp.einsum(
        "blc,cd->bld", shifted(hidden, -centre), weight[0], preferred_element_type=jnp.float32
    )
    for tap_index in range(1, weight.shape[0]):
        running = running + jnp.einsum(
            "blc,cd->bld",
            shifted(hidden, tap_index - centre),
            weight[tap_index],
            preferred_element_type=jnp.float32,
        )
    return running


def conv_backward(hidden, grad_values, weight):
    centre = weight.shape[0] // 2
    weight_grad = jnp.stack(
        [
            jnp.einsum(
                "blc,bld->cd",
                shifted(hidden, tap_index - centre),
                grad_values,
                preferred_element_type=jnp.float32,
            )
            for tap_index in range(weight.shape[0])
        ]
    )
    hidden_grad = jnp.einsum(
        "bld,cd->blc", shifted(grad_values, centre), weight[0], preferred_element_type=jnp.float32
    )
    for tap_index in range(1, weight.shape[0]):
        hidden_grad = hidden_grad + jnp.einsum(
            "bld,cd->blc",
            shifted(grad_values, centre - tap_index),
            weight[tap_index],
            preferred_element_type=jnp.float32,
        )
    return (weight_grad, hidden_grad)


def normalize(values, frame_mask, frame_count):
    first_sum, second_sum = lax.psum(
        (
            jnp.sum(values * frame_mask, axis=(0, 1)),
            jnp.sum(values * values * frame_mask, axis=(0, 1)),
        ),
        ("dp", "rep"),
    )
    centre = first_sum / frame_count
    spread = second_sum / frame_count - centre * centre
    scale_inv = lax.rsqrt(spread + 1e-05)
    return ((values - centre) * scale_inv, scale_inv)


def norm_backward(grad_out, normed, scale_inv, gain, frame_mask, frame_count):
    shift_grad, gain_grad = lax.psum(
        (jnp.sum(grad_out, axis=(0, 1)), jnp.sum(grad_out * normed, axis=(0, 1))), ("dp", "rep")
    )
    grad_values = (
        gain * scale_inv * (grad_out - shift_grad / frame_count - normed * gain_grad / frame_count)
    )
    return (frame_mask * grad_values, gain_grad, shift_grad)


def layer_list(fetched):
    middle = fetched[1].shape[0]
    return (
        [jnp.swapaxes(fetched[0], 1, 2)]
        + [fetched[1][layer] for layer in range(middle)]
        + [fetched[2]]
    )


def local(
    mel, grad_post, lengths, regroup, w_first, w_mid, w_last, gains, shifts, gain_last, shift_last
):
    devices_dp = lax.axis_size("dp")
    replicas = lax.axis_size("rep")
    dp_index = lax.axis_index("dp")
    rep_index = lax.axis_index("rep")
    group_size = regroup.shape[1]
    utt_dev = group_size // devices_dp
    utt_micro = utt_dev // MB
    frames_all = mel.shape[1] * devices_dp
    middle = w_mid.shape[0]
    offsets = (jnp.arange(replicas, dtype=jnp.int32) * group_size)[:, None]
    lens_order = lengths[(regroup + offsets).reshape(-1)].reshape(
        replicas, devices_dp, MB, utt_micro
    )
    counts = jnp.sum(lens_order, axis=(0, 1, 3)).astype(jnp.float32)
    own_lens = lax.dynamic_index_in_dim(
        lax.dynamic_index_in_dim(lens_order, rep_index, 0, False), dp_index, 0, False
    )
    frame_ids = jnp.arange(frames_all, dtype=jnp.int32)
    masks = (frame_ids[None, None, :] < own_lens[:, :, None]).astype(jnp.float32)[..., None]
    local_order = lax.dynamic_index_in_dim(regroup, rep_index, 0, False)
    moved_mel, moved_grad = (
        lax.all_to_all(mel[local_order], "dp", split_axis=0, concat_axis=1, tiled=True),
        lax.all_to_all(grad_post[local_order], "dp", split_axis=0, concat_axis=1, tiled=True),
    )
    gain_list = [gains[layer] for layer in range(middle + 1)] + [gain_last]
    shift_list = [shifts[layer] for layer in range(middle + 1)] + [shift_last]
    depth = middle + 2
    gain_grads = [jnp.zeros_like(entry) for entry in gain_list]
    shift_grads = [jnp.zeros_like(entry) for entry in shift_list]
    owned = (
        jnp.zeros(w_first.shape, jnp.float32),
        jnp.zeros(w_mid.shape, jnp.float32),
        jnp.zeros(w_last.shape, jnp.float32),
    )
    refined = []
    input_grads = []
    for micro_index in range(MB):
        mel_block = moved_mel[micro_index * utt_micro : (micro_index + 1) * utt_micro]
        grad_block = moved_grad[micro_index * utt_micro : (micro_index + 1) * utt_micro].astype(
            jnp.float32
        )
        frame_mask = masks[micro_index]
        frame_count = counts[micro_index]
        fetched = (
            lax.all_gather(w_first, "dp", axis=1, tiled=True),
            lax.all_gather(w_mid, "dp", axis=2, tiled=True),
            lax.all_gather(w_last, "dp", axis=1, tiled=True),
        )
        weights = layer_list(fetched)
        hidden = (mel_block.astype(jnp.float32) * frame_mask).astype(jnp.bfloat16)
        inputs = []
        kept = []
        for layer in range(depth):
            inputs.append(hidden)
            normed, scale_inv = normalize(
                conv_forward(hidden, weights[layer]), frame_mask, frame_count
            )
            kept.append((normed, scale_inv))
            activated = gain_list[layer] * normed + shift_list[layer]
            if layer < depth - 1:
                hidden = (frame_mask * jnp.tanh(activated)).astype(jnp.bfloat16)
            else:
                refined.append(
                    (mel_block.astype(jnp.float32) + frame_mask * activated).astype(jnp.bfloat16)
                )
        fetched = (
            lax.all_gather(w_first, "dp", axis=1, tiled=True),
            lax.all_gather(w_mid, "dp", axis=2, tiled=True),
            lax.all_gather(w_last, "dp", axis=1, tiled=True),
        )
        weights = layer_list(fetched)
        grad_out = frame_mask * grad_block
        weight_grads = [None] * depth
        for layer in reversed(range(depth)):
            normed, scale_inv = kept[layer]
            grad_values, gain_grad, shift_grad = norm_backward(
                grad_out, normed, scale_inv, gain_list[layer], frame_mask, frame_count
            )
            gain_grads[layer] = gain_grads[layer] + gain_grad
            shift_grads[layer] = shift_grads[layer] + shift_grad
            weight_grad, hidden_grad = conv_backward(
                inputs[layer], grad_values.astype(jnp.bfloat16), weights[layer]
            )
            weight_grads[layer] = weight_grad
            if layer > 0:
                before = kept[layer - 1]
                activated = jnp.tanh(gain_list[layer - 1] * before[0] + shift_list[layer - 1])
                grad_out = frame_mask * hidden_grad * (1.0 - activated * activated)
            else:
                input_grads.append((grad_block + frame_mask * hidden_grad).astype(jnp.bfloat16))
        local_grads = (
            jnp.swapaxes(weight_grads[0], 1, 2),
            jnp.stack(weight_grads[1 : depth - 1]),
            weight_grads[depth - 1],
        )
        pieces = (
            lax.psum_scatter(local_grads[0], "dp", scatter_dimension=1, tiled=True),
            lax.psum_scatter(local_grads[1], "dp", scatter_dimension=2, tiled=True),
            lax.psum_scatter(local_grads[2], "dp", scatter_dimension=1, tiled=True),
        )
        owned = tuple((total + piece for total, piece in zip(owned, pieces)))
    final_first, final_mid, final_last = jax.tree.map(
        lambda part: part.astype(jnp.float32), lax.psum(shortened(owned), "rep")
    )
    back_mel, back_grad = (
        lax.all_to_all(
            jnp.concatenate(refined, axis=0), "dp", split_axis=1, concat_axis=0, tiled=True
        ),
        lax.all_to_all(
            jnp.concatenate(input_grads, axis=0), "dp", split_axis=1, concat_axis=0, tiled=True
        ),
    )
    inverse = (
        jnp.zeros((group_size,), jnp.int32)
        .at[local_order]
        .set(jnp.arange(group_size, dtype=jnp.int32))
    )
    return (
        back_mel[inverse],
        back_grad[inverse],
        final_first,
        final_mid,
        final_last,
        jnp.stack(gain_grads[: depth - 1]),
        jnp.stack(shift_grads[: depth - 1]),
        gain_grads[depth - 1],
        shift_grads[depth - 1],
    )


def solution(mesh):
    in_specs = (
        P("rep", "dp", None),
        P("rep", "dp", None),
        P(),
        P(),
        P(None, "dp", None),
        P(None, None, "dp", None),
        P(None, "dp", None),
        P(),
        P(),
        P(),
        P(),
    )
    out_specs = (
        P("rep", "dp", None),
        P("rep", "dp", None),
        P(None, "dp", None),
        P(None, None, "dp", None),
        P(None, "dp", None),
        P(),
        P(),
        P(),
        P(),
    )
    step = local_kernel if mesh.shape["dp"] == SUB and mesh.shape["rep"] == CORES else local
    return jax.shard_map(step, mesh=mesh, in_specs=in_specs, out_specs=out_specs, check_vma=False)
```

```python
import functools

import jax
import jax.numpy as jnp
from jax import lax
from jax.experimental import pallas as pl
from jax.experimental.pallas import tpu as pltpu
from jax.sharding import PartitionSpec as P

MB = 2
PLANE = 4
CORES = 2
SUB = 16
LANES = 128
MESH = pl.DeviceIdType.MESH
bf16 = jnp.bfloat16
f32 = jnp.float32
EPS = 1e-05


def nn(a, b):
    return jnp.dot(a, b, preferred_element_type=f32)


def nt(a, b):
    return lax.dot_general(a, b, (((1,), (1,)), ((), ())), preferred_element_type=f32)


def tn(a, b):
    return lax.dot_general(a, b, (((0,), (0,)), ((), ())), preferred_element_type=f32)


def kernel(
    n_dp, utts, frames, chans, mels, taps, middle,
    len_s, reg_s, mel, gpost, wf, wm, wl, gains, shifts, gl, sl,
    o_mel, o_grad, o_wf, o_wm, o_wl, o_gains, o_shifts, o_gl, o_sl,
    mel_s, grd_s, bak_s, bak2_s, mel_r, grd_r, bak_r, bak2_r,
    mel_p, grd_p, mask, h0, h, xh, z, zl, gz, gzl,
    W, WF, WL, GF, G1, rbufs,
    ar_s, ar_r, ar_t, a1, a2, a3, a4, invs, glp, slp, lens,
    ars_sem, arr_sem, a2a_s, a2a_r, gz_s, gz_r, gp_s, gp_r, gq_s, gq_r, gb_s, gb_r,
    r0_s, r0_r, r1_s, r1_r, r2_s, r2_r, r3_s, r3_r, ro_s, ro_r,
):
    nz = n_dp // PLANE
    total = n_dp * CORES
    T = n_dp * frames
    HALO = 2 * SUB
    MT = T // 2
    CL = chans // LANES
    ctile = 32
    dp = lax.axis_index("dp")
    rep = lax.axis_index("rep")
    zc = lax.div(dp, PLANE)
    s = lax.rem(dp, PLANE)
    sx = s + 1 - 2 * lax.rem(s, 2)
    sy = s + 2 - 4 * lax.div(s, 2)
    s1 = sx + rep * (sy - sx)
    s2 = sy + rep * (sx - sy)
    sd = 3 - s
    lin = dp * CORES + rep
    other = 1 - rep
    sib = (dp, other)
    peer1 = (zc * PLANE + s1, rep)
    peer2 = (zc * PLANE + s2, rep)

    def send(src, dst, ss, rs, to):
        pltpu.make_async_remote_copy(
            src_ref=src, dst_ref=dst, send_sem=ss, recv_sem=rs, device_id=to, device_id_type=MESH
        ).start()

    def wait(ref, sem):
        pltpu.make_async_copy(ref, ref, sem).wait()

    W[:, :, zc, s] = wm[...]
    WF[:, zc, s] = jnp.zeros((taps, CORES) + WF.shape[4:], bf16)
    WL[:, zc, s] = jnp.zeros((taps, CORES) + WL.shape[4:], bf16)
    WF[:, zc, s, :, :, 0:mels] = wf[...]
    WL[:, zc, s, :, :, 0:mels] = wl[...]

    barrier = pltpu.get_barrier_semaphore()
    for i in range(1, total):
        to = lax.rem(lin + i, total)
        pl.semaphore_signal(
            barrier, inc=1, device_id=(lax.div(to, CORES), lax.rem(to, CORES)), device_id_type=MESH
        )

    mel_s[...] = jnp.zeros(mel_s.shape, bf16)
    grd_s[...] = jnp.zeros(grd_s.shape, bf16)

    @pl.loop(0, utts)
    def _(k):
        u = reg_s[rep, k]
        mel_s[k, :, 0:mels] = mel[u]
        grd_s[k, :, 0:mels] = gpost[u]

    pl.semaphore_wait(barrier, total - 1)

    def chunk(c):
        if c == 0:
            return WF
        if c == middle + 1:
            return WL
        return W.at[c - 1]

    def g0(c):
        w = chunk(c)
        for i in range(1, nz):
            to = lax.rem(zc + i, nz) * PLANE + s
            piece = w.at[:, zc, s, rep]
            send(piece, piece, gz_s.at[c], gz_r.at[c], (to, rep))

    def three(w):
        return w.at[:, pl.ds(0, nz - 1), 0, 0]

    def g1(c):
        w = chunk(c)
        wait(three(w), gz_r.at[c])
        col = w.at[:, :, s, rep]
        send(col, col, gp_s.at[c], gp_r.at[c], peer1)
        send(col, col, gq_s.at[c], gq_r.at[c], peer2)
        send(col, col, gb_s.at[c], gb_r.at[c], sib)

    def g2(c):
        w = chunk(c)
        wait(w.at[:, :, 0, 0], gp_r.at[c])
        col = w.at[:, :, s1, rep]
        send(col, col, gq_s.at[c], gq_r.at[c], peer2)
        send(col, col, gb_s.at[c], gb_r.at[c], sib)

    def g3(c):
        w = chunk(c)
        wait(w.at[:, :, pl.ds(0, 2), 0], gq_r.at[c])
        for q in (s2, sd):
            col = w.at[:, :, q, rep]
            send(col, col, gb_s.at[c], gb_r.at[c], sib)

    def g4(c):
        wait(chunk(c).at[:, :, :, 0], gb_r.at[c])

    def gdrain(c):
        w = chunk(c)
        wait(three(w), gz_s.at[c])
        wait(w.at[:, :, 0, 0], gp_s.at[c])
        wait(w.at[:, :, pl.ds(0, 2), 0], gq_s.at[c])
        wait(w.at[:, :, :, 0], gb_s.at[c])

    def deal(src, dst, which):
        for i in range(1, n_dp):
            to = lax.rem(dp + i, n_dp)
            send(
                src.at[pl.ds(to * MB, MB)], dst.at[dp], a2a_s.at[which], a2a_r.at[which], (to, rep)
            )
        dst[dp] = src[pl.ds(dp * MB, MB)]

    def dealt(dst, which):
        wait(dst.at[pl.ds(0, n_dp - 1)], a2a_r.at[which])

    def back(src, dst, which):
        for i in range(1, n_dp):
            to = lax.rem(dp + i, n_dp)
            send(
                src.at[to], dst.at[pl.ds(dp * MB, MB)], a2a_s.at[which], a2a_r.at[which], (to, rep)
            )
        dst[pl.ds(dp * MB, MB)] = src[dp]

    def backed(dst, which):
        wait(dst.at[pl.ds(0, utts - MB)], a2a_r.at[which])

    def ar_go(rd, vs):
        n = 8 // len(vs)
        for q, v in enumerate(vs):
            for i in range(n):
                if (i + 1) * LANES <= v.shape[1]:
                    row = v[:, i * LANES : (i + 1) * LANES]
                else:
                    row = jnp.zeros((1, LANES), f32)
                at = q * n + i
                ar_s[rd, at : at + 1, :] = row
                ar_r[rd, lin, at : at + 1, :] = row
        for i in range(1, total):
            to = lax.rem(lin + i, total)
            send(
                ar_s.at[rd], ar_r.at[rd, lin], ars_sem.at[rd], arr_sem.at[rd],
                (lax.div(to, CORES), lax.rem(to, CORES)),
            )

    def ar_get(rd, n):
        wait(ar_r.at[rd, pl.ds(0, total - 1)], arr_sem.at[rd])
        acc = ar_r[rd, 0]
        for i in range(1, total):
            acc = acc + ar_r[rd, i]
        ar_t[...] = acc
        q = CL if n == CL else 2
        return [
            jnp.concatenate([ar_t[e * q + i : e * q + i + 1, :] for i in range(n)], axis=1)
            for e in range(8 // q)
        ]

    def fold(v):
        return jnp.sum(v.reshape(v.shape[0] // 8, 8, v.shape[1]), axis=0)

    def wide(mk, d):
        return jnp.concatenate([mk] * (d // LANES), axis=1) if d > LANES else mk

    def clear(d):
        a1[:, 0:d] = jnp.zeros((8, d), f32)
        a2[:, 0:d] = jnp.zeros((8, d), f32)
        if d == LANES:
            a3[...] = jnp.zeros((8, d), f32)
            a4[...] = jnp.zeros((8, d), f32)

    def ar_acc(rd, d):
        accs = (a1, a2, a3, a4) if d == LANES else (a1, a2)
        ar_go(rd, [jnp.sum(v[:, 0:d], axis=0, keepdims=True) for v in accs])

    def halo(ref):
        d = ref.shape[1]
        row = lax.rem(lax.broadcasted_iota(jnp.int32, (HALO, d), 0), SUB)
        low = pltpu.roll(ref[T : T + HALO, :].astype(f32), 1, 0)
        ref[0:HALO, :] = jnp.where(row == 0, 0.0, low).astype(bf16)
        high = pltpu.roll(ref[HALO : 2 * HALO, :].astype(f32), HALO - 1, 0)
        ref[T + HALO : T + 2 * HALO, :] = jnp.where(row == SUB - 1, 0.0, high).astype(bf16)

    cnt = []
    own = []
    for m in range(MB):

        def body(j, c, m=m):
            for r in range(CORES):
                c = c + len_s[r * utts + reg_s[r, j * MB + m]]
            return c

        cnt.append(lax.fori_loop(0, n_dp, body, jnp.int32(0)).astype(f32))
        own.append(len_s[rep * utts + reg_s[rep, dp * MB + m]])

    last = middle + 1

    def mean_inv(rd, m, n):
        v1, v2 = ar_get(rd, n)
        mean = v1 / cnt[m]
        var = v2 / cnt[m] - mean * mean
        inv = lax.rsqrt(var + EPS)
        invs[rd, 0:1, 0 : n * LANES] = inv
        return mean, inv

    def conv(layer, m):
        rd = layer * MB + m
        d = LANES if layer == last else chans
        dst = zl if layer == last else z
        clear(d)

        @pl.loop(0, T // MT)
        def _(t):
            base = pl.multiple_of(t * MT, MT)
            acc = None
            for k in range(taps):
                rows = pl.ds(base + SUB * k, MT)
                if layer == 0:
                    part = nt(h0[m, rows, :], WF[k].reshape(chans, LANES))
                elif layer == last:
                    part = nn(h[layer - 1, m, rows, :], WL[k].reshape(chans, LANES))
                else:
                    part = nn(h[layer - 1, m, rows, :], W[layer - 1, k].reshape(chans, chans))
                acc = part if acc is None else acc + part
            dst[m, pl.ds(base, MT), :] = acc
            zm = acc * wide(mask[m, pl.ds(base, MT), :], d)
            a1[:, 0:d] += fold(zm)
            a2[:, 0:d] += fold(zm * acc)
            if layer == last:
                gy = mask[m, pl.ds(base, MT), :] * grd_p[m, pl.ds(base, MT), :]
                a3[...] += fold(gy)
                a4[...] += fold(gy * acc)

        ar_acc(rd, d)

    def norm(layer, m):
        mean, inv = mean_inv(layer * MB + m, m, CL)
        g = gains[layer : layer + 1, :]
        b = shifts[layer : layer + 1, :]

        @pl.loop(0, T // ctile)
        def _(i):
            base = pl.multiple_of(i * ctile, ctile)
            rows = pl.ds(base, ctile)
            xv = (z[m, rows, :] - mean) * inv
            hv = wide(mask[m, rows, :], chans) * jnp.tanh(g * xv + b)
            xh[layer, m, rows, :] = xv.astype(bf16)
            h[layer, m, pl.ds(base + HALO, ctile), :] = hv.astype(bf16)

        halo(h.at[layer, m])

    def grad_tail(layer, m, base, acc):
        g = gains[layer : layer + 1, :]
        b = shifts[layer : layer + 1, :]
        rows = pl.ds(base, MT)
        xv = xh[layer, m, rows, :].astype(f32)
        th = jnp.tanh(g * xv + b)
        gy = wide(mask[m, rows, :], chans) * acc * (1.0 - th * th)
        z[m, rows, :] = gy
        a1[...] += fold(gy)
        a2[...] += fold(gy * xv)

    def bround(layer, m):
        return (last + 1 + layer) * MB + m

    def coefs(layer, m, n, g, og, os):
        v1, v2 = ar_get(bround(layer, m), n)
        og(v2, m > 0)
        os(v1, m > 0)
        a = g * invs[layer * MB + m, 0:1, 0 : n * LANES]
        return a, a * v1 / cnt[m], a * v2 / cnt[m]

    def grad_z(layer, m):
        def og(v, add):
            o_gains[layer : layer + 1, :] = v + o_gains[layer : layer + 1, :] if add else v

        def os(v, add):
            o_shifts[layer : layer + 1, :] = v + o_shifts[layer : layer + 1, :] if add else v

        a, c1, c2 = coefs(layer, m, CL, gains[layer : layer + 1, :], og, os)

        @pl.loop(0, T // ctile)
        def _(i):
            base = pl.multiple_of(i * ctile, ctile)
            rows = pl.ds(base, ctile)
            v = a * z[m, rows, :] - c1 - c2 * xh[layer, m, rows, :].astype(f32)
            gz[m, pl.ds(base + HALO, ctile), :] = (wide(mask[m, rows, :], chans) * v).astype(bf16)

        halo(gz.at[m])

    def grad_h(layer, m):
        clear(chans)

        @pl.loop(0, T // MT)
        def _(t):
            base = pl.multiple_of(t * MT, MT)
            acc = None
            for k in range(taps):
                rows = pl.ds(base + SUB * (taps - 1 - k), MT)
                if layer == last:
                    part = nt(gzl[m, rows, :], WL[k].reshape(chans, LANES))
                else:
                    part = nt(gz[m, rows, :], W[layer - 1, k].reshape(chans, chans))
                acc = part if acc is None else acc + part
            grad_tail(layer - 1, m, base, acc)

        ar_acc(bround(layer - 1, m), chans)

    def gchunk(layer):
        return GF if layer == 0 else G1 if layer == 1 else chunk(layer)

    def wgrad(layer):
        gdrain(layer)
        w = gchunk(layer)

        @pl.loop(0, taps)
        def _(k):
            if layer == 0:
                rows = pl.ds(pl.multiple_of(SUB * k, SUB), T)
                acc = tn(gz[0, HALO : HALO + T, :], h0[0, rows, :])
                for m in range(1, MB):
                    acc = acc + tn(gz[m, HALO : HALO + T, :], h0[m, rows, :])
            else:
                g = gzl if layer == last else gz
                rows = pl.ds(pl.multiple_of(SUB * (taps - 1 - k), SUB), T)
                acc = tn(h[layer - 1, 0, HALO : HALO + T, :], g[0, rows, :])
                for m in range(1, MB):
                    acc = acc + tn(h[layer - 1, m, HALO : HALO + T, :], g[m, rows, :])
            w[k] = acc.astype(bf16).reshape(w.shape[1:])

        send(w.at[:, :, :, other], rbuf(layer)[0], r0_s.at[layer], r0_r.at[layer], sib)

    def rbuf(layer):
        return rbufs[layer]

    def total_of(a, b):
        return (a.astype(f32) + b.astype(f32)).astype(bf16)

    def ra(layer):
        w = gchunk(layer)
        r0, r1 = rbuf(layer)[0:2]
        wait(r0, r0_r.at[layer])
        for k in range(taps):
            r0[k] = total_of(r0[k], w[k, :, :, rep])
        for slot, q in ((1, sd), (0, s2)):
            send(r0.at[:, :, q], r1.at[slot], r1_s.at[layer], r1_r.at[layer], peer2)

    def rb(layer):
        r0, r1, r2 = rbuf(layer)[0:3]
        wait(r1, r1_r.at[layer])
        for slot, q in ((1, s1), (0, s)):
            for k in range(taps):
                r1[slot, k] = total_of(r1[slot, k], r0[k, :, q])
        send(r1.at[1], r2, r2_s.at[layer], r2_r.at[layer], peer1)

    def rc(layer):
        r1, r2, r3 = rbuf(layer)[1:4]
        wait(r2, r2_r.at[layer])
        for k in range(taps):
            r2[k] = total_of(r2[k], r1[0, k])
        for i in range(1, nz):
            zt = lax.rem(zc + i, nz)
            send(
                r2.at[:, zt], r3.at[i - 1], r3_s.at[layer], r3_r.at[layer],
                (zt * PLANE + s, rep),
            )

    def outs(layer):
        return o_wf if layer == 0 else o_wl if layer == last else o_wm.at[layer - 1]

    def rd_(layer):
        r2, r3 = rbuf(layer)[2:4]
        fs, fr = rbuf(layer)[4:6]
        wait(r3, r3_r.at[layer])
        out = outs(layer)
        for k in range(taps):
            v = r2[k, zc].astype(f32)
            for i in range(nz - 1):
                v = v + r3[i, k].astype(f32)
            fs[k] = v
            out[k, rep] = v[:, 0 : out.shape[3]]
        send(fs, fr, ro_s.at[layer], ro_r.at[layer], sib)

    def rdrain(layer):
        r0, r1, r2, r3, fs, fr = rbuf(layer)
        out = outs(layer)
        wait(fr, ro_r.at[layer])
        for k in range(taps):
            out[k, other] = fr[k][:, 0 : out.shape[3]]
        wait(fs, ro_s.at[layer])
        wait(r0, r0_s.at[layer])
        wait(r1, r1_s.at[layer])
        wait(r2, r2_s.at[layer])
        wait(r3, r3_s.at[layer])

    g0(0)
    g0(1)
    deal(mel_s, mel_r, 0)
    g0(2)
    glp[...] = jnp.zeros(glp.shape, f32)
    slp[...] = jnp.zeros(slp.shape, f32)
    glp[0:1, 0:mels] = gl[...]
    slp[0:1, 0:mels] = sl[...]
    for m in range(MB):

        @pl.loop(0, T // ctile)
        def _(i):
            base = pl.multiple_of(i * ctile, ctile)
            r = base + lax.broadcasted_iota(jnp.int32, (ctile, LANES), 0)
            t = lax.rem(r, SUB) * frames + lax.div(r, SUB)
            mask[m, pl.ds(base, ctile), :] = jnp.where(t < own[m], 1.0, 0.0)

    g1(0)
    g2(0)
    g3(0)
    g1(1)

    @pl.loop(0, utts)
    def _(u):
        def body(k, c):
            return jnp.where(reg_s[rep, k] == u, k, c)

        lens[u] = lax.fori_loop(0, utts, body, jnp.int32(0))

    dealt(mel_r, 0)
    for m in range(MB):
        for j in range(n_dp):
            mel_p.at[m][pl.ds(j, frames, stride=SUB), :] = mel_r[j, m].astype(f32)
        h0[m, HALO : HALO + T, :] = (mel_p[m] * mask[m]).astype(bf16)
        halo(h0.at[m])
        if m == 0:
            g4(0)
        conv(0, m)
        if m == 0:
            g2(1)
    g1(2)
    g0(3)
    for layer in range(1, last + 1):
        g3(layer)
        g4(layer)
        for m in range(MB):
            norm(layer - 1, m)
            if layer == last:
                if m == 0:
                    dealt(grd_r, 1)
                for j in range(n_dp):
                    grd_p.at[m][pl.ds(j, frames, stride=SUB), :] = grd_r[j, m].astype(f32)
            conv(layer, m)
            if m == 0:
                if layer + 1 <= last:
                    g2(layer + 1)
            else:
                if layer + 2 <= last:
                    g1(layer + 2)
                if layer + 3 <= last:
                    g0(layer + 3)
                if layer == 2:
                    deal(grd_s, grd_r, 1)

    g_last = glp[0:1, :]
    b_last = slp[0:1, :]
    ct = 64
    for m in range(MB):
        tot = ar_get(last * MB + m, 1)
        mean = tot[0] / cnt[m]
        var = tot[1] / cnt[m] - mean * mean
        inv = lax.rsqrt(var + EPS)
        v1 = tot[2]
        v2 = inv * (tot[3] - mean * v1)
        if m == 0:
            o_gl[...] = v2[:, 0:mels]
            o_sl[...] = v1[:, 0:mels]
        else:
            o_gl[...] = o_gl[...] + v2[:, 0:mels]
            o_sl[...] = o_sl[...] + v1[:, 0:mels]
        a = g_last * inv
        c1 = a * v1 / cnt[m]
        c2 = a * v2 / cnt[m]

        @pl.loop(0, T // ct)
        def _(i):
            base = pl.multiple_of(i * ct, ct)
            rows = pl.ds(base, ct)
            mk = mask[m, rows, :]
            xv = (zl[m, rows, :] - mean) * inv
            mel_p[m, rows, :] = mel_p[m, rows, :] + mk * (g_last * xv + b_last)
            v = a * grd_p[m, rows, :] - c1 - c2 * xv
            gzl[m, pl.ds(base + HALO, ct), :] = (mk * v).astype(bf16)

        halo(gzl.at[m])
        grad_h(last, m)
    wgrad(last)
    for m in range(MB):
        for j in range(n_dp):
            bak_s[j, m] = mel_p.at[m][pl.ds(j, frames, stride=SUB), :].astype(bf16)
    back(bak_s, bak_r, 2)
    for layer in range(middle, 1, -1):
        for m in range(MB):
            grad_z(layer, m)
            grad_h(layer, m)
            if m == 0:
                ra(layer + 1)
                if layer + 2 <= last:
                    rc(layer + 2)
        wgrad(layer)
        rb(layer + 1)
        if layer + 2 <= last:
            rd_(layer + 2)
    for m in range(MB):
        grad_z(1, m)
    wgrad(1)
    ra(2)
    rc(3)
    grad_h(1, 0)
    rb(2)
    rd_(3)
    grad_h(1, 1)
    ra(1)
    backed(bak_r, 2)

    @pl.loop(0, utts)
    def _(u):
        o_mel[u] = bak_r[lens[u], :, 0:mels]

    for m in range(MB):
        grad_z(0, m)
    wgrad(0)
    rc(2)
    for m in range(MB):

        @pl.loop(0, T // MT)
        def _(t):
            base = pl.multiple_of(t * MT, MT)
            acc = None
            for k in range(taps):
                rows = pl.ds(base + SUB * (taps - 1 - k), MT)
                part = nn(gz[m, rows, :], WF[k].reshape(chans, LANES))
                acc = part if acc is None else acc + part
            rows = pl.ds(base, MT)
            grd_p[m, rows, :] = grd_p[m, rows, :] + mask[m, rows, :] * acc

        for j in range(n_dp):
            bak2_s[j, m] = grd_p.at[m][pl.ds(j, frames, stride=SUB), :].astype(bf16)
        if m == 0:
            rb(1)
            ra(0)
    back(bak2_s, bak2_r, 3)
    rb(0)
    rd_(2)
    rc(1)
    rc(0)
    rd_(1)
    rd_(0)
    backed(bak2_r, 3)

    @pl.loop(0, utts)
    def _(u):
        o_grad[u] = bak2_r[lens[u], :, 0:mels]

    for layer in reversed(range(last + 1)):
        rdrain(layer)
    wait(mel_r.at[pl.ds(0, n_dp - 1)], a2a_s.at[0])
    wait(grd_r.at[pl.ds(0, n_dp - 1)], a2a_s.at[1])
    wait(bak_r.at[pl.ds(0, utts - MB)], a2a_s.at[2])
    wait(bak2_r.at[pl.ds(0, utts - MB)], a2a_s.at[3])

    @pl.loop(0, (2 * last + 1) * MB)
    def _(r):
        wait(ar_r.at[r, pl.ds(0, total - 1)], ars_sem.at[r])


def local_kernel(
    mel, grad_post, lengths, regroup, w_first, w_mid, w_last, gains, shifts, gain_last, shift_last
):
    n_dp = lax.axis_size("dp")
    nz = n_dp // PLANE
    utts, frames, mels = mel.shape
    middle, taps, shard, chans = w_mid.shape
    depth = middle + 2
    T = n_dp * frames
    TH = T + 4 * SUB
    rows = shard // CORES
    total = n_dp * CORES
    rounds = (2 * depth - 1) * MB
    V = pltpu.VMEM
    D = pltpu.SemaphoreType.DMA
    S = jax.ShapeDtypeStruct
    out_shape = (
        S(mel.shape, bf16),
        S(mel.shape, bf16),
        S((taps, CORES, rows, mels), f32),
        S((middle, taps, CORES, rows, chans), f32),
        S((taps, CORES, rows, mels), f32),
        S(gains.shape, f32),
        S(gains.shape, f32),
        S((1, mels), f32),
        S((1, mels), f32),
    )
    frame_buf = V((utts, frames, LANES), bf16)
    frame_buf2 = V((n_dp, MB, frames, LANES), bf16)
    landing = [
        [
            V((taps, nz, PLANE, rows, d), bf16),
            V((2, taps, nz, rows, d), bf16),
            V((taps, nz, rows, d), bf16),
            V((nz - 1, taps, rows, d), bf16),
            V((taps, rows, d), f32),
            V((taps, rows, d), f32),
        ]
        for d in [LANES] + [chans] * middle + [LANES]
    ]
    scratch = [
        frame_buf, frame_buf, frame_buf2, frame_buf2, frame_buf2, frame_buf2, frame_buf, frame_buf,
        V((MB, T, LANES), f32), V((MB, T, LANES), f32), V((MB, T, LANES), f32),
        V((MB, TH, LANES), bf16), V((middle + 1, MB, TH, chans), bf16),
        V((middle + 1, MB, T, chans), bf16),
        V((MB, T, chans), f32), V((MB, T, LANES), f32),
        V((MB, TH, chans), bf16), V((MB, TH, LANES), bf16),
        V((middle, taps, nz, PLANE, CORES, rows, chans), bf16),
        V((taps, nz, PLANE, CORES, rows, LANES), bf16),
        V((taps, nz, PLANE, CORES, rows, LANES), bf16),
        V((taps, nz, PLANE, CORES, rows, LANES), bf16),
        V((taps, nz, PLANE, CORES, rows, chans), bf16),
        landing,
        V((rounds, 8, LANES), f32), V((rounds, total, 8, LANES), f32), V((8, LANES), f32),
        V((8, chans), f32), V((8, chans), f32), V((8, LANES), f32), V((8, LANES), f32), V((depth * MB, 8, chans), f32),
        V((8, LANES), f32), V((8, LANES), f32), pltpu.SMEM((utts,), jnp.int32),
        D((rounds,)), D((rounds,)), D((4,)), D((4,)),
    ] + [D((depth,))] * 18
    body = functools.partial(kernel, n_dp, utts, frames, chans, mels, taps, middle)
    vmem = pl.BlockSpec(memory_space=pltpu.VMEM)
    smem = pl.BlockSpec(memory_space=pltpu.SMEM)
    out = pl.pallas_call(
        body,
        out_shape=out_shape,
        in_specs=[smem, smem] + [vmem] * 9,
        out_specs=(vmem,) * 9,
        scratch_shapes=scratch,
        compiler_params=pltpu.CompilerParams(
            collective_id=0, has_side_effects=True, vmem_limit_bytes=64 * 2**20
        ),
        name="postnet_step",
    )(
        lengths, regroup, mel, grad_post,
        w_first.reshape(taps, CORES, rows, mels),
        w_mid.reshape(middle, taps, CORES, rows, chans),
        w_last.reshape(taps, CORES, rows, mels),
        gains, shifts, gain_last[None, :], shift_last[None, :],
    )
    return (
        out[0], out[1],
        out[2].reshape(w_first.shape), out[3].reshape(w_mid.shape), out[4].reshape(w_last.shape),
        out[5], out[6], out[7][0], out[8][0],
    )


def shortened(value):

    def short(part):
        return part.astype(jnp.bfloat16) if part.dtype == jnp.float32 else part

    return jax.tree.map(short, value)


def shifted(hidden, offset):
    if offset == 0:
        return hidden
    frames = hidden.shape[1]
    reach = abs(offset)
    padded = jnp.pad(hidden, ((0, 0), (reach, reach), (0, 0)))
    return padded[:, reach + offset : reach + offset + frames]


def conv_forward(hidden, weight):
    centre = weight.shape[0] // 2
    running = jnp.einsum(
        "blc,cd->bld", shifted(hidden, -centre), weight[0], preferred_element_type=jnp.float32
    )
    for tap_index in range(1, weight.shape[0]):
        running = running + jnp.einsum(
            "blc,cd->bld",
            shifted(hidden, tap_index - centre),
            weight[tap_index],
            preferred_element_type=jnp.float32,
        )
    return running


def conv_backward(hidden, grad_values, weight):
    centre = weight.shape[0] // 2
    weight_grad = jnp.stack(
        [
            jnp.einsum(
                "blc,bld->cd",
                shifted(hidden, tap_index - centre),
                grad_values,
                preferred_element_type=jnp.float32,
            )
            for tap_index in range(weight.shape[0])
        ]
    )
    hidden_grad = jnp.einsum(
        "bld,cd->blc", shifted(grad_values, centre), weight[0], preferred_element_type=jnp.float32
    )
    for tap_index in range(1, weight.shape[0]):
        hidden_grad = hidden_grad + jnp.einsum(
            "bld,cd->blc",
            shifted(grad_values, centre - tap_index),
            weight[tap_index],
            preferred_element_type=jnp.float32,
        )
    return (weight_grad, hidden_grad)


def normalize(values, frame_mask, frame_count):
    first_sum, second_sum = lax.psum(
        (
            jnp.sum(values * frame_mask, axis=(0, 1)),
            jnp.sum(values * values * frame_mask, axis=(0, 1)),
        ),
        ("dp", "rep"),
    )
    centre = first_sum / frame_count
    spread = second_sum / frame_count - centre * centre
    scale_inv = lax.rsqrt(spread + 1e-05)
    return ((values - centre) * scale_inv, scale_inv)


def norm_backward(grad_out, normed, scale_inv, gain, frame_mask, frame_count):
    shift_grad, gain_grad = lax.psum(
        (jnp.sum(grad_out, axis=(0, 1)), jnp.sum(grad_out * normed, axis=(0, 1))), ("dp", "rep")
    )
    grad_values = (
        gain * scale_inv * (grad_out - shift_grad / frame_count - normed * gain_grad / frame_count)
    )
    return (frame_mask * grad_values, gain_grad, shift_grad)


def layer_list(fetched):
    middle = fetched[1].shape[0]
    return (
        [jnp.swapaxes(fetched[0], 1, 2)]
        + [fetched[1][layer] for layer in range(middle)]
        + [fetched[2]]
    )


def local(
    mel, grad_post, lengths, regroup, w_first, w_mid, w_last, gains, shifts, gain_last, shift_last
):
    devices_dp = lax.axis_size("dp")
    replicas = lax.axis_size("rep")
    dp_index = lax.axis_index("dp")
    rep_index = lax.axis_index("rep")
    group_size = regroup.shape[1]
    utt_dev = group_size // devices_dp
    utt_micro = utt_dev // MB
    frames_all = mel.shape[1] * devices_dp
    middle = w_mid.shape[0]
    offsets = (jnp.arange(replicas, dtype=jnp.int32) * group_size)[:, None]
    lens_order = lengths[(regroup + offsets).reshape(-1)].reshape(
        replicas, devices_dp, MB, utt_micro
    )
    counts = jnp.sum(lens_order, axis=(0, 1, 3)).astype(jnp.float32)
    own_lens = lax.dynamic_index_in_dim(
        lax.dynamic_index_in_dim(lens_order, rep_index, 0, False), dp_index, 0, False
    )
    frame_ids = jnp.arange(frames_all, dtype=jnp.int32)
    masks = (frame_ids[None, None, :] < own_lens[:, :, None]).astype(jnp.float32)[..., None]
    local_order = lax.dynamic_index_in_dim(regroup, rep_index, 0, False)
    moved_mel, moved_grad = (
        lax.all_to_all(mel[local_order], "dp", split_axis=0, concat_axis=1, tiled=True),
        lax.all_to_all(grad_post[local_order], "dp", split_axis=0, concat_axis=1, tiled=True),
    )
    gain_list = [gains[layer] for layer in range(middle + 1)] + [gain_last]
    shift_list = [shifts[layer] for layer in range(middle + 1)] + [shift_last]
    depth = middle + 2
    gain_grads = [jnp.zeros_like(entry) for entry in gain_list]
    shift_grads = [jnp.zeros_like(entry) for entry in shift_list]
    owned = (
        jnp.zeros(w_first.shape, jnp.float32),
        jnp.zeros(w_mid.shape, jnp.float32),
        jnp.zeros(w_last.shape, jnp.float32),
    )
    refined = []
    input_grads = []
    for micro_index in range(MB):
        mel_block = moved_mel[micro_index * utt_micro : (micro_index + 1) * utt_micro]
        grad_block = moved_grad[micro_index * utt_micro : (micro_index + 1) * utt_micro].astype(
            jnp.float32
        )
        frame_mask = masks[micro_index]
        frame_count = counts[micro_index]
        fetched = (
            lax.all_gather(w_first, "dp", axis=1, tiled=True),
            lax.all_gather(w_mid, "dp", axis=2, tiled=True),
            lax.all_gather(w_last, "dp", axis=1, tiled=True),
        )
        weights = layer_list(fetched)
        hidden = (mel_block.astype(jnp.float32) * frame_mask).astype(jnp.bfloat16)
        inputs = []
        kept = []
        for layer in range(depth):
            inputs.append(hidden)
            normed, scale_inv = normalize(
                conv_forward(hidden, weights[layer]), frame_mask, frame_count
            )
            kept.append((normed, scale_inv))
            activated = gain_list[layer] * normed + shift_list[layer]
            if layer < depth - 1:
                hidden = (frame_mask * jnp.tanh(activated)).astype(jnp.bfloat16)
            else:
                refined.append(
                    (mel_block.astype(jnp.float32) + frame_mask * activated).astype(jnp.bfloat16)
                )
        fetched = (
            lax.all_gather(w_first, "dp", axis=1, tiled=True),
            lax.all_gather(w_mid, "dp", axis=2, tiled=True),
            lax.all_gather(w_last, "dp", axis=1, tiled=True),
        )
        weights = layer_list(fetched)
        grad_out = frame_mask * grad_block
        weight_grads = [None] * depth
        for layer in reversed(range(depth)):
            normed, scale_inv = kept[layer]
            grad_values, gain_grad, shift_grad = norm_backward(
                grad_out, normed, scale_inv, gain_list[layer], frame_mask, frame_count
            )
            gain_grads[layer] = gain_grads[layer] + gain_grad
            shift_grads[layer] = shift_grads[layer] + shift_grad
            weight_grad, hidden_grad = conv_backward(
                inputs[layer], grad_values.astype(jnp.bfloat16), weights[layer]
            )
            weight_grads[layer] = weight_grad
            if layer > 0:
                before = kept[layer - 1]
                activated = jnp.tanh(gain_list[layer - 1] * before[0] + shift_list[layer - 1])
                grad_out = frame_mask * hidden_grad * (1.0 - activated * activated)
            else:
                input_grads.append((grad_block + frame_mask * hidden_grad).astype(jnp.bfloat16))
        local_grads = (
            jnp.swapaxes(weight_grads[0], 1, 2),
            jnp.stack(weight_grads[1 : depth - 1]),
            weight_grads[depth - 1],
        )
        pieces = (
            lax.psum_scatter(local_grads[0], "dp", scatter_dimension=1, tiled=True),
            lax.psum_scatter(local_grads[1], "dp", scatter_dimension=2, tiled=True),
            lax.psum_scatter(local_grads[2], "dp", scatter_dimension=1, tiled=True),
        )
        owned = tuple((total + piece for total, piece in zip(owned, pieces)))
    final_first, final_mid, final_last = jax.tree.map(
        lambda part: part.astype(jnp.float32), lax.psum(shortened(owned), "rep")
    )
    back_mel, back_grad = (
        lax.all_to_all(
            jnp.concatenate(refined, axis=0), "dp", split_axis=1, concat_axis=0, tiled=True
        ),
        lax.all_to_all(
            jnp.concatenate(input_grads, axis=0), "dp", split_axis=1, concat_axis=0, tiled=True
        ),
    )
    inverse = (
        jnp.zeros((group_size,), jnp.int32)
        .at[local_order]
        .set(jnp.arange(group_size, dtype=jnp.int32))
    )
    return (
        back_mel[inverse],
        back_grad[inverse],
        final_first,
        final_mid,
        final_last,
        jnp.stack(gain_grads[: depth - 1]),
        jnp.stack(shift_grads[: depth - 1]),
        gain_grads[depth - 1],
        shift_grads[depth - 1],
    )


def solution(mesh):
    in_specs = (
        P("rep", "dp", None),
        P("rep", "dp", None),
        P(),
        P(),
        P(None, "dp", None),
        P(None, None, "dp", None),
        P(None, "dp", None),
        P(),
        P(),
        P(),
        P(),
    )
    out_specs = (
        P("rep", "dp", None),
        P("rep", "dp", None),
        P(None, "dp", None),
        P(None, None, "dp", None),
        P(None, "dp", None),
        P(),
        P(),
        P(),
        P(),
    )
    step = local_kernel if mesh.shape["dp"] == SUB and mesh.shape["rep"] == CORES else local
    return jax.shard_map(step, mesh=mesh, in_specs=in_specs, out_specs=out_specs, check_vma=False)
```

```python
import functools

import jax
import jax.numpy as jnp
from jax import lax
from jax.experimental import pallas as pl
from jax.experimental.pallas import tpu as pltpu
from jax.sharding import PartitionSpec as P

MB = 2
PLANE = 4
CORES = 2
SUB = 16
LANES = 128
MESH = pl.DeviceIdType.MESH
bf16 = jnp.bfloat16
f32 = jnp.float32
EPS = 1e-05


def nn(a, b):
    return jnp.dot(a, b, preferred_element_type=f32)


def nt(a, b):
    return lax.dot_general(a, b, (((1,), (1,)), ((), ())), preferred_element_type=f32)


def tn(a, b):
    return lax.dot_general(a, b, (((0,), (0,)), ((), ())), preferred_element_type=f32)


def kernel(
    n_dp, utts, frames, chans, mels, taps, middle,
    len_s, reg_s, mel, gpost, wf, wm, wl, gains, shifts, gl, sl,
    o_mel, o_grad, o_wf, o_wm, o_wl, o_gains, o_shifts, o_gl, o_sl,
    mel_s, grd_s, bak_s, bak2_s, mel_r, grd_r, bak_r, bak2_r,
    whole, pad_m, pad_g, mel_p, grd_p, mask, h0, h, xh, z, zl, gz, gzl,
    W, WF, WL, GF, G1, rbufs,
    pl_s, pl_r, z_s, z_r, ar_t, a1, a2, a3, a4, invs, glp, slp, lens,
    pls_sem, plr_sem, zs_sem, zr_sem, a2a_s, a2a_r, gz_s, gz_r, gp_s, gp_r, gq_s, gq_r, gb_s, gb_r,
    r0_s, r0_r, r1_s, r1_r, r2_s, r2_r, r3_s, r3_r, ro_s, ro_r,
):
    nz = n_dp // PLANE
    total = n_dp * CORES
    T = n_dp * frames
    HALO = 2 * SUB
    MT = T // 2
    CL = chans // LANES
    ctile = 32
    dp = lax.axis_index("dp")
    rep = lax.axis_index("rep")
    zc = lax.div(dp, PLANE)
    s = lax.rem(dp, PLANE)
    sx = s + 1 - 2 * lax.rem(s, 2)
    sy = s + 2 - 4 * lax.div(s, 2)
    s1 = sx + rep * (sy - sx)
    s2 = sy + rep * (sx - sy)
    sd = 3 - s
    lin = dp * CORES + rep
    group = PLANE * CORES
    mine = s * CORES + rep
    other = 1 - rep
    sib = (dp, other)
    peer1 = (zc * PLANE + s1, rep)
    peer2 = (zc * PLANE + s2, rep)

    def send(src, dst, ss, rs, to):
        pltpu.make_async_remote_copy(
            src_ref=src, dst_ref=dst, send_sem=ss, recv_sem=rs, device_id=to, device_id_type=MESH
        ).start()

    def wait(ref, sem):
        pltpu.make_async_copy(ref, ref, sem).wait()

    W[:, :, zc, s] = wm[...]
    WF[:, zc, s] = jnp.zeros((taps, CORES) + WF.shape[4:], bf16)
    WL[:, zc, s] = jnp.zeros((taps, CORES) + WL.shape[4:], bf16)
    WF[:, zc, s, :, :, 0:mels] = wf[...]
    WL[:, zc, s, :, :, 0:mels] = wl[...]

    barrier = pltpu.get_barrier_semaphore()
    for i in range(1, total):
        to = lax.rem(lin + i, total)
        pl.semaphore_signal(
            barrier, inc=1, device_id=(lax.div(to, CORES), lax.rem(to, CORES)), device_id_type=MESH
        )

    lane = lax.broadcasted_iota(jnp.int32, (frames, LANES), 1)
    lane_b = lax.broadcasted_iota(jnp.int32, (SUB, LANES), 1)
    half = LANES // 2
    tail = mels - half
    parts = frames // SUB

    def pack(dst, j, vs):
        low = jnp.where(lane < half, vs[0], pltpu.roll(vs[1], half, 1))
        rest = jnp.zeros((SUB, LANES), f32)
        for m in range(MB):
            for r in range(parts):
                at = (m * parts + r) * tail
                piece = vs[m][r * SUB : (r + 1) * SUB, :]
                moved = pltpu.roll(piece, (at - half) % LANES, 1) if at != half else piece
                rest = jnp.where((lane_b >= at) & (lane_b < at + tail), moved, rest)
        dst[j, 0:frames, :] = low.astype(bf16)
        dst[j, frames : frames + SUB, :] = rest.astype(bf16)

    def unpack(src, j):
        low = src[j, 0:frames, :].astype(f32)
        rest = src[j, frames : frames + SUB, :].astype(f32)
        vs = []
        for m in range(MB):
            pieces = []
            for r in range(parts):
                shift = (half - (m * parts + r) * tail) % LANES
                pieces.append(pltpu.roll(rest, shift, 1) if shift else rest)
            high = jnp.where(lane < mels, jnp.concatenate(pieces, axis=0), 0.0)
            vs.append(jnp.where(lane < half, pltpu.roll(low, half, 1) if m else low, high))
        return vs

    pad_m[...] = jnp.zeros(pad_m.shape, f32)
    pad_g[...] = jnp.zeros(pad_g.shape, f32)

    def pack_pair(src, pad, dst):
        @pl.loop(0, n_dp)
        def _(j):
            for m in range(MB):
                pad[m, :, 0:mels] = src[reg_s[rep, j * MB + m]].astype(f32)
            pack(dst, j, [pad[m] for m in range(MB)])

    pack_pair(mel, pad_m, mel_s)

    pl.semaphore_wait(barrier, total - 1)

    def chunk(c):
        if c == 0:
            return WF
        if c == middle + 1:
            return WL
        return W.at[c - 1]

    def g0(c):
        w = chunk(c)
        for i in range(1, nz):
            to = lax.rem(zc + i, nz) * PLANE + s
            piece = w.at[:, zc, s, rep]
            send(piece, piece, gz_s.at[c], gz_r.at[c], (to, rep))

    def three(w):
        return w.at[:, pl.ds(0, nz - 1), 0, 0]

    def g1(c):
        w = chunk(c)
        wait(three(w), gz_r.at[c])
        col = w.at[:, :, s, rep]
        send(col, col, gp_s.at[c], gp_r.at[c], peer1)
        send(col, col, gq_s.at[c], gq_r.at[c], peer2)
        send(col, col, gb_s.at[c], gb_r.at[c], sib)

    def g2(c):
        w = chunk(c)
        wait(w.at[:, :, 0, 0], gp_r.at[c])
        col = w.at[:, :, s1, rep]
        send(col, col, gq_s.at[c], gq_r.at[c], peer2)
        send(col, col, gb_s.at[c], gb_r.at[c], sib)

    def g3(c):
        w = chunk(c)
        wait(w.at[:, :, pl.ds(0, 2), 0], gq_r.at[c])
        for q in (s2, sd):
            col = w.at[:, :, q, rep]
            send(col, col, gb_s.at[c], gb_r.at[c], sib)

    def g4(c):
        wait(chunk(c).at[:, :, :, 0], gb_r.at[c])

    def gdrain(c):
        w = chunk(c)
        wait(three(w), gz_s.at[c])
        wait(w.at[:, :, 0, 0], gp_s.at[c])
        wait(w.at[:, :, pl.ds(0, 2), 0], gq_s.at[c])
        wait(w.at[:, :, :, 0], gb_s.at[c])

    def deal(src, dst, which):
        for i in range(1, n_dp):
            to = lax.rem(dp + i, n_dp)
            send(src.at[to], dst.at[dp], a2a_s.at[which], a2a_r.at[which], (to, rep))
        dst[dp] = src[dp]

    def dealt(dst, which):
        wait(dst.at[pl.ds(0, n_dp - 1)], a2a_r.at[which])

    def spread(src, dst):
        for j in range(n_dp):
            for m, v in enumerate(unpack(src, j)):
                dst.at[m][pl.ds(j, frames, stride=SUB), :] = v

    def collect(src, dst):
        for j in range(n_dp):
            pack(dst, j, [src.at[m][pl.ds(j, frames, stride=SUB), :] for m in range(MB)])

    def restore(src, out):
        for j in range(n_dp):
            for m, v in enumerate(unpack(src, j)):
                whole[j * MB + m] = v.astype(bf16)

        @pl.loop(0, utts)
        def _(u):
            out[u] = whole[lens[u], :, 0:mels]

    def ar_go(rd, vs):
        n = 8 // len(vs)
        for e, v in enumerate(vs):
            for i in range(n):
                if (i + 1) * LANES <= v.shape[1]:
                    row = v[:, i * LANES : (i + 1) * LANES]
                else:
                    row = jnp.zeros((1, LANES), f32)
                at = e * n + i
                pl_s[rd, at : at + 1, :] = row
                pl_r[rd, mine, at : at + 1, :] = row
        for i in range(1, group):
            to = lax.rem(mine + i, group)
            send(
                pl_s.at[rd], pl_r.at[rd, mine], pls_sem.at[rd], plr_sem.at[rd],
                (zc * PLANE + lax.div(to, CORES), lax.rem(to, CORES)),
            )

    def ar_mid(rd):
        wait(pl_r.at[rd, pl.ds(0, group - 1)], plr_sem.at[rd])
        acc = pl_r[rd, 0]
        for i in range(1, group):
            acc = acc + pl_r[rd, i]
        z_s[rd] = acc
        z_r[rd, zc] = acc
        for i in range(1, nz):
            to = lax.rem(zc + i, nz) * PLANE + s
            send(z_s.at[rd], z_r.at[rd, zc], zs_sem.at[rd], zr_sem.at[rd], (to, rep))

    def ar_get(rd, n):
        wait(z_r.at[rd, pl.ds(0, nz - 1)], zr_sem.at[rd])
        acc = z_r[rd, 0]
        for i in range(1, nz):
            acc = acc + z_r[rd, i]
        ar_t[...] = acc
        q = CL if n == CL else 2
        return [
            jnp.concatenate([ar_t[e * q + i : e * q + i + 1, :] for i in range(n)], axis=1)
            for e in range(8 // q)
        ]

    def fold(v):
        return jnp.sum(v.reshape(v.shape[0] // 8, 8, v.shape[1]), axis=0)

    def wide(mk, d):
        return jnp.concatenate([mk] * (d // LANES), axis=1) if d > LANES else mk

    def clear(d):
        a1[:, 0:d] = jnp.zeros((8, d), f32)
        a2[:, 0:d] = jnp.zeros((8, d), f32)
        if d == LANES:
            a3[...] = jnp.zeros((8, d), f32)
            a4[...] = jnp.zeros((8, d), f32)

    def ar_acc(rd, d, before=None):
        if before is not None:
            ar_mid(before)
        accs = (a1, a2, a3, a4) if d == LANES else (a1, a2)
        ar_go(rd, [jnp.sum(v[:, 0:d], axis=0, keepdims=True) for v in accs])

    def halo(ref):
        d = ref.shape[1]
        row = lax.rem(lax.broadcasted_iota(jnp.int32, (HALO, d), 0), SUB)
        low = pltpu.roll(ref[T : T + HALO, :].astype(f32), 1, 0)
        ref[0:HALO, :] = jnp.where(row == 0, 0.0, low).astype(bf16)
        high = pltpu.roll(ref[HALO : 2 * HALO, :].astype(f32), HALO - 1, 0)
        ref[T + HALO : T + 2 * HALO, :] = jnp.where(row == SUB - 1, 0.0, high).astype(bf16)

    cnt = []
    own = []
    for m in range(MB):

        def body(j, c, m=m):
            for r in range(CORES):
                c = c + len_s[r * utts + reg_s[r, j * MB + m]]
            return c

        cnt.append(lax.fori_loop(0, n_dp, body, jnp.int32(0)).astype(f32))
        own.append(len_s[rep * utts + reg_s[rep, dp * MB + m]])

    last = middle + 1

    def mean_inv(rd, m, n):
        v1, v2 = ar_get(rd, n)
        mean = v1 / cnt[m]
        var = v2 / cnt[m] - mean * mean
        inv = lax.rsqrt(var + EPS)
        invs[rd, 0:1, 0 : n * LANES] = inv
        return mean, inv

    def conv(layer, m):
        rd = layer * MB + m
        d = LANES if layer == last else chans
        dst = zl if layer == last else z
        clear(d)

        @pl.loop(0, T // MT)
        def _(t):
            base = pl.multiple_of(t * MT, MT)
            acc = None
            for k in range(taps):
                rows = pl.ds(base + SUB * k, MT)
                if layer == 0:
                    part = nt(h0[m, rows, :], WF[k].reshape(chans, LANES))
                elif layer == last:
                    part = nn(h[layer - 1, m, rows, :], WL[k].reshape(chans, LANES))
                else:
                    part = nn(h[layer - 1, m, rows, :], W[layer - 1, k].reshape(chans, chans))
                acc = part if acc is None else acc + part
            dst[m, pl.ds(base, MT), :] = acc
            zm = acc * wide(mask[m, pl.ds(base, MT), :], d)
            a1[:, 0:d] += fold(zm)
            a2[:, 0:d] += fold(zm * acc)
            if layer == last:
                gy = mask[m, pl.ds(base, MT), :] * grd_p[m, pl.ds(base, MT), :]
                a3[...] += fold(gy)
                a4[...] += fold(gy * acc)

        ar_acc(rd, d, rd - m if m else None)

    def norm(layer, m):
        mean, inv = mean_inv(layer * MB + m, m, CL)
        g = gains[layer : layer + 1, :]
        b = shifts[layer : layer + 1, :]

        @pl.loop(0, T // ctile)
        def _(i):
            base = pl.multiple_of(i * ctile, ctile)
            rows = pl.ds(base, ctile)
            xv = (z[m, rows, :] - mean) * inv
            hv = wide(mask[m, rows, :], chans) * jnp.tanh(g * xv + b)
            xh[layer, m, rows, :] = xv.astype(bf16)
            h[layer, m, pl.ds(base + HALO, ctile), :] = hv.astype(bf16)

        halo(h.at[layer, m])

    def grad_tail(layer, m, base, acc):
        g = gains[layer : layer + 1, :]
        b = shifts[layer : layer + 1, :]
        rows = pl.ds(base, MT)
        xv = xh[layer, m, rows, :].astype(f32)
        th = jnp.tanh(g * xv + b)
        gy = wide(mask[m, rows, :], chans) * acc * (1.0 - th * th)
        z[m, rows, :] = gy
        a1[...] += fold(gy)
        a2[...] += fold(gy * xv)

    def bround(layer, m):
        return (last + 1 + layer) * MB + m

    def coefs(layer, m, n, g, og, os):
        v1, v2 = ar_get(bround(layer, m), n)
        og(v2, m > 0)
        os(v1, m > 0)
        a = g * invs[layer * MB + m, 0:1, 0 : n * LANES]
        return a, a * v1 / cnt[m], a * v2 / cnt[m]

    def grad_z(layer, m):
        def og(v, add):
            o_gains[layer : layer + 1, :] = v + o_gains[layer : layer + 1, :] if add else v

        def os(v, add):
            o_shifts[layer : layer + 1, :] = v + o_shifts[layer : layer + 1, :] if add else v

        a, c1, c2 = coefs(layer, m, CL, gains[layer : layer + 1, :], og, os)

        @pl.loop(0, T // ctile)
        def _(i):
            base = pl.multiple_of(i * ctile, ctile)
            rows = pl.ds(base, ctile)
            v = a * z[m, rows, :] - c1 - c2 * xh[layer, m, rows, :].astype(f32)
            gz[m, pl.ds(base + HALO, ctile), :] = (wide(mask[m, rows, :], chans) * v).astype(bf16)

        halo(gz.at[m])

    def grad_h(layer, m):
        clear(chans)

        @pl.loop(0, T // MT)
        def _(t):
            base = pl.multiple_of(t * MT, MT)
            acc = None
            for k in range(taps):
                rows = pl.ds(base + SUB * (taps - 1 - k), MT)
                if layer == last:
                    part = nt(gzl[m, rows, :], WL[k].reshape(chans, LANES))
                else:
                    part = nt(gz[m, rows, :], W[layer - 1, k].reshape(chans, chans))
                acc = part if acc is None else acc + part
            grad_tail(layer - 1, m, base, acc)

        ar_acc(bround(layer - 1, m), chans, bround(layer - 1, 0) if m else None)

    def gchunk(layer):
        return GF if layer == 0 else G1 if layer == 1 else chunk(layer)

    def wgrad(layer):
        gdrain(layer)
        w = gchunk(layer)

        @pl.loop(0, taps)
        def _(k):
            if layer == 0:
                rows = pl.ds(pl.multiple_of(SUB * k, SUB), T)
                acc = tn(gz[0, HALO : HALO + T, :], h0[0, rows, :])
                for m in range(1, MB):
                    acc = acc + tn(gz[m, HALO : HALO + T, :], h0[m, rows, :])
            else:
                g = gzl if layer == last else gz
                rows = pl.ds(pl.multiple_of(SUB * (taps - 1 - k), SUB), T)
                acc = tn(h[layer - 1, 0, HALO : HALO + T, :], g[0, rows, :])
                for m in range(1, MB):
                    acc = acc + tn(h[layer - 1, m, HALO : HALO + T, :], g[m, rows, :])
            w[k] = acc.astype(bf16).reshape(w.shape[1:])

        send(w.at[:, :, :, other], rbuf(layer)[0], r0_s.at[layer], r0_r.at[layer], sib)

    def rbuf(layer):
        return rbufs[layer]

    def total_of(a, b):
        return (a.astype(f32) + b.astype(f32)).astype(bf16)

    def ra(layer):
        w = gchunk(layer)
        r0, r1 = rbuf(layer)[0:2]
        wait(r0, r0_r.at[layer])
        for k in range(taps):
            r0[k] = total_of(r0[k], w[k, :, :, rep])
        for slot, q in ((1, sd), (0, s2)):
            send(r0.at[:, :, q], r1.at[slot], r1_s.at[layer], r1_r.at[layer], peer2)

    def rb(layer):
        r0, r1, r2 = rbuf(layer)[0:3]
        wait(r1, r1_r.at[layer])
        for slot, q in ((1, s1), (0, s)):
            for k in range(taps):
                r1[slot, k] = total_of(r1[slot, k], r0[k, :, q])
        send(r1.at[1], r2, r2_s.at[layer], r2_r.at[layer], peer1)

    def rc(layer):
        r1, r2, r3 = rbuf(layer)[1:4]
        wait(r2, r2_r.at[layer])
        for k in range(taps):
            r2[k] = total_of(r2[k], r1[0, k])
        for i in range(1, nz):
            zt = lax.rem(zc + i, nz)
            send(
                r2.at[:, zt], r3.at[i - 1], r3_s.at[layer], r3_r.at[layer],
                (zt * PLANE + s, rep),
            )

    def outs(layer):
        return o_wf if layer == 0 else o_wl if layer == last else o_wm.at[layer - 1]

    def rd_(layer):
        r2, r3 = rbuf(layer)[2:4]
        fs, fr = rbuf(layer)[4:6]
        wait(r3, r3_r.at[layer])
        out = outs(layer)
        for k in range(taps):
            v = r2[k, zc].astype(f32)
            for i in range(nz - 1):
                v = v + r3[i, k].astype(f32)
            fs[k] = v
            out[k, rep] = v[:, 0 : out.shape[3]]
        send(fs, fr, ro_s.at[layer], ro_r.at[layer], sib)

    def rdrain(layer):
        r0, r1, r2, r3, fs, fr = rbuf(layer)
        out = outs(layer)
        wait(fr, ro_r.at[layer])
        for k in range(taps):
            out[k, other] = fr[k][:, 0 : out.shape[3]]
        wait(fs, ro_s.at[layer])
        wait(r0, r0_s.at[layer])
        wait(r1, r1_s.at[layer])
        wait(r2, r2_s.at[layer])
        wait(r3, r3_s.at[layer])

    g0(0)
    g0(1)
    deal(mel_s, mel_r, 0)
    g0(2)
    glp[...] = jnp.zeros(glp.shape, f32)
    slp[...] = jnp.zeros(slp.shape, f32)
    glp[0:1, 0:mels] = gl[...]
    slp[0:1, 0:mels] = sl[...]
    for m in range(MB):

        @pl.loop(0, T // ctile)
        def _(i):
            base = pl.multiple_of(i * ctile, ctile)
            r = base + lax.broadcasted_iota(jnp.int32, (ctile, LANES), 0)
            t = lax.rem(r, SUB) * frames + lax.div(r, SUB)
            mask[m, pl.ds(base, ctile), :] = jnp.where(t < own[m], 1.0, 0.0)

    g1(0)
    g2(0)
    g3(0)
    g1(1)

    @pl.loop(0, utts)
    def _(u):
        at = jnp.int32(0)
        for k in range(utts):
            at = jnp.where(reg_s[rep, k] == u, k, at)
        lens[u] = at

    pack_pair(gpost, pad_g, grd_s)
    dealt(mel_r, 0)
    spread(mel_r, mel_p)
    for m in range(MB):
        h0[m, HALO : HALO + T, :] = (mel_p[m] * mask[m]).astype(bf16)
        halo(h0.at[m])
        if m == 0:
            g4(0)
        conv(0, m)
        if m == 0:
            g2(1)
    g1(2)
    g0(3)
    for layer in range(1, last + 1):
        g3(layer)
        g4(layer)
        ar_mid((layer - 1) * MB + 1)
        for m in range(MB):
            norm(layer - 1, m)
            if layer == last and m == 0:
                dealt(grd_r, 1)
                spread(grd_r, grd_p)
            conv(layer, m)
            if m == 0:
                if layer + 1 <= last:
                    g2(layer + 1)
            else:
                if layer + 2 <= last:
                    g1(layer + 2)
                if layer + 3 <= last:
                    g0(layer + 3)
                if layer == 2:
                    deal(grd_s, grd_r, 1)

    ar_mid(last * MB + 1)
    g_last = glp[0:1, :]
    b_last = slp[0:1, :]
    ct = 64
    for m in range(MB):
        tot = ar_get(last * MB + m, 1)
        mean = tot[0] / cnt[m]
        var = tot[1] / cnt[m] - mean * mean
        inv = lax.rsqrt(var + EPS)
        v1 = tot[2]
        v2 = inv * (tot[3] - mean * v1)
        if m == 0:
            o_gl[...] = v2[:, 0:mels]
            o_sl[...] = v1[:, 0:mels]
        else:
            o_gl[...] = o_gl[...] + v2[:, 0:mels]
            o_sl[...] = o_sl[...] + v1[:, 0:mels]
        a = g_last * inv
        c1 = a * v1 / cnt[m]
        c2 = a * v2 / cnt[m]

        @pl.loop(0, T // ct)
        def _(i):
            base = pl.multiple_of(i * ct, ct)
            rows = pl.ds(base, ct)
            mk = mask[m, rows, :]
            xv = (zl[m, rows, :] - mean) * inv
            mel_p[m, rows, :] = mel_p[m, rows, :] + mk * (g_last * xv + b_last)
            v = a * grd_p[m, rows, :] - c1 - c2 * xv
            gzl[m, pl.ds(base + HALO, ct), :] = (mk * v).astype(bf16)

        halo(gzl.at[m])
        grad_h(last, m)
    wgrad(last)
    ar_mid(bround(middle, 1))
    collect(mel_p, bak_s)
    deal(bak_s, bak_r, 2)
    for layer in range(middle, 1, -1):
        for m in range(MB):
            grad_z(layer, m)
            grad_h(layer, m)
            if m == 0:
                ra(layer + 1)
                if layer + 2 <= last:
                    rc(layer + 2)
        wgrad(layer)
        ar_mid(bround(layer - 1, 1))
        rb(layer + 1)
        if layer + 2 <= last:
            rd_(layer + 2)
    for m in range(MB):
        grad_z(1, m)
    wgrad(1)
    ra(2)
    rc(3)
    grad_h(1, 0)
    rb(2)
    rd_(3)
    grad_h(1, 1)
    ra(1)
    ar_mid(bround(0, 1))
    dealt(bak_r, 2)
    restore(bak_r, o_mel)

    for m in range(MB):
        grad_z(0, m)
    wgrad(0)
    rc(2)
    for m in range(MB):

        @pl.loop(0, T // MT)
        def _(t):
            base = pl.multiple_of(t * MT, MT)
            acc = None
            for k in range(taps):
                rows = pl.ds(base + SUB * (taps - 1 - k), MT)
                part = nn(gz[m, rows, :], WF[k].reshape(chans, LANES))
                acc = part if acc is None else acc + part
            rows = pl.ds(base, MT)
            grd_p[m, rows, :] = grd_p[m, rows, :] + mask[m, rows, :] * acc

        if m == 0:
            rb(1)
            ra(0)
    collect(grd_p, bak2_s)
    deal(bak2_s, bak2_r, 3)
    rb(0)
    rd_(2)
    rc(1)
    rc(0)
    rd_(1)
    rd_(0)
    dealt(bak2_r, 3)
    restore(bak2_r, o_grad)

    for layer in reversed(range(last + 1)):
        rdrain(layer)
    wait(mel_r.at[pl.ds(0, n_dp - 1)], a2a_s.at[0])
    wait(grd_r.at[pl.ds(0, n_dp - 1)], a2a_s.at[1])
    wait(bak_r.at[pl.ds(0, n_dp - 1)], a2a_s.at[2])
    wait(bak2_r.at[pl.ds(0, n_dp - 1)], a2a_s.at[3])

    @pl.loop(0, (2 * last + 1) * MB)
    def _(r):
        wait(pl_r.at[r, pl.ds(0, group - 1)], pls_sem.at[r])
        wait(z_r.at[r, pl.ds(0, nz - 1)], zs_sem.at[r])


def local_kernel(
    mel, grad_post, lengths, regroup, w_first, w_mid, w_last, gains, shifts, gain_last, shift_last
):
    n_dp = lax.axis_size("dp")
    nz = n_dp // PLANE
    utts, frames, mels = mel.shape
    middle, taps, shard, chans = w_mid.shape
    depth = middle + 2
    T = n_dp * frames
    TH = T + 4 * SUB
    rows = shard // CORES
    rounds = (2 * depth - 1) * MB
    V = pltpu.VMEM
    D = pltpu.SemaphoreType.DMA
    S = jax.ShapeDtypeStruct
    out_shape = (
        S(mel.shape, bf16),
        S(mel.shape, bf16),
        S((taps, CORES, rows, mels), f32),
        S((middle, taps, CORES, rows, chans), f32),
        S((taps, CORES, rows, mels), f32),
        S(gains.shape, f32),
        S(gains.shape, f32),
        S((1, mels), f32),
        S((1, mels), f32),
    )
    packed = V((n_dp, frames + SUB, LANES), bf16)
    landing = [
        [
            V((taps, nz, PLANE, rows, d), bf16),
            V((2, taps, nz, rows, d), bf16),
            V((taps, nz, rows, d), bf16),
            V((nz - 1, taps, rows, d), bf16),
            V((taps, rows, d), f32),
            V((taps, rows, d), f32),
        ]
        for d in [LANES] + [chans] * middle + [LANES]
    ]
    scratch = [
        packed, packed, packed, packed, packed, packed, packed, packed,
        V((utts, frames, LANES), bf16), V((MB, frames, LANES), f32), V((MB, frames, LANES), f32),
        V((MB, T, LANES), f32), V((MB, T, LANES), f32), V((MB, T, LANES), f32),
        V((MB, TH, LANES), bf16), V((middle + 1, MB, TH, chans), bf16),
        V((middle + 1, MB, T, chans), bf16),
        V((MB, T, chans), f32), V((MB, T, LANES), f32),
        V((MB, TH, chans), bf16), V((MB, TH, LANES), bf16),
        V((middle, taps, nz, PLANE, CORES, rows, chans), bf16),
        V((taps, nz, PLANE, CORES, rows, LANES), bf16),
        V((taps, nz, PLANE, CORES, rows, LANES), bf16),
        V((taps, nz, PLANE, CORES, rows, LANES), bf16),
        V((taps, nz, PLANE, CORES, rows, chans), bf16),
        landing,
        V((rounds, 8, LANES), f32), V((rounds, PLANE * CORES, 8, LANES), f32),
        V((rounds, 8, LANES), f32), V((rounds, nz, 8, LANES), f32), V((8, LANES), f32),
        V((8, chans), f32), V((8, chans), f32), V((8, LANES), f32), V((8, LANES), f32), V((depth * MB, 8, chans), f32),
        V((8, LANES), f32), V((8, LANES), f32), pltpu.SMEM((utts,), jnp.int32),
        D((rounds,)), D((rounds,)), D((rounds,)), D((rounds,)), D((4,)), D((4,)),
    ] + [D((depth,))] * 18
    body = functools.partial(kernel, n_dp, utts, frames, chans, mels, taps, middle)
    vmem = pl.BlockSpec(memory_space=pltpu.VMEM)
    smem = pl.BlockSpec(memory_space=pltpu.SMEM)
    out = pl.pallas_call(
        body,
        out_shape=out_shape,
        in_specs=[smem, smem] + [vmem] * 9,
        out_specs=(vmem,) * 9,
        scratch_shapes=scratch,
        compiler_params=pltpu.CompilerParams(
            collective_id=0, has_side_effects=True, vmem_limit_bytes=64 * 2**20
        ),
        name="postnet_step",
    )(
        lengths, regroup, mel, grad_post,
        w_first.reshape(taps, CORES, rows, mels),
        w_mid.reshape(middle, taps, CORES, rows, chans),
        w_last.reshape(taps, CORES, rows, mels),
        gains, shifts, gain_last[None, :], shift_last[None, :],
    )
    return (
        out[0], out[1],
        out[2].reshape(w_first.shape), out[3].reshape(w_mid.shape), out[4].reshape(w_last.shape),
        out[5], out[6], out[7][0], out[8][0],
    )


def shortened(value):

    def short(part):
        return part.astype(jnp.bfloat16) if part.dtype == jnp.float32 else part

    return jax.tree.map(short, value)


def shifted(hidden, offset):
    if offset == 0:
        return hidden
    frames = hidden.shape[1]
    reach = abs(offset)
    padded = jnp.pad(hidden, ((0, 0), (reach, reach), (0, 0)))
    return padded[:, reach + offset : reach + offset + frames]


def conv_forward(hidden, weight):
    centre = weight.shape[0] // 2
    running = jnp.einsum(
        "blc,cd->bld", shifted(hidden, -centre), weight[0], preferred_element_type=jnp.float32
    )
    for tap_index in range(1, weight.shape[0]):
        running = running + jnp.einsum(
            "blc,cd->bld",
            shifted(hidden, tap_index - centre),
            weight[tap_index],
            preferred_element_type=jnp.float32,
        )
    return running


def conv_backward(hidden, grad_values, weight):
    centre = weight.shape[0] // 2
    weight_grad = jnp.stack(
        [
            jnp.einsum(
                "blc,bld->cd",
                shifted(hidden, tap_index - centre),
                grad_values,
                preferred_element_type=jnp.float32,
            )
            for tap_index in range(weight.shape[0])
        ]
    )
    hidden_grad = jnp.einsum(
        "bld,cd->blc", shifted(grad_values, centre), weight[0], preferred_element_type=jnp.float32
    )
    for tap_index in range(1, weight.shape[0]):
        hidden_grad = hidden_grad + jnp.einsum(
            "bld,cd->blc",
            shifted(grad_values, centre - tap_index),
            weight[tap_index],
            preferred_element_type=jnp.float32,
        )
    return (weight_grad, hidden_grad)


def normalize(values, frame_mask, frame_count):
    first_sum, second_sum = lax.psum(
        (
            jnp.sum(values * frame_mask, axis=(0, 1)),
            jnp.sum(values * values * frame_mask, axis=(0, 1)),
        ),
        ("dp", "rep"),
    )
    centre = first_sum / frame_count
    spread = second_sum / frame_count - centre * centre
    scale_inv = lax.rsqrt(spread + 1e-05)
    return ((values - centre) * scale_inv, scale_inv)


def norm_backward(grad_out, normed, scale_inv, gain, frame_mask, frame_count):
    shift_grad, gain_grad = lax.psum(
        (jnp.sum(grad_out, axis=(0, 1)), jnp.sum(grad_out * normed, axis=(0, 1))), ("dp", "rep")
    )
    grad_values = (
        gain * scale_inv * (grad_out - shift_grad / frame_count - normed * gain_grad / frame_count)
    )
    return (frame_mask * grad_values, gain_grad, shift_grad)


def layer_list(fetched):
    middle = fetched[1].shape[0]
    return (
        [jnp.swapaxes(fetched[0], 1, 2)]
        + [fetched[1][layer] for layer in range(middle)]
        + [fetched[2]]
    )


def local(
    mel, grad_post, lengths, regroup, w_first, w_mid, w_last, gains, shifts, gain_last, shift_last
):
    devices_dp = lax.axis_size("dp")
    replicas = lax.axis_size("rep")
    dp_index = lax.axis_index("dp")
    rep_index = lax.axis_index("rep")
    group_size = regroup.shape[1]
    utt_dev = group_size // devices_dp
    utt_micro = utt_dev // MB
    frames_all = mel.shape[1] * devices_dp
    middle = w_mid.shape[0]
    offsets = (jnp.arange(replicas, dtype=jnp.int32) * group_size)[:, None]
    lens_order = lengths[(regroup + offsets).reshape(-1)].reshape(
        replicas, devices_dp, MB, utt_micro
    )
    counts = jnp.sum(lens_order, axis=(0, 1, 3)).astype(jnp.float32)
    own_lens = lax.dynamic_index_in_dim(
        lax.dynamic_index_in_dim(lens_order, rep_index, 0, False), dp_index, 0, False
    )
    frame_ids = jnp.arange(frames_all, dtype=jnp.int32)
    masks = (frame_ids[None, None, :] < own_lens[:, :, None]).astype(jnp.float32)[..., None]
    local_order = lax.dynamic_index_in_dim(regroup, rep_index, 0, False)
    moved_mel, moved_grad = (
        lax.all_to_all(mel[local_order], "dp", split_axis=0, concat_axis=1, tiled=True),
        lax.all_to_all(grad_post[local_order], "dp", split_axis=0, concat_axis=1, tiled=True),
    )
    gain_list = [gains[layer] for layer in range(middle + 1)] + [gain_last]
    shift_list = [shifts[layer] for layer in range(middle + 1)] + [shift_last]
    depth = middle + 2
    gain_grads = [jnp.zeros_like(entry) for entry in gain_list]
    shift_grads = [jnp.zeros_like(entry) for entry in shift_list]
    owned = (
        jnp.zeros(w_first.shape, jnp.float32),
        jnp.zeros(w_mid.shape, jnp.float32),
        jnp.zeros(w_last.shape, jnp.float32),
    )
    refined = []
    input_grads = []
    for micro_index in range(MB):
        mel_block = moved_mel[micro_index * utt_micro : (micro_index + 1) * utt_micro]
        grad_block = moved_grad[micro_index * utt_micro : (micro_index + 1) * utt_micro].astype(
            jnp.float32
        )
        frame_mask = masks[micro_index]
        frame_count = counts[micro_index]
        fetched = (
            lax.all_gather(w_first, "dp", axis=1, tiled=True),
            lax.all_gather(w_mid, "dp", axis=2, tiled=True),
            lax.all_gather(w_last, "dp", axis=1, tiled=True),
        )
        weights = layer_list(fetched)
        hidden = (mel_block.astype(jnp.float32) * frame_mask).astype(jnp.bfloat16)
        inputs = []
        kept = []
        for layer in range(depth):
            inputs.append(hidden)
            normed, scale_inv = normalize(
                conv_forward(hidden, weights[layer]), frame_mask, frame_count
            )
            kept.append((normed, scale_inv))
            activated = gain_list[layer] * normed + shift_list[layer]
            if layer < depth - 1:
                hidden = (frame_mask * jnp.tanh(activated)).astype(jnp.bfloat16)
            else:
                refined.append(
                    (mel_block.astype(jnp.float32) + frame_mask * activated).astype(jnp.bfloat16)
                )
        fetched = (
            lax.all_gather(w_first, "dp", axis=1, tiled=True),
            lax.all_gather(w_mid, "dp", axis=2, tiled=True),
            lax.all_gather(w_last, "dp", axis=1, tiled=True),
        )
        weights = layer_list(fetched)
        grad_out = frame_mask * grad_block
        weight_grads = [None] * depth
        for layer in reversed(range(depth)):
            normed, scale_inv = kept[layer]
            grad_values, gain_grad, shift_grad = norm_backward(
                grad_out, normed, scale_inv, gain_list[layer], frame_mask, frame_count
            )
            gain_grads[layer] = gain_grads[layer] + gain_grad
            shift_grads[layer] = shift_grads[layer] + shift_grad
            weight_grad, hidden_grad = conv_backward(
                inputs[layer], grad_values.astype(jnp.bfloat16), weights[layer]
            )
            weight_grads[layer] = weight_grad
            if layer > 0:
                before = kept[layer - 1]
                activated = jnp.tanh(gain_list[layer - 1] * before[0] + shift_list[layer - 1])
                grad_out = frame_mask * hidden_grad * (1.0 - activated * activated)
            else:
                input_grads.append((grad_block + frame_mask * hidden_grad).astype(jnp.bfloat16))
        local_grads = (
            jnp.swapaxes(weight_grads[0], 1, 2),
            jnp.stack(weight_grads[1 : depth - 1]),
            weight_grads[depth - 1],
        )
        pieces = (
            lax.psum_scatter(local_grads[0], "dp", scatter_dimension=1, tiled=True),
            lax.psum_scatter(local_grads[1], "dp", scatter_dimension=2, tiled=True),
            lax.psum_scatter(local_grads[2], "dp", scatter_dimension=1, tiled=True),
        )
        owned = tuple((total + piece for total, piece in zip(owned, pieces)))
    final_first, final_mid, final_last = jax.tree.map(
        lambda part: part.astype(jnp.float32), lax.psum(shortened(owned), "rep")
    )
    back_mel, back_grad = (
        lax.all_to_all(
            jnp.concatenate(refined, axis=0), "dp", split_axis=1, concat_axis=0, tiled=True
        ),
        lax.all_to_all(
            jnp.concatenate(input_grads, axis=0), "dp", split_axis=1, concat_axis=0, tiled=True
        ),
    )
    inverse = (
        jnp.zeros((group_size,), jnp.int32)
        .at[local_order]
        .set(jnp.arange(group_size, dtype=jnp.int32))
    )
    return (
        back_mel[inverse],
        back_grad[inverse],
        final_first,
        final_mid,
        final_last,
        jnp.stack(gain_grads[: depth - 1]),
        jnp.stack(shift_grads[: depth - 1]),
        gain_grads[depth - 1],
        shift_grads[depth - 1],
    )


def solution(mesh):
    in_specs = (
        P("rep", "dp", None),
        P("rep", "dp", None),
        P(),
        P(),
        P(None, "dp", None),
        P(None, None, "dp", None),
        P(None, "dp", None),
        P(),
        P(),
        P(),
        P(),
    )
    out_specs = (
        P("rep", "dp", None),
        P("rep", "dp", None),
        P(None, "dp", None),
        P(None, None, "dp", None),
        P(None, "dp", None),
        P(),
        P(),
        P(),
        P(),
    )
    step = local_kernel if mesh.shape["dp"] == SUB and mesh.shape["rep"] == CORES else local
    return jax.shard_map(step, mesh=mesh, in_specs=in_specs, out_specs=out_specs, check_vma=False)
```

```python
import functools

import jax
import jax.numpy as jnp
from jax import lax
from jax.experimental import pallas as pl
from jax.experimental.pallas import tpu as pltpu
from jax.sharding import PartitionSpec as P

MB = 2
PLANE = 4
CORES = 2
SUB = 16
LANES = 128
MESH = pl.DeviceIdType.MESH
bf16 = jnp.bfloat16
f32 = jnp.float32
EPS = 1e-05


def nn(a, b):
    return jnp.dot(a, b, preferred_element_type=f32)


def nt(a, b):
    return lax.dot_general(a, b, (((1,), (1,)), ((), ())), preferred_element_type=f32)


def tn(a, b):
    return lax.dot_general(a, b, (((0,), (0,)), ((), ())), preferred_element_type=f32)


def kernel(
    n_dp, utts, frames, chans, mels, taps, middle,
    len_s, reg_s, mel, gpost, wf, wm, wl, gains, shifts, gl, sl,
    o_mel, o_grad, o_wf, o_wm, o_wl, o_gains, o_shifts, o_gl, o_sl,
    mel_s, grd_s, bak_s, bak2_s, mel_r, grd_r, bak_r, bak2_r,
    whole, pad_m, pad_g, mel_p, grd_p, mask, h0, h, xh, z, zl, gz, gzl,
    W, WF, WL, GF, G1, rbufs,
    dr_s, dr_r, pl_s, pl_r, z_s, z_r, ar_t, a1, a2, a3, a4, invs, glp, slp, lens,
    drs_sem, drr_sem, pls_sem, plr_sem, zs_sem, zr_sem, a2a_s, a2a_r, gz_s, gz_r, gp_s, gp_r, gq_s, gq_r, gb_s, gb_r,
    r0_s, r0_r, r1_s, r1_r, r2_s, r2_r, r3_s, r3_r, ro_s, ro_r,
):
    nz = n_dp // PLANE
    total = n_dp * CORES
    T = n_dp * frames
    HALO = 2 * SUB
    MT = T // 2
    CL = chans // LANES
    ctile = 64
    dp = lax.axis_index("dp")
    rep = lax.axis_index("rep")
    zc = lax.div(dp, PLANE)
    s = lax.rem(dp, PLANE)
    sx = s + 1 - 2 * lax.rem(s, 2)
    sy = s + 2 - 4 * lax.div(s, 2)
    s1 = sx + rep * (sy - sx)
    s2 = sy + rep * (sx - sy)
    sd = 3 - s
    lin = dp * CORES + rep
    group = PLANE * CORES
    mine = s * CORES + rep
    other = 1 - rep
    sib = (dp, other)
    peer1 = (zc * PLANE + s1, rep)
    peer2 = (zc * PLANE + s2, rep)

    def send(src, dst, ss, rs, to):
        pltpu.make_async_remote_copy(
            src_ref=src, dst_ref=dst, send_sem=ss, recv_sem=rs, device_id=to, device_id_type=MESH
        ).start()

    def wait(ref, sem):
        pltpu.make_async_copy(ref, ref, sem).wait()

    W[:, :, zc, s] = wm[...]
    WF[:, zc, s] = jnp.zeros((taps, CORES) + WF.shape[4:], bf16)
    WL[:, zc, s] = jnp.zeros((taps, CORES) + WL.shape[4:], bf16)
    WF[:, zc, s, :, :, 0:mels] = wf[...]
    WL[:, zc, s, :, :, 0:mels] = wl[...]

    barrier = pltpu.get_barrier_semaphore()
    for i in range(1, total):
        to = lax.rem(lin + i, total)
        pl.semaphore_signal(
            barrier, inc=1, device_id=(lax.div(to, CORES), lax.rem(to, CORES)), device_id_type=MESH
        )

    lane = lax.broadcasted_iota(jnp.int32, (frames, LANES), 1)
    lane_b = lax.broadcasted_iota(jnp.int32, (SUB, LANES), 1)
    half = LANES // 2
    tail = mels - half
    parts = frames // SUB

    def pack(dst, j, vs):
        low = jnp.where(lane < half, vs[0], pltpu.roll(vs[1], half, 1))
        rest = jnp.zeros((SUB, LANES), f32)
        for m in range(MB):
            for r in range(parts):
                at = (m * parts + r) * tail
                piece = vs[m][r * SUB : (r + 1) * SUB, :]
                moved = pltpu.roll(piece, (at - half) % LANES, 1) if at != half else piece
                rest = jnp.where((lane_b >= at) & (lane_b < at + tail), moved, rest)
        dst[j, 0:frames, :] = low.astype(bf16)
        dst[j, frames : frames + SUB, :] = rest.astype(bf16)

    def unpack(src, j):
        low = src[j, 0:frames, :].astype(f32)
        rest = src[j, frames : frames + SUB, :].astype(f32)
        vs = []
        for m in range(MB):
            pieces = []
            for r in range(parts):
                shift = (half - (m * parts + r) * tail) % LANES
                pieces.append(pltpu.roll(rest, shift, 1) if shift else rest)
            high = jnp.where(lane < mels, jnp.concatenate(pieces, axis=0), 0.0)
            vs.append(jnp.where(lane < half, pltpu.roll(low, half, 1) if m else low, high))
        return vs

    pad_m[...] = jnp.zeros(pad_m.shape, f32)
    pad_g[...] = jnp.zeros(pad_g.shape, f32)

    def pack_pair(src, pad, dst):
        @pl.loop(0, n_dp)
        def _(j):
            for m in range(MB):
                pad[m, :, 0:mels] = src[reg_s[rep, j * MB + m]].astype(f32)
            pack(dst, j, [pad[m] for m in range(MB)])

    pack_pair(mel, pad_m, mel_s)

    pl.semaphore_wait(barrier, total - 1)

    def chunk(c):
        if c == 0:
            return WF
        if c == middle + 1:
            return WL
        return W.at[c - 1]

    units = []
    for layer in range(middle + 2):
        cuts = (0, 2, taps) if layer == 1 else (0, taps)
        units += [(layer, k0, k1) for k0, k1 in zip(cuts[:-1], cuts[1:])]

    def parts_of(c):
        return [
            (u, chunk(c).at[pl.ds(k0, k1 - k0)])
            for u, (layer, k0, k1) in enumerate(units)
            if layer == c
        ]

    def three(w):
        return w.at[:, pl.ds(0, nz - 1), 0, 0]

    def g0u(u, w):
        for i in range(1, nz):
            to = lax.rem(zc + i, nz) * PLANE + s
            piece = w.at[:, zc, s, rep]
            send(piece, piece, gz_s.at[u], gz_r.at[u], (to, rep))

    def g1u(u, w):
        wait(three(w), gz_r.at[u])
        col = w.at[:, :, s, rep]
        send(col, col, gp_s.at[u], gp_r.at[u], peer1)
        send(col, col, gq_s.at[u], gq_r.at[u], peer2)
        send(col, col, gb_s.at[u], gb_r.at[u], sib)

    def g2u(u, w):
        wait(w.at[:, :, 0, 0], gp_r.at[u])
        col = w.at[:, :, s1, rep]
        send(col, col, gq_s.at[u], gq_r.at[u], peer2)
        send(col, col, gb_s.at[u], gb_r.at[u], sib)

    def g3u(u, w):
        wait(w.at[:, :, pl.ds(0, 2), 0], gq_r.at[u])
        for q in (s2, sd):
            col = w.at[:, :, q, rep]
            send(col, col, gb_s.at[u], gb_r.at[u], sib)

    def g4u(u, w):
        wait(w.at[:, :, :, 0], gb_r.at[u])

    def gdrainu(u, w):
        wait(three(w), gz_s.at[u])
        wait(w.at[:, :, 0, 0], gp_s.at[u])
        wait(w.at[:, :, pl.ds(0, 2), 0], gq_s.at[u])
        wait(w.at[:, :, :, 0], gb_s.at[u])

    def each(fn):
        def run(c, only=None):
            for i, (u, w) in enumerate(parts_of(c)):
                if only is None or i == only:
                    fn(u, w)

        return run

    g0, g1, g2, g3, g4, gdrain = [each(f) for f in (g0u, g1u, g2u, g3u, g4u, gdrainu)]

    def deal(src, dst, which):
        for i in range(1, n_dp):
            to = lax.rem(dp + i, n_dp)
            send(src.at[to], dst.at[dp], a2a_s.at[which], a2a_r.at[which], (to, rep))
        dst[dp] = src[dp]

    def dealt(dst, which):
        wait(dst.at[pl.ds(0, n_dp - 1)], a2a_r.at[which])

    def spread(src, dst):
        for j in range(n_dp):
            for m, v in enumerate(unpack(src, j)):
                dst.at[m][pl.ds(j, frames, stride=SUB), :] = v

    def collect(src, dst):
        for j in range(n_dp):
            pack(dst, j, [src.at[m][pl.ds(j, frames, stride=SUB), :] for m in range(MB)])

    def restore(src, out):
        for j in range(n_dp):
            for m, v in enumerate(unpack(src, j)):
                whole[j * MB + m] = v.astype(bf16)

        @pl.loop(0, utts)
        def _(u):
            out[u] = whole[lens[u], :, 0:mels]

    direct = (middle + 2) * MB

    def ar_go(rd, vs):
        n = 8 // len(vs)
        if rd < direct:
            src, dst, slot = dr_s.at[rd], dr_r.at[rd], lin
        else:
            src, dst, slot = pl_s.at[rd - direct], pl_r.at[rd - direct], mine
        for e, v in enumerate(vs):
            for i in range(n):
                if (i + 1) * LANES <= v.shape[1]:
                    row = v[:, i * LANES : (i + 1) * LANES]
                else:
                    row = jnp.zeros((1, LANES), f32)
                at = e * n + i
                src[at : at + 1, :] = row
                dst[slot, at : at + 1, :] = row
        if rd < direct:
            for i in range(1, total):
                to = lax.rem(lin + i, total)
                send(
                    src, dst.at[lin], drs_sem.at[rd], drr_sem.at[rd],
                    (lax.div(to, CORES), lax.rem(to, CORES)),
                )
            return
        for i in range(1, group):
            to = lax.rem(mine + i, group)
            send(
                src, dst.at[mine], pls_sem.at[rd - direct], plr_sem.at[rd - direct],
                (zc * PLANE + lax.div(to, CORES), lax.rem(to, CORES)),
            )

    def ar_mid(rd):
        if rd < direct:
            return
        rd = rd - direct
        wait(pl_r.at[rd, pl.ds(0, group - 1)], plr_sem.at[rd])
        acc = pl_r[rd, 0]
        for i in range(1, group):
            acc = acc + pl_r[rd, i]
        z_s[rd] = acc
        z_r[rd, zc] = acc
        for i in range(1, nz):
            to = lax.rem(zc + i, nz) * PLANE + s
            send(z_s.at[rd], z_r.at[rd, zc], zs_sem.at[rd], zr_sem.at[rd], (to, rep))

    def ar_get(rd, n):
        if rd < direct:
            wait(dr_r.at[rd, pl.ds(0, total - 1)], drr_sem.at[rd])
            acc = dr_r[rd, 0]
            for i in range(1, total):
                acc = acc + dr_r[rd, i]
        else:
            wait(z_r.at[rd - direct, pl.ds(0, nz - 1)], zr_sem.at[rd - direct])
            acc = z_r[rd - direct, 0]
            for i in range(1, nz):
                acc = acc + z_r[rd - direct, i]
        ar_t[...] = acc
        q = CL if n == CL else 2
        return [
            jnp.concatenate([ar_t[e * q + i : e * q + i + 1, :] for i in range(n)], axis=1)
            for e in range(8 // q)
        ]

    def fold(v):
        return jnp.sum(v.reshape(v.shape[0] // 8, 8, v.shape[1]), axis=0)

    def wide(mk, d):
        return jnp.concatenate([mk] * (d // LANES), axis=1) if d > LANES else mk

    def clear(d):
        a1[:, 0:d] = jnp.zeros((8, d), f32)
        a2[:, 0:d] = jnp.zeros((8, d), f32)
        if d == LANES:
            a3[...] = jnp.zeros((8, d), f32)
            a4[...] = jnp.zeros((8, d), f32)

    def ar_acc(rd, d, before=None):
        if before is not None:
            ar_mid(before)
        accs = (a1, a2, a3, a4) if d == LANES else (a1, a2)
        ar_go(rd, [jnp.sum(v[:, 0:d], axis=0, keepdims=True) for v in accs])

    def halo(ref):
        d = ref.shape[1]
        row = lax.rem(lax.broadcasted_iota(jnp.int32, (HALO, d), 0), SUB)
        low = pltpu.roll(ref[T : T + HALO, :].astype(f32), 1, 0)
        ref[0:HALO, :] = jnp.where(row == 0, 0.0, low).astype(bf16)
        high = pltpu.roll(ref[HALO : 2 * HALO, :].astype(f32), HALO - 1, 0)
        ref[T + HALO : T + 2 * HALO, :] = jnp.where(row == SUB - 1, 0.0, high).astype(bf16)

    cnt = []
    own = []
    for m in range(MB):

        def body(j, c, m=m):
            for r in range(CORES):
                c = c + len_s[r * utts + reg_s[r, j * MB + m]]
            return c

        cnt.append(lax.fori_loop(0, n_dp, body, jnp.int32(0)).astype(f32))
        own.append(len_s[rep * utts + reg_s[rep, dp * MB + m]])

    last = middle + 1

    def mean_inv(rd, m, n):
        v1, v2 = ar_get(rd, n)
        mean = v1 / cnt[m]
        var = v2 / cnt[m] - mean * mean
        inv = lax.rsqrt(var + EPS)
        invs[rd, 0:1, 0 : n * LANES] = inv
        return mean, inv

    pairs = [tuple(range(k, min(k + 2, taps))) for k in range(0, taps, 2)]

    def joined(vs):
        return jnp.concatenate(vs, axis=1) if len(vs) > 1 else vs[0]

    def conv(layer, m):
        rd = layer * MB + m
        d = LANES if layer == last else chans
        dst = zl if layer == last else z
        clear(d)

        @pl.loop(0, T // MT)
        def _(t):
            base = pl.multiple_of(t * MT, MT)
            acc = None
            if layer == 0:
                for ks in pairs:
                    prod = nt(
                        joined([h0[m, pl.ds(base + SUB * k, MT), :] for k in ks]),
                        joined([WF[k].reshape(chans, LANES) for k in ks]),
                    )
                    acc = prod if acc is None else acc + prod
            else:
                for k in range(taps):
                    rows = pl.ds(base + SUB * k, MT)
                    if layer == last:
                        prod = nn(h[layer - 1, m, rows, :], WL[k].reshape(chans, LANES))
                    else:
                        prod = nn(h[layer - 1, m, rows, :], W[layer - 1, k].reshape(chans, chans))
                    acc = prod if acc is None else acc + prod
            dst[m, pl.ds(base, MT), :] = acc
            zm = acc * wide(mask[m, pl.ds(base, MT), :], d)
            a1[:, 0:d] += fold(zm)
            a2[:, 0:d] += fold(zm * acc)
            if layer == last:
                gy = mask[m, pl.ds(base, MT), :] * grd_p[m, pl.ds(base, MT), :]
                a3[...] += fold(gy)
                a4[...] += fold(gy * acc)

        ar_acc(rd, d, rd - m if m else None)

    def norm(layer, m):
        mean, inv = mean_inv(layer * MB + m, m, CL)
        g = gains[layer : layer + 1, :]
        b = shifts[layer : layer + 1, :]

        @pl.loop(0, T // ctile)
        def _(i):
            base = pl.multiple_of(i * ctile, ctile)
            rows = pl.ds(base, ctile)
            xv = (z[m, rows, :] - mean) * inv
            hv = wide(mask[m, rows, :], chans) * jnp.tanh(g * xv + b)
            xh[layer, m, rows, :] = xv.astype(bf16)
            h[layer, m, pl.ds(base + HALO, ctile), :] = hv.astype(bf16)

        halo(h.at[layer, m])

    def grad_tail(layer, m, base, acc):
        g = gains[layer : layer + 1, :]
        b = shifts[layer : layer + 1, :]
        rows = pl.ds(base, MT)
        xv = xh[layer, m, rows, :].astype(f32)
        th = jnp.tanh(g * xv + b)
        gy = wide(mask[m, rows, :], chans) * acc * (1.0 - th * th)
        z[m, rows, :] = gy
        a1[...] += fold(gy)
        a2[...] += fold(gy * xv)

    def bround(layer, m):
        return (last + 1 + layer) * MB + m

    def coefs(layer, m, n, g, og, os):
        v1, v2 = ar_get(bround(layer, m), n)
        og(v2, m > 0)
        os(v1, m > 0)
        a = g * invs[layer * MB + m, 0:1, 0 : n * LANES]
        return a, a * v1 / cnt[m], a * v2 / cnt[m]

    def grad_z(layer, m):
        def og(v, add):
            o_gains[layer : layer + 1, :] = v + o_gains[layer : layer + 1, :] if add else v

        def os(v, add):
            o_shifts[layer : layer + 1, :] = v + o_shifts[layer : layer + 1, :] if add else v

        a, c1, c2 = coefs(layer, m, CL, gains[layer : layer + 1, :], og, os)

        @pl.loop(0, T // ctile)
        def _(i):
            base = pl.multiple_of(i * ctile, ctile)
            rows = pl.ds(base, ctile)
            v = a * z[m, rows, :] - c1 - c2 * xh[layer, m, rows, :].astype(f32)
            gz[m, pl.ds(base + HALO, ctile), :] = (wide(mask[m, rows, :], chans) * v).astype(bf16)

        halo(gz.at[m])

    def grad_h(layer, m):
        clear(chans)

        @pl.loop(0, T // MT)
        def _(t):
            base = pl.multiple_of(t * MT, MT)
            acc = None
            if layer == last:
                for ks in pairs:
                    prod = nt(
                        joined([gzl[m, pl.ds(base + SUB * (taps - 1 - k), MT), :] for k in ks]),
                        joined([WL[k].reshape(chans, LANES) for k in ks]),
                    )
                    acc = prod if acc is None else acc + prod
            else:
                for k in range(taps):
                    rows = pl.ds(base + SUB * (taps - 1 - k), MT)
                    prod = nt(gz[m, rows, :], W[layer - 1, k].reshape(chans, chans))
                    acc = prod if acc is None else acc + prod
            grad_tail(layer - 1, m, base, acc)

        ar_acc(bround(layer - 1, m), chans, bround(layer - 1, 0) if m else None)

    def gchunk(layer):
        return GF if layer == 0 else G1 if layer == 1 else chunk(layer)

    def wgrad(layer, split=0, between=()):
        gdrain(layer)
        w = gchunk(layer)

        def narrow(ks):
            acc = None
            for m in range(MB):
                if layer == 0:
                    right = joined([h0[m, pl.ds(SUB * k, T), :] for k in ks])
                    prod = tn(gz[m, HALO : HALO + T, :], right)
                else:
                    right = joined([gzl[m, pl.ds(SUB * (taps - 1 - k), T), :] for k in ks])
                    prod = tn(h[layer - 1, m, HALO : HALO + T, :], right)
                acc = prod if acc is None else acc + prod
            for i, k in enumerate(ks):
                v = acc[:, i * LANES : (i + 1) * LANES]
                w[k] = v.astype(bf16).reshape(w.shape[1:])

        def one(k):
            rows = pl.ds(pl.multiple_of(SUB * (taps - 1 - k), SUB), T)
            acc = tn(h[layer - 1, 0, HALO : HALO + T, :], gz[0, rows, :])
            for m in range(1, MB):
                acc = acc + tn(h[layer - 1, m, HALO : HALO + T, :], gz[m, rows, :])
            w[k] = acc.astype(bf16).reshape(w.shape[1:])

        if layer in (0, last):
            for ks in pairs:
                narrow(ks)
        else:
            if split:
                pl.loop(0, split)(one)
                for fn, arg in between:
                    fn(arg)
            pl.loop(split, taps)(one)
        send(w.at[:, :, :, other], rbuf(layer)[0], r0_s.at[layer], r0_r.at[layer], sib)

    def rbuf(layer):
        return rbufs[layer]

    def total_of(a, b):
        return (a.astype(f32) + b.astype(f32)).astype(bf16)

    def ra(layer):
        w = gchunk(layer)
        r0, r1 = rbuf(layer)[0:2]
        wait(r0, r0_r.at[layer])
        for k in range(taps):
            r0[k] = total_of(r0[k], w[k, :, :, rep])
        for slot, q in ((1, sd), (0, s2)):
            send(r0.at[:, :, q], r1.at[slot], r1_s.at[layer], r1_r.at[layer], peer2)

    def rb(layer):
        r0, r1, r2 = rbuf(layer)[0:3]
        wait(r1, r1_r.at[layer])
        for slot, q in ((1, s1), (0, s)):
            for k in range(taps):
                r1[slot, k] = total_of(r1[slot, k], r0[k, :, q])
        send(r1.at[1], r2, r2_s.at[layer], r2_r.at[layer], peer1)

    def rc(layer):
        r1, r2, r3 = rbuf(layer)[1:4]
        wait(r2, r2_r.at[layer])
        for k in range(taps):
            r2[k] = total_of(r2[k], r1[0, k])
        for i in range(1, nz):
            zt = lax.rem(zc + i, nz)
            send(
                r2.at[:, zt], r3.at[i - 1], r3_s.at[layer], r3_r.at[layer],
                (zt * PLANE + s, rep),
            )

    def outs(layer):
        return o_wf if layer == 0 else o_wl if layer == last else o_wm.at[layer - 1]

    def rd_(layer):
        r2, r3 = rbuf(layer)[2:4]
        fs, fr = rbuf(layer)[4:6]
        wait(r3, r3_r.at[layer])
        out = outs(layer)
        for k in range(taps):
            v = r2[k, zc].astype(f32)
            for i in range(nz - 1):
                v = v + r3[i, k].astype(f32)
            fs[k] = v
            out[k, rep] = v[:, 0 : out.shape[3]]
        send(fs, fr, ro_s.at[layer], ro_r.at[layer], sib)

    def rdrain(layer):
        r0, r1, r2, r3, fs, fr = rbuf(layer)
        out = outs(layer)
        wait(fr, ro_r.at[layer])
        for k in range(taps):
            out[k, other] = fr[k][:, 0 : out.shape[3]]
        wait(fs, ro_s.at[layer])
        wait(r0, r0_s.at[layer])
        wait(r1, r1_s.at[layer])
        wait(r2, r2_s.at[layer])
        wait(r3, r3_s.at[layer])

    g0(0)
    g0(1)
    deal(mel_s, mel_r, 0)
    g0(2)
    glp[...] = jnp.zeros(glp.shape, f32)
    slp[...] = jnp.zeros(slp.shape, f32)
    glp[0:1, 0:mels] = gl[...]
    slp[0:1, 0:mels] = sl[...]
    for m in range(MB):

        @pl.loop(0, T // ctile)
        def _(i):
            base = pl.multiple_of(i * ctile, ctile)
            r = base + lax.broadcasted_iota(jnp.int32, (ctile, LANES), 0)
            t = lax.rem(r, SUB) * frames + lax.div(r, SUB)
            mask[m, pl.ds(base, ctile), :] = jnp.where(t < own[m], 1.0, 0.0)

    g1(0)
    g1(1, 0)
    g2(0)
    g1(1, 1)
    g3(0)
    g2(1, 0)

    @pl.loop(0, utts)
    def _(u):
        at = jnp.int32(0)
        for k in range(utts):
            at = jnp.where(reg_s[rep, k] == u, k, at)
        lens[u] = at

    pack_pair(gpost, pad_g, grd_s)
    dealt(mel_r, 0)
    spread(mel_r, mel_p)
    for m in range(MB):
        h0[m, HALO : HALO + T, :] = (mel_p[m] * mask[m]).astype(bf16)
        halo(h0.at[m])
        if m == 0:
            g4(0)
        if m == 0:
            g2(1, 1)
            g3(1, 0)
        conv(0, m)
    g1(2)
    g0(3)
    for layer in range(1, last + 1):
        ar_mid((layer - 1) * MB + 1)
        g3(layer, 1 if layer == 1 else None)
        g4(layer)
        for m in range(MB):
            norm(layer - 1, m)
            if layer == last and m == 0:
                dealt(grd_r, 1)
                spread(grd_r, grd_p)
            conv(layer, m)
            if m == 0:
                if layer + 1 <= last:
                    g2(layer + 1)
            else:
                if layer + 2 <= last:
                    g1(layer + 2)
                if layer + 3 <= last:
                    g0(layer + 3)
                if layer == 2:
                    deal(grd_s, grd_r, 1)

    ar_mid(last * MB + 1)
    g_last = glp[0:1, :]
    b_last = slp[0:1, :]
    ct = 64
    for m in range(MB):
        tot = ar_get(last * MB + m, 1)
        mean = tot[0] / cnt[m]
        var = tot[1] / cnt[m] - mean * mean
        inv = lax.rsqrt(var + EPS)
        v1 = tot[2]
        v2 = inv * (tot[3] - mean * v1)
        if m == 0:
            o_gl[...] = v2[:, 0:mels]
            o_sl[...] = v1[:, 0:mels]
        else:
            o_gl[...] = o_gl[...] + v2[:, 0:mels]
            o_sl[...] = o_sl[...] + v1[:, 0:mels]
        a = g_last * inv
        c1 = a * v1 / cnt[m]
        c2 = a * v2 / cnt[m]

        @pl.loop(0, T // ct)
        def _(i):
            base = pl.multiple_of(i * ct, ct)
            rows = pl.ds(base, ct)
            mk = mask[m, rows, :]
            xv = (zl[m, rows, :] - mean) * inv
            mel_p[m, rows, :] = mel_p[m, rows, :] + mk * (g_last * xv + b_last)
            v = a * grd_p[m, rows, :] - c1 - c2 * xv
            gzl[m, pl.ds(base + HALO, ct), :] = (mk * v).astype(bf16)

        halo(gzl.at[m])
        grad_h(last, m)
    wgrad(last)
    collect(mel_p, bak_s)
    ar_mid(bround(middle, 1))
    deal(bak_s, bak_r, 2)
    for layer in range(middle, 1, -1):
        for m in range(MB):
            grad_z(layer, m)
            grad_h(layer, m)
            if m == 0:
                ra(layer + 1)
        mid = (ar_mid, bround(layer - 1, 1))
        if layer + 1 == last:
            rb(layer + 1)
            wgrad(layer, 3, (mid, (rc, layer + 1)))
            rd_(layer + 1)
        else:
            wgrad(layer, 3, (mid, (rb, layer + 1)))
    for m in range(MB):
        grad_z(1, m)
    wgrad(1, 2, ((rc, 3), (ra, 2)) if middle > 2 else ())
    grad_h(1, 0)
    rb(2)
    rd_(3)
    grad_h(1, 1)
    ra(1)
    dealt(bak_r, 2)
    restore(bak_r, o_mel)
    ar_mid(bround(0, 1))
    rc(2)
    for m in range(MB):
        grad_z(0, m)
    wgrad(0)
    for m in range(MB):

        @pl.loop(0, T // MT)
        def _(t):
            base = pl.multiple_of(t * MT, MT)
            acc = None
            for k in range(taps):
                rows = pl.ds(base + SUB * (taps - 1 - k), MT)
                part = nn(gz[m, rows, :], WF[k].reshape(chans, LANES))
                acc = part if acc is None else acc + part
            rows = pl.ds(base, MT)
            grd_p[m, rows, :] = grd_p[m, rows, :] + mask[m, rows, :] * acc

    rb(1)
    collect(grd_p, bak2_s)
    deal(bak2_s, bak2_r, 3)
    ra(0)
    rd_(2)
    rc(1)
    rb(0)
    rc(0)
    dealt(bak2_r, 3)
    restore(bak2_r, o_grad)
    rd_(1)
    rd_(0)
    for layer in reversed(range(last + 1)):
        rdrain(layer)
    wait(mel_r.at[pl.ds(0, n_dp - 1)], a2a_s.at[0])
    wait(grd_r.at[pl.ds(0, n_dp - 1)], a2a_s.at[1])
    wait(bak_r.at[pl.ds(0, n_dp - 1)], a2a_s.at[2])
    wait(bak2_r.at[pl.ds(0, n_dp - 1)], a2a_s.at[3])

    @pl.loop(0, direct)
    def _(r):
        wait(dr_r.at[r, pl.ds(0, total - 1)], drs_sem.at[r])

    @pl.loop(0, last * MB)
    def _(r):
        wait(pl_r.at[r, pl.ds(0, group - 1)], pls_sem.at[r])
        wait(z_r.at[r, pl.ds(0, nz - 1)], zs_sem.at[r])


def local_kernel(
    mel, grad_post, lengths, regroup, w_first, w_mid, w_last, gains, shifts, gain_last, shift_last
):
    n_dp = lax.axis_size("dp")
    nz = n_dp // PLANE
    utts, frames, mels = mel.shape
    middle, taps, shard, chans = w_mid.shape
    depth = middle + 2
    T = n_dp * frames
    TH = T + 4 * SUB
    rows = shard // CORES
    direct = depth * MB
    rounds = (depth - 1) * MB
    V = pltpu.VMEM
    D = pltpu.SemaphoreType.DMA
    S = jax.ShapeDtypeStruct
    out_shape = (
        S(mel.shape, bf16),
        S(mel.shape, bf16),
        S((taps, CORES, rows, mels), f32),
        S((middle, taps, CORES, rows, chans), f32),
        S((taps, CORES, rows, mels), f32),
        S(gains.shape, f32),
        S(gains.shape, f32),
        S((1, mels), f32),
        S((1, mels), f32),
    )
    packed = V((n_dp, frames + SUB, LANES), bf16)
    landing = [
        [
            V((taps, nz, PLANE, rows, d), bf16),
            V((2, taps, nz, rows, d), bf16),
            V((taps, nz, rows, d), bf16),
            V((nz - 1, taps, rows, d), bf16),
            V((taps, rows, d), f32),
            V((taps, rows, d), f32),
        ]
        for d in [LANES] + [chans] * middle + [LANES]
    ]
    scratch = [
        packed, packed, packed, packed, packed, packed, packed, packed,
        V((utts, frames, LANES), bf16), V((MB, frames, LANES), f32), V((MB, frames, LANES), f32),
        V((MB, T, LANES), f32), V((MB, T, LANES), f32), V((MB, T, LANES), f32),
        V((MB, TH, LANES), bf16), V((middle + 1, MB, TH, chans), bf16),
        V((middle + 1, MB, T, chans), bf16),
        V((MB, T, chans), f32), V((MB, T, LANES), f32),
        V((MB, TH, chans), bf16), V((MB, TH, LANES), bf16),
        V((middle, taps, nz, PLANE, CORES, rows, chans), bf16),
        V((taps, nz, PLANE, CORES, rows, LANES), bf16),
        V((taps, nz, PLANE, CORES, rows, LANES), bf16),
        V((taps, nz, PLANE, CORES, rows, LANES), bf16),
        V((taps, nz, PLANE, CORES, rows, chans), bf16),
        landing,
        V((direct, 8, LANES), f32), V((direct, n_dp * CORES, 8, LANES), f32),
        V((rounds, 8, LANES), f32), V((rounds, PLANE * CORES, 8, LANES), f32),
        V((rounds, 8, LANES), f32), V((rounds, nz, 8, LANES), f32), V((8, LANES), f32),
        V((8, chans), f32), V((8, chans), f32), V((8, LANES), f32), V((8, LANES), f32), V((depth * MB, 8, chans), f32),
        V((8, LANES), f32), V((8, LANES), f32), pltpu.SMEM((utts,), jnp.int32),
        D((direct,)), D((direct,)),
        D((rounds,)), D((rounds,)), D((rounds,)), D((rounds,)), D((4,)), D((4,)),
    ] + [D((depth + 1,))] * 18
    body = functools.partial(kernel, n_dp, utts, frames, chans, mels, taps, middle)
    vmem = pl.BlockSpec(memory_space=pltpu.VMEM)
    smem = pl.BlockSpec(memory_space=pltpu.SMEM)
    out = pl.pallas_call(
        body,
        out_shape=out_shape,
        in_specs=[smem, smem] + [vmem] * 9,
        out_specs=(vmem,) * 9,
        scratch_shapes=scratch,
        compiler_params=pltpu.CompilerParams(
            collective_id=0, has_side_effects=True, vmem_limit_bytes=64 * 2**20
        ),
        name="postnet_step",
    )(
        lengths, regroup, mel, grad_post,
        w_first.reshape(taps, CORES, rows, mels),
        w_mid.reshape(middle, taps, CORES, rows, chans),
        w_last.reshape(taps, CORES, rows, mels),
        gains, shifts, gain_last[None, :], shift_last[None, :],
    )
    return (
        out[0], out[1],
        out[2].reshape(w_first.shape), out[3].reshape(w_mid.shape), out[4].reshape(w_last.shape),
        out[5], out[6], out[7][0], out[8][0],
    )


def shortened(value):

    def short(part):
        return part.astype(jnp.bfloat16) if part.dtype == jnp.float32 else part

    return jax.tree.map(short, value)


def shifted(hidden, offset):
    if offset == 0:
        return hidden
    frames = hidden.shape[1]
    reach = abs(offset)
    padded = jnp.pad(hidden, ((0, 0), (reach, reach), (0, 0)))
    return padded[:, reach + offset : reach + offset + frames]


def conv_forward(hidden, weight):
    centre = weight.shape[0] // 2
    running = jnp.einsum(
        "blc,cd->bld", shifted(hidden, -centre), weight[0], preferred_element_type=jnp.float32
    )
    for tap_index in range(1, weight.shape[0]):
        running = running + jnp.einsum(
            "blc,cd->bld",
            shifted(hidden, tap_index - centre),
            weight[tap_index],
            preferred_element_type=jnp.float32,
        )
    return running


def conv_backward(hidden, grad_values, weight):
    centre = weight.shape[0] // 2
    weight_grad = jnp.stack(
        [
            jnp.einsum(
                "blc,bld->cd",
                shifted(hidden, tap_index - centre),
                grad_values,
                preferred_element_type=jnp.float32,
            )
            for tap_index in range(weight.shape[0])
        ]
    )
    hidden_grad = jnp.einsum(
        "bld,cd->blc", shifted(grad_values, centre), weight[0], preferred_element_type=jnp.float32
    )
    for tap_index in range(1, weight.shape[0]):
        hidden_grad = hidden_grad + jnp.einsum(
            "bld,cd->blc",
            shifted(grad_values, centre - tap_index),
            weight[tap_index],
            preferred_element_type=jnp.float32,
        )
    return (weight_grad, hidden_grad)


def normalize(values, frame_mask, frame_count):
    first_sum, second_sum = lax.psum(
        (
            jnp.sum(values * frame_mask, axis=(0, 1)),
            jnp.sum(values * values * frame_mask, axis=(0, 1)),
        ),
        ("dp", "rep"),
    )
    centre = first_sum / frame_count
    spread = second_sum / frame_count - centre * centre
    scale_inv = lax.rsqrt(spread + 1e-05)
    return ((values - centre) * scale_inv, scale_inv)


def norm_backward(grad_out, normed, scale_inv, gain, frame_mask, frame_count):
    shift_grad, gain_grad = lax.psum(
        (jnp.sum(grad_out, axis=(0, 1)), jnp.sum(grad_out * normed, axis=(0, 1))), ("dp", "rep")
    )
    grad_values = (
        gain * scale_inv * (grad_out - shift_grad / frame_count - normed * gain_grad / frame_count)
    )
    return (frame_mask * grad_values, gain_grad, shift_grad)


def layer_list(fetched):
    middle = fetched[1].shape[0]
    return (
        [jnp.swapaxes(fetched[0], 1, 2)]
        + [fetched[1][layer] for layer in range(middle)]
        + [fetched[2]]
    )


def local(
    mel, grad_post, lengths, regroup, w_first, w_mid, w_last, gains, shifts, gain_last, shift_last
):
    devices_dp = lax.axis_size("dp")
    replicas = lax.axis_size("rep")
    dp_index = lax.axis_index("dp")
    rep_index = lax.axis_index("rep")
    group_size = regroup.shape[1]
    utt_dev = group_size // devices_dp
    utt_micro = utt_dev // MB
    frames_all = mel.shape[1] * devices_dp
    middle = w_mid.shape[0]
    offsets = (jnp.arange(replicas, dtype=jnp.int32) * group_size)[:, None]
    lens_order = lengths[(regroup + offsets).reshape(-1)].reshape(
        replicas, devices_dp, MB, utt_micro
    )
    counts = jnp.sum(lens_order, axis=(0, 1, 3)).astype(jnp.float32)
    own_lens = lax.dynamic_index_in_dim(
        lax.dynamic_index_in_dim(lens_order, rep_index, 0, False), dp_index, 0, False
    )
    frame_ids = jnp.arange(frames_all, dtype=jnp.int32)
    masks = (frame_ids[None, None, :] < own_lens[:, :, None]).astype(jnp.float32)[..., None]
    local_order = lax.dynamic_index_in_dim(regroup, rep_index, 0, False)
    moved_mel, moved_grad = (
        lax.all_to_all(mel[local_order], "dp", split_axis=0, concat_axis=1, tiled=True),
        lax.all_to_all(grad_post[local_order], "dp", split_axis=0, concat_axis=1, tiled=True),
    )
    gain_list = [gains[layer] for layer in range(middle + 1)] + [gain_last]
    shift_list = [shifts[layer] for layer in range(middle + 1)] + [shift_last]
    depth = middle + 2
    gain_grads = [jnp.zeros_like(entry) for entry in gain_list]
    shift_grads = [jnp.zeros_like(entry) for entry in shift_list]
    owned = (
        jnp.zeros(w_first.shape, jnp.float32),
        jnp.zeros(w_mid.shape, jnp.float32),
        jnp.zeros(w_last.shape, jnp.float32),
    )
    refined = []
    input_grads = []
    for micro_index in range(MB):
        mel_block = moved_mel[micro_index * utt_micro : (micro_index + 1) * utt_micro]
        grad_block = moved_grad[micro_index * utt_micro : (micro_index + 1) * utt_micro].astype(
            jnp.float32
        )
        frame_mask = masks[micro_index]
        frame_count = counts[micro_index]
        fetched = (
            lax.all_gather(w_first, "dp", axis=1, tiled=True),
            lax.all_gather(w_mid, "dp", axis=2, tiled=True),
            lax.all_gather(w_last, "dp", axis=1, tiled=True),
        )
        weights = layer_list(fetched)
        hidden = (mel_block.astype(jnp.float32) * frame_mask).astype(jnp.bfloat16)
        inputs = []
        kept = []
        for layer in range(depth):
            inputs.append(hidden)
            normed, scale_inv = normalize(
                conv_forward(hidden, weights[layer]), frame_mask, frame_count
            )
            kept.append((normed, scale_inv))
            activated = gain_list[layer] * normed + shift_list[layer]
            if layer < depth - 1:
                hidden = (frame_mask * jnp.tanh(activated)).astype(jnp.bfloat16)
            else:
                refined.append(
                    (mel_block.astype(jnp.float32) + frame_mask * activated).astype(jnp.bfloat16)
                )
        fetched = (
            lax.all_gather(w_first, "dp", axis=1, tiled=True),
            lax.all_gather(w_mid, "dp", axis=2, tiled=True),
            lax.all_gather(w_last, "dp", axis=1, tiled=True),
        )
        weights = layer_list(fetched)
        grad_out = frame_mask * grad_block
        weight_grads = [None] * depth
        for layer in reversed(range(depth)):
            normed, scale_inv = kept[layer]
            grad_values, gain_grad, shift_grad = norm_backward(
                grad_out, normed, scale_inv, gain_list[layer], frame_mask, frame_count
            )
            gain_grads[layer] = gain_grads[layer] + gain_grad
            shift_grads[layer] = shift_grads[layer] + shift_grad
            weight_grad, hidden_grad = conv_backward(
                inputs[layer], grad_values.astype(jnp.bfloat16), weights[layer]
            )
            weight_grads[layer] = weight_grad
            if layer > 0:
                before = kept[layer - 1]
                activated = jnp.tanh(gain_list[layer - 1] * before[0] + shift_list[layer - 1])
                grad_out = frame_mask * hidden_grad * (1.0 - activated * activated)
            else:
                input_grads.append((grad_block + frame_mask * hidden_grad).astype(jnp.bfloat16))
        local_grads = (
            jnp.swapaxes(weight_grads[0], 1, 2),
            jnp.stack(weight_grads[1 : depth - 1]),
            weight_grads[depth - 1],
        )
        pieces = (
            lax.psum_scatter(local_grads[0], "dp", scatter_dimension=1, tiled=True),
            lax.psum_scatter(local_grads[1], "dp", scatter_dimension=2, tiled=True),
            lax.psum_scatter(local_grads[2], "dp", scatter_dimension=1, tiled=True),
        )
        owned = tuple((total + piece for total, piece in zip(owned, pieces)))
    final_first, final_mid, final_last = jax.tree.map(
        lambda part: part.astype(jnp.float32), lax.psum(shortened(owned), "rep")
    )
    back_mel, back_grad = (
        lax.all_to_all(
            jnp.concatenate(refined, axis=0), "dp", split_axis=1, concat_axis=0, tiled=True
        ),
        lax.all_to_all(
            jnp.concatenate(input_grads, axis=0), "dp", split_axis=1, concat_axis=0, tiled=True
        ),
    )
    inverse = (
        jnp.zeros((group_size,), jnp.int32)
        .at[local_order]
        .set(jnp.arange(group_size, dtype=jnp.int32))
    )
    return (
        back_mel[inverse],
        back_grad[inverse],
        final_first,
        final_mid,
        final_last,
        jnp.stack(gain_grads[: depth - 1]),
        jnp.stack(shift_grads[: depth - 1]),
        gain_grads[depth - 1],
        shift_grads[depth - 1],
    )


def solution(mesh):
    in_specs = (
        P("rep", "dp", None),
        P("rep", "dp", None),
        P(),
        P(),
        P(None, "dp", None),
        P(None, None, "dp", None),
        P(None, "dp", None),
        P(),
        P(),
        P(),
        P(),
    )
    out_specs = (
        P("rep", "dp", None),
        P("rep", "dp", None),
        P(None, "dp", None),
        P(None, None, "dp", None),
        P(None, "dp", None),
        P(),
        P(),
        P(),
        P(),
    )
    step = local_kernel if mesh.shape["dp"] == SUB and mesh.shape["rep"] == CORES else local
    return jax.shard_map(step, mesh=mesh, in_specs=in_specs, out_specs=out_specs, check_vma=False)
```

```python
import functools

import jax
import jax.numpy as jnp
from jax import lax
from jax.experimental import pallas as pl
from jax.experimental.pallas import tpu as pltpu
from jax.sharding import PartitionSpec as P

MB = 2
PLANE = 4
CORES = 2
SUB = 16
LANES = 128
MESH = pl.DeviceIdType.MESH
bf16 = jnp.bfloat16
f32 = jnp.float32
EPS = 1e-05


def nn(a, b):
    return jnp.dot(a, b, preferred_element_type=f32)


def nt(a, b):
    return lax.dot_general(a, b, (((1,), (1,)), ((), ())), preferred_element_type=f32)


def tn(a, b):
    return lax.dot_general(a, b, (((0,), (0,)), ((), ())), preferred_element_type=f32)


def kernel(
    n_dp, utts, frames, chans, mels, taps, middle,
    len_s, reg_s, mel, gpost, wf, wm, wl, gains, shifts, gl, sl,
    o_mel, o_grad, o_wf, o_wm, o_wl, o_gains, o_shifts, o_gl, o_sl,
    mel_s, grd_s, bak_s, bak2_s, mel_r, grd_r, bak_r, bak2_r,
    whole, pad_m, pad_g, mel_p, grd_p, mask, h0, h, xh, z, zl, gz, gzl,
    W, WF, WL, GF, G1, rbufs,
    dr_s, dr_r, pl_s, pl_r, z_s, z_r, ar_t, a1, a2, a3, a4, invs, glp, slp, lens,
    drs_sem, drr_sem, pls_sem, plr_sem, zs_sem, zr_sem, a2a_s, a2a_r, gz_s, gz_r, gp_s, gp_r, gq_s, gq_r, gb_s, gb_r,
    r0_s, r0_r, r1_s, r1_r, r2_s, r2_r, r3_s, r3_r, ro_s, ro_r,
):
    nz = n_dp // PLANE
    total = n_dp * CORES
    T = n_dp * frames
    HALO = 2 * SUB
    MT = T // 2
    CL = chans // LANES
    ctile = 64
    dp = lax.axis_index("dp")
    rep = lax.axis_index("rep")
    zc = lax.div(dp, PLANE)
    s = lax.rem(dp, PLANE)
    sx = s + 1 - 2 * lax.rem(s, 2)
    sy = s + 2 - 4 * lax.div(s, 2)
    s1 = sx + rep * (sy - sx)
    s2 = sy + rep * (sx - sy)
    sd = 3 - s
    lin = dp * CORES + rep
    group = PLANE * CORES
    mine = s * CORES + rep
    other = 1 - rep
    sib = (dp, other)
    peer1 = (zc * PLANE + s1, rep)
    peer2 = (zc * PLANE + s2, rep)

    def send(src, dst, ss, rs, to):
        pltpu.make_async_remote_copy(
            src_ref=src, dst_ref=dst, send_sem=ss, recv_sem=rs, device_id=to, device_id_type=MESH
        ).start()

    def wait(ref, sem):
        pltpu.make_async_copy(ref, ref, sem).wait()

    W[:, :, zc, s] = wm[...]
    WF[:, zc, s] = jnp.zeros((taps, CORES) + WF.shape[4:], bf16)
    WL[:, zc, s] = jnp.zeros((taps, CORES) + WL.shape[4:], bf16)
    WF[:, zc, s, :, :, 0:mels] = wf[...]
    WL[:, zc, s, :, :, 0:mels] = wl[...]

    barrier = pltpu.get_barrier_semaphore()
    for i in range(1, total):
        to = lax.rem(lin + i, total)
        pl.semaphore_signal(
            barrier, inc=1, device_id=(lax.div(to, CORES), lax.rem(to, CORES)), device_id_type=MESH
        )

    lane = lax.broadcasted_iota(jnp.int32, (frames, LANES), 1)
    lane_b = lax.broadcasted_iota(jnp.int32, (SUB, LANES), 1)
    half = LANES // 2
    tail = mels - half
    parts = frames // SUB

    def pack(dst, j, vs):
        low = jnp.where(lane < half, vs[0], pltpu.roll(vs[1], half, 1))
        rest = jnp.zeros((SUB, LANES), f32)
        for m in range(MB):
            for r in range(parts):
                at = (m * parts + r) * tail
                piece = vs[m][r * SUB : (r + 1) * SUB, :]
                moved = pltpu.roll(piece, (at - half) % LANES, 1) if at != half else piece
                rest = jnp.where((lane_b >= at) & (lane_b < at + tail), moved, rest)
        dst[j, 0:frames, :] = low.astype(bf16)
        dst[j, frames : frames + SUB, :] = rest.astype(bf16)

    def unpack(src, j):
        low = src[j, 0:frames, :].astype(f32)
        rest = src[j, frames : frames + SUB, :].astype(f32)
        vs = []
        for m in range(MB):
            pieces = []
            for r in range(parts):
                shift = (half - (m * parts + r) * tail) % LANES
                pieces.append(pltpu.roll(rest, shift, 1) if shift else rest)
            high = jnp.where(lane < mels, jnp.concatenate(pieces, axis=0), 0.0)
            vs.append(jnp.where(lane < half, pltpu.roll(low, half, 1) if m else low, high))
        return vs

    pad_m[...] = jnp.zeros(pad_m.shape, f32)
    pad_g[...] = jnp.zeros(pad_g.shape, f32)

    def pack_pair(src, pad, dst):
        @pl.loop(0, n_dp)
        def _(j):
            for m in range(MB):
                pad[m, :, 0:mels] = src[reg_s[rep, j * MB + m]].astype(f32)
            pack(dst, j, [pad[m] for m in range(MB)])

    pack_pair(mel, pad_m, mel_s)

    pl.semaphore_wait(barrier, total - 1)

    def chunk(c):
        if c == 0:
            return WF
        if c == middle + 1:
            return WL
        return W.at[c - 1]

    units = []
    for layer in range(middle + 2):
        cuts = (0, 2, taps) if layer == 1 else (0, taps)
        units += [(layer, k0, k1) for k0, k1 in zip(cuts[:-1], cuts[1:])]

    def parts_of(c):
        return [
            (u, chunk(c).at[pl.ds(k0, k1 - k0)])
            for u, (layer, k0, k1) in enumerate(units)
            if layer == c
        ]

    def three(w):
        return w.at[:, pl.ds(0, nz - 1), 0, 0]

    def g0u(u, w):
        for i in range(1, nz):
            to = lax.rem(zc + i, nz) * PLANE + s
            piece = w.at[:, zc, s, rep]
            send(piece, piece, gz_s.at[u], gz_r.at[u], (to, rep))

    def g1u(u, w):
        wait(three(w), gz_r.at[u])
        col = w.at[:, :, s, rep]
        send(col, col, gp_s.at[u], gp_r.at[u], peer1)
        send(col, col, gq_s.at[u], gq_r.at[u], peer2)
        send(col, col, gb_s.at[u], gb_r.at[u], sib)

    def g2u(u, w):
        wait(w.at[:, :, 0, 0], gp_r.at[u])
        col = w.at[:, :, s1, rep]
        send(col, col, gq_s.at[u], gq_r.at[u], peer2)
        send(col, col, gb_s.at[u], gb_r.at[u], sib)

    def g3u(u, w):
        wait(w.at[:, :, pl.ds(0, 2), 0], gq_r.at[u])
        for q in (s2, sd):
            col = w.at[:, :, q, rep]
            send(col, col, gb_s.at[u], gb_r.at[u], sib)

    def g4u(u, w):
        wait(w.at[:, :, :, 0], gb_r.at[u])

    def gdrainu(u, w):
        wait(three(w), gz_s.at[u])
        wait(w.at[:, :, 0, 0], gp_s.at[u])
        wait(w.at[:, :, pl.ds(0, 2), 0], gq_s.at[u])
        wait(w.at[:, :, :, 0], gb_s.at[u])

    def each(fn):
        def run(c, only=None):
            for i, (u, w) in enumerate(parts_of(c)):
                if only is None or i == only:
                    fn(u, w)

        return run

    g0, g1, g2, g3, g4, gdrain = [each(f) for f in (g0u, g1u, g2u, g3u, g4u, gdrainu)]

    def deal(src, dst, which):
        for i in range(1, n_dp):
            to = lax.rem(dp + i, n_dp)
            send(src.at[to], dst.at[dp], a2a_s.at[which], a2a_r.at[which], (to, rep))
        dst[dp] = src[dp]

    def dealt(dst, which):
        wait(dst.at[pl.ds(0, n_dp - 1)], a2a_r.at[which])

    def spread(src, dst):
        for j in range(n_dp):
            for m, v in enumerate(unpack(src, j)):
                dst.at[m][pl.ds(j, frames, stride=SUB), :] = v

    def collect(src, dst):
        for j in range(n_dp):
            pack(dst, j, [src.at[m][pl.ds(j, frames, stride=SUB), :] for m in range(MB)])

    def restore(src, out):
        for j in range(n_dp):
            for m, v in enumerate(unpack(src, j)):
                whole[j * MB + m] = v.astype(bf16)

        @pl.loop(0, utts)
        def _(u):
            out[u] = whole[lens[u], :, 0:mels]

    all_rounds = (2 * (middle + 2) - 1) * MB
    exposed = [(middle + 2) * MB + m for m in range(MB)]
    exposed += [(middle + 2 + middle) * MB + m for m in range(MB)]
    straight = list(range((middle + 2) * MB)) + exposed
    stepped = [r for r in range(all_rounds) if r not in straight]

    def ar_go(rd, vs):
        n = 8 // len(vs)
        plain = rd in straight
        rd = straight.index(rd) if plain else stepped.index(rd)
        if plain:
            src, dst, slot = dr_s.at[rd], dr_r.at[rd], lin
        else:
            src, dst, slot = pl_s.at[rd], pl_r.at[rd], mine
        for e, v in enumerate(vs):
            for i in range(n):
                if (i + 1) * LANES <= v.shape[1]:
                    row = v[:, i * LANES : (i + 1) * LANES]
                else:
                    row = jnp.zeros((1, LANES), f32)
                at = e * n + i
                src[at : at + 1, :] = row
                dst[slot, at : at + 1, :] = row
        if plain:
            for i in range(1, total):
                to = lax.rem(lin + i, total)
                send(
                    src, dst.at[lin], drs_sem.at[rd], drr_sem.at[rd],
                    (lax.div(to, CORES), lax.rem(to, CORES)),
                )
            return
        for i in range(1, group):
            to = lax.rem(mine + i, group)
            send(
                src, dst.at[mine], pls_sem.at[rd], plr_sem.at[rd],
                (zc * PLANE + lax.div(to, CORES), lax.rem(to, CORES)),
            )

    def ar_mid(rd):
        if rd in straight:
            return
        rd = stepped.index(rd)
        wait(pl_r.at[rd, pl.ds(0, group - 1)], plr_sem.at[rd])
        acc = pl_r[rd, 0]
        for i in range(1, group):
            acc = acc + pl_r[rd, i]
        z_s[rd] = acc
        z_r[rd, zc] = acc
        for i in range(1, nz):
            to = lax.rem(zc + i, nz) * PLANE + s
            send(z_s.at[rd], z_r.at[rd, zc], zs_sem.at[rd], zr_sem.at[rd], (to, rep))

    def ar_get(rd, n):
        if rd in straight:
            rd = straight.index(rd)
            wait(dr_r.at[rd, pl.ds(0, total - 1)], drr_sem.at[rd])
            acc = dr_r[rd, 0]
            for i in range(1, total):
                acc = acc + dr_r[rd, i]
        else:
            rd = stepped.index(rd)
            wait(z_r.at[rd, pl.ds(0, nz - 1)], zr_sem.at[rd])
            acc = z_r[rd, 0]
            for i in range(1, nz):
                acc = acc + z_r[rd, i]
        ar_t[...] = acc
        q = CL if n == CL else 2
        return [
            jnp.concatenate([ar_t[e * q + i : e * q + i + 1, :] for i in range(n)], axis=1)
            for e in range(8 // q)
        ]

    def fold(v):
        return jnp.sum(v.reshape(v.shape[0] // 8, 8, v.shape[1]), axis=0)

    def wide(mk, d):
        return jnp.concatenate([mk] * (d // LANES), axis=1) if d > LANES else mk

    def clear(d):
        a1[:, 0:d] = jnp.zeros((8, d), f32)
        a2[:, 0:d] = jnp.zeros((8, d), f32)
        if d == LANES:
            a3[...] = jnp.zeros((8, d), f32)
            a4[...] = jnp.zeros((8, d), f32)

    def ar_acc(rd, d, before=None):
        if before is not None:
            ar_mid(before)
        accs = (a1, a2, a3, a4) if d == LANES else (a1, a2)
        ar_go(rd, [jnp.sum(v[:, 0:d], axis=0, keepdims=True) for v in accs])

    def halo(ref):
        d = ref.shape[1]
        row = lax.rem(lax.broadcasted_iota(jnp.int32, (HALO, d), 0), SUB)
        low = pltpu.roll(ref[T : T + HALO, :].astype(f32), 1, 0)
        ref[0:HALO, :] = jnp.where(row == 0, 0.0, low).astype(bf16)
        high = pltpu.roll(ref[HALO : 2 * HALO, :].astype(f32), HALO - 1, 0)
        ref[T + HALO : T + 2 * HALO, :] = jnp.where(row == SUB - 1, 0.0, high).astype(bf16)

    cnt = []
    own = []
    for m in range(MB):

        def body(j, c, m=m):
            for r in range(CORES):
                c = c + len_s[r * utts + reg_s[r, j * MB + m]]
            return c

        cnt.append(lax.fori_loop(0, n_dp, body, jnp.int32(0)).astype(f32))
        own.append(len_s[rep * utts + reg_s[rep, dp * MB + m]])

    last = middle + 1

    def mean_inv(rd, m, n):
        v1, v2 = ar_get(rd, n)
        mean = v1 / cnt[m]
        var = v2 / cnt[m] - mean * mean
        inv = lax.rsqrt(var + EPS)
        invs[rd, 0:1, 0 : n * LANES] = inv
        return mean, inv

    pairs = [tuple(range(k, min(k + 2, taps))) for k in range(0, taps, 2)]

    def joined(vs):
        return jnp.concatenate(vs, axis=1) if len(vs) > 1 else vs[0]

    def conv(layer, m):
        rd = layer * MB + m
        d = LANES if layer == last else chans
        dst = zl if layer == last else z
        clear(d)

        @pl.loop(0, T // MT)
        def _(t):
            base = pl.multiple_of(t * MT, MT)
            acc = None
            if layer == 0:
                for ks in pairs:
                    prod = nt(
                        joined([h0[m, pl.ds(base + SUB * k, MT), :] for k in ks]),
                        joined([WF[k].reshape(chans, LANES) for k in ks]),
                    )
                    acc = prod if acc is None else acc + prod
            else:
                for k in range(taps):
                    rows = pl.ds(base + SUB * k, MT)
                    if layer == last:
                        prod = nn(h[layer - 1, m, rows, :], WL[k].reshape(chans, LANES))
                    else:
                        prod = nn(h[layer - 1, m, rows, :], W[layer - 1, k].reshape(chans, chans))
                    acc = prod if acc is None else acc + prod
            dst[m, pl.ds(base, MT), :] = acc
            zm = acc * wide(mask[m, pl.ds(base, MT), :], d)
            a1[:, 0:d] += fold(zm)
            a2[:, 0:d] += fold(zm * acc)
            if layer == last:
                gy = mask[m, pl.ds(base, MT), :] * grd_p[m, pl.ds(base, MT), :]
                a3[...] += fold(gy)
                a4[...] += fold(gy * acc)

        ar_acc(rd, d, rd - m if m else None)

    def norm(layer, m):
        mean, inv = mean_inv(layer * MB + m, m, CL)
        g = gains[layer : layer + 1, :]
        b = shifts[layer : layer + 1, :]

        @pl.loop(0, T // ctile)
        def _(i):
            base = pl.multiple_of(i * ctile, ctile)
            rows = pl.ds(base, ctile)
            xv = (z[m, rows, :] - mean) * inv
            hv = wide(mask[m, rows, :], chans) * jnp.tanh(g * xv + b)
            xh[layer, m, rows, :] = xv.astype(bf16)
            h[layer, m, pl.ds(base + HALO, ctile), :] = hv.astype(bf16)

        halo(h.at[layer, m])

    def grad_tail(layer, m, base, acc):
        g = gains[layer : layer + 1, :]
        b = shifts[layer : layer + 1, :]
        rows = pl.ds(base, MT)
        xv = xh[layer, m, rows, :].astype(f32)
        th = jnp.tanh(g * xv + b)
        gy = wide(mask[m, rows, :], chans) * acc * (1.0 - th * th)
        z[m, rows, :] = gy
        a1[...] += fold(gy)
        a2[...] += fold(gy * xv)

    def bround(layer, m):
        return (last + 1 + layer) * MB + m

    def coefs(layer, m, n, g, og, os):
        v1, v2 = ar_get(bround(layer, m), n)
        og(v2, m > 0)
        os(v1, m > 0)
        a = g * invs[layer * MB + m, 0:1, 0 : n * LANES]
        return a, a * v1 / cnt[m], a * v2 / cnt[m]

    def grad_z(layer, m):
        def og(v, add):
            o_gains[layer : layer + 1, :] = v + o_gains[layer : layer + 1, :] if add else v

        def os(v, add):
            o_shifts[layer : layer + 1, :] = v + o_shifts[layer : layer + 1, :] if add else v

        a, c1, c2 = coefs(layer, m, CL, gains[layer : layer + 1, :], og, os)

        @pl.loop(0, T // ctile)
        def _(i):
            base = pl.multiple_of(i * ctile, ctile)
            rows = pl.ds(base, ctile)
            v = a * z[m, rows, :] - c1 - c2 * xh[layer, m, rows, :].astype(f32)
            gz[m, pl.ds(base + HALO, ctile), :] = (wide(mask[m, rows, :], chans) * v).astype(bf16)

        halo(gz.at[m])

    def grad_h(layer, m):
        clear(chans)

        @pl.loop(0, T // MT)
        def _(t):
            base = pl.multiple_of(t * MT, MT)
            acc = None
            if layer == last:
                for ks in pairs:
                    prod = nt(
                        joined([gzl[m, pl.ds(base + SUB * (taps - 1 - k), MT), :] for k in ks]),
                        joined([WL[k].reshape(chans, LANES) for k in ks]),
                    )
                    acc = prod if acc is None else acc + prod
            else:
                for k in range(taps):
                    rows = pl.ds(base + SUB * (taps - 1 - k), MT)
                    prod = nt(gz[m, rows, :], W[layer - 1, k].reshape(chans, chans))
                    acc = prod if acc is None else acc + prod
            grad_tail(layer - 1, m, base, acc)

        ar_acc(bround(layer - 1, m), chans, bround(layer - 1, 0) if m else None)

    def gchunk(layer):
        return GF if layer == 0 else G1 if layer == 1 else chunk(layer)

    def wgrad(layer, split=0, between=()):
        gdrain(layer)
        w = gchunk(layer)

        def narrow(ks):
            acc = None
            for m in range(MB):
                if layer == 0:
                    right = joined([h0[m, pl.ds(SUB * k, T), :] for k in ks])
                    prod = tn(gz[m, HALO : HALO + T, :], right)
                else:
                    right = joined([gzl[m, pl.ds(SUB * (taps - 1 - k), T), :] for k in ks])
                    prod = tn(h[layer - 1, m, HALO : HALO + T, :], right)
                acc = prod if acc is None else acc + prod
            for i, k in enumerate(ks):
                v = acc[:, i * LANES : (i + 1) * LANES]
                w[k] = v.astype(bf16).reshape(w.shape[1:])

        def one(k):
            rows = pl.ds(pl.multiple_of(SUB * (taps - 1 - k), SUB), T)
            acc = tn(h[layer - 1, 0, HALO : HALO + T, :], gz[0, rows, :])
            for m in range(1, MB):
                acc = acc + tn(h[layer - 1, m, HALO : HALO + T, :], gz[m, rows, :])
            w[k] = acc.astype(bf16).reshape(w.shape[1:])

        if layer in (0, last):
            for ks in pairs:
                narrow(ks)
        else:
            if split:
                pl.loop(0, split)(one)
                for fn, arg in between:
                    fn(arg)
            pl.loop(split, taps)(one)
        send(w.at[:, :, :, other], rbuf(layer)[0], r0_s.at[layer], r0_r.at[layer], sib)

    def rbuf(layer):
        return rbufs[layer]

    def total_of(a, b):
        return (a.astype(f32) + b.astype(f32)).astype(bf16)

    def ra(layer):
        w = gchunk(layer)
        r0, r1 = rbuf(layer)[0:2]
        wait(r0, r0_r.at[layer])
        for k in range(taps):
            r0[k] = total_of(r0[k], w[k, :, :, rep])
        for slot, q in ((1, sd), (0, s2)):
            send(r0.at[:, :, q], r1.at[slot], r1_s.at[layer], r1_r.at[layer], peer2)

    def rb(layer):
        r0, r1, r2 = rbuf(layer)[0:3]
        wait(r1, r1_r.at[layer])
        for slot, q in ((1, s1), (0, s)):
            for k in range(taps):
                r1[slot, k] = total_of(r1[slot, k], r0[k, :, q])
        send(r1.at[1], r2, r2_s.at[layer], r2_r.at[layer], peer1)

    def rc(layer):
        r1, r2, r3 = rbuf(layer)[1:4]
        wait(r2, r2_r.at[layer])
        for k in range(taps):
            r2[k] = total_of(r2[k], r1[0, k])
        for i in range(1, nz):
            zt = lax.rem(zc + i, nz)
            send(
                r2.at[:, zt], r3.at[i - 1], r3_s.at[layer], r3_r.at[layer],
                (zt * PLANE + s, rep),
            )

    def outs(layer):
        return o_wf if layer == 0 else o_wl if layer == last else o_wm.at[layer - 1]

    def rd_(layer):
        r2, r3 = rbuf(layer)[2:4]
        fs, fr = rbuf(layer)[4:6]
        wait(r3, r3_r.at[layer])
        out = outs(layer)
        for k in range(taps):
            v = r2[k, zc].astype(f32)
            for i in range(nz - 1):
                v = v + r3[i, k].astype(f32)
            fs[k] = v
            out[k, rep] = v[:, 0 : out.shape[3]]
        send(fs, fr, ro_s.at[layer], ro_r.at[layer], sib)

    def rdrain(layer):
        r0, r1, r2, r3, fs, fr = rbuf(layer)
        out = outs(layer)
        wait(fr, ro_r.at[layer])
        for k in range(taps):
            out[k, other] = fr[k][:, 0 : out.shape[3]]
        wait(fs, ro_s.at[layer])
        wait(r0, r0_s.at[layer])
        wait(r1, r1_s.at[layer])
        wait(r2, r2_s.at[layer])
        wait(r3, r3_s.at[layer])

    g0(0)
    g0(1)
    deal(mel_s, mel_r, 0)
    g0(2)
    glp[...] = jnp.zeros(glp.shape, f32)
    slp[...] = jnp.zeros(slp.shape, f32)
    glp[0:1, 0:mels] = gl[...]
    slp[0:1, 0:mels] = sl[...]
    for m in range(MB):

        @pl.loop(0, T // ctile)
        def _(i):
            base = pl.multiple_of(i * ctile, ctile)
            r = base + lax.broadcasted_iota(jnp.int32, (ctile, LANES), 0)
            t = lax.rem(r, SUB) * frames + lax.div(r, SUB)
            mask[m, pl.ds(base, ctile), :] = jnp.where(t < own[m], 1.0, 0.0)

    g1(0)
    g1(1, 0)
    g2(0)
    g1(1, 1)
    g3(0)
    g2(1, 0)

    @pl.loop(0, utts)
    def _(u):
        at = jnp.int32(0)
        for k in range(utts):
            at = jnp.where(reg_s[rep, k] == u, k, at)
        lens[u] = at

    pack_pair(gpost, pad_g, grd_s)
    dealt(mel_r, 0)
    spread(mel_r, mel_p)
    for m in range(MB):
        h0[m, HALO : HALO + T, :] = (mel_p[m] * mask[m]).astype(bf16)
        halo(h0.at[m])
        if m == 0:
            g4(0)
        if m == 0:
            g2(1, 1)
            g3(1, 0)
        conv(0, m)
    g1(2)
    g0(3)
    for layer in range(1, last + 1):
        ar_mid((layer - 1) * MB + 1)
        g3(layer, 1 if layer == 1 else None)
        g4(layer)
        for m in range(MB):
            norm(layer - 1, m)
            if layer == last and m == 0:
                dealt(grd_r, 1)
                spread(grd_r, grd_p)
            conv(layer, m)
            if m == 0:
                if layer + 1 <= last:
                    g2(layer + 1)
            else:
                if layer + 2 <= last:
                    g1(layer + 2)
                if layer + 3 <= last:
                    g0(layer + 3)
                if layer == 2:
                    deal(grd_s, grd_r, 1)

    ar_mid(last * MB + 1)
    g_last = glp[0:1, :]
    b_last = slp[0:1, :]
    ct = 64
    for m in range(MB):
        tot = ar_get(last * MB + m, 1)
        mean = tot[0] / cnt[m]
        var = tot[1] / cnt[m] - mean * mean
        inv = lax.rsqrt(var + EPS)
        v1 = tot[2]
        v2 = inv * (tot[3] - mean * v1)
        if m == 0:
            o_gl[...] = v2[:, 0:mels]
            o_sl[...] = v1[:, 0:mels]
        else:
            o_gl[...] = o_gl[...] + v2[:, 0:mels]
            o_sl[...] = o_sl[...] + v1[:, 0:mels]
        a = g_last * inv
        c1 = a * v1 / cnt[m]
        c2 = a * v2 / cnt[m]

        @pl.loop(0, T // ct)
        def _(i):
            base = pl.multiple_of(i * ct, ct)
            rows = pl.ds(base, ct)
            mk = mask[m, rows, :]
            xv = (zl[m, rows, :] - mean) * inv
            mel_p[m, rows, :] = mel_p[m, rows, :] + mk * (g_last * xv + b_last)
            v = a * grd_p[m, rows, :] - c1 - c2 * xv
            gzl[m, pl.ds(base + HALO, ct), :] = (mk * v).astype(bf16)

        halo(gzl.at[m])
        grad_h(last, m)
    wgrad(last)
    collect(mel_p, bak_s)
    ar_mid(bround(middle, 1))
    deal(bak_s, bak_r, 2)
    for layer in range(middle, 1, -1):
        for m in range(MB):
            grad_z(layer, m)
            grad_h(layer, m)
            if m == 0:
                ra(layer + 1)
        mid = (ar_mid, bround(layer - 1, 1))
        if layer + 1 == last:
            rb(layer + 1)
            wgrad(layer, 3, (mid, (rc, layer + 1)))
            rd_(layer + 1)
        else:
            wgrad(layer, 3, (mid, (rb, layer + 1)))
    for m in range(MB):
        grad_z(1, m)
    wgrad(1, 2, ((rc, 3), (ra, 2)) if middle > 2 else ())
    grad_h(1, 0)
    rb(2)
    rd_(3)
    grad_h(1, 1)
    ra(1)
    dealt(bak_r, 2)
    restore(bak_r, o_mel)
    ar_mid(bround(0, 1))
    rc(2)
    for m in range(MB):
        grad_z(0, m)
    wgrad(0)
    for m in range(MB):

        @pl.loop(0, T // MT)
        def _(t):
            base = pl.multiple_of(t * MT, MT)
            acc = None
            for k in range(taps):
                rows = pl.ds(base + SUB * (taps - 1 - k), MT)
                part = nn(gz[m, rows, :], WF[k].reshape(chans, LANES))
                acc = part if acc is None else acc + part
            rows = pl.ds(base, MT)
            grd_p[m, rows, :] = grd_p[m, rows, :] + mask[m, rows, :] * acc

    rb(1)
    collect(grd_p, bak2_s)
    deal(bak2_s, bak2_r, 3)
    ra(0)
    rd_(2)
    rc(1)
    rb(0)
    rc(0)
    dealt(bak2_r, 3)
    restore(bak2_r, o_grad)
    rd_(1)
    rd_(0)
    for layer in reversed(range(last + 1)):
        rdrain(layer)
    wait(mel_r.at[pl.ds(0, n_dp - 1)], a2a_s.at[0])
    wait(grd_r.at[pl.ds(0, n_dp - 1)], a2a_s.at[1])
    wait(bak_r.at[pl.ds(0, n_dp - 1)], a2a_s.at[2])
    wait(bak2_r.at[pl.ds(0, n_dp - 1)], a2a_s.at[3])

    @pl.loop(0, len(straight))
    def _(r):
        wait(dr_r.at[r, pl.ds(0, total - 1)], drs_sem.at[r])

    @pl.loop(0, len(stepped))
    def _(r):
        wait(pl_r.at[r, pl.ds(0, group - 1)], pls_sem.at[r])
        wait(z_r.at[r, pl.ds(0, nz - 1)], zs_sem.at[r])


def local_kernel(
    mel, grad_post, lengths, regroup, w_first, w_mid, w_last, gains, shifts, gain_last, shift_last
):
    n_dp = lax.axis_size("dp")
    nz = n_dp // PLANE
    utts, frames, mels = mel.shape
    middle, taps, shard, chans = w_mid.shape
    depth = middle + 2
    T = n_dp * frames
    TH = T + 4 * SUB
    rows = shard // CORES
    direct = (depth + 2) * MB
    rounds = (depth - 3) * MB
    V = pltpu.VMEM
    D = pltpu.SemaphoreType.DMA
    S = jax.ShapeDtypeStruct
    out_shape = (
        S(mel.shape, bf16),
        S(mel.shape, bf16),
        S((taps, CORES, rows, mels), f32),
        S((middle, taps, CORES, rows, chans), f32),
        S((taps, CORES, rows, mels), f32),
        S(gains.shape, f32),
        S(gains.shape, f32),
        S((1, mels), f32),
        S((1, mels), f32),
    )
    packed = V((n_dp, frames + SUB, LANES), bf16)
    landing = [
        [
            V((taps, nz, PLANE, rows, d), bf16),
            V((2, taps, nz, rows, d), bf16),
            V((taps, nz, rows, d), bf16),
            V((nz - 1, taps, rows, d), bf16),
            V((taps, rows, d), f32),
            V((taps, rows, d), f32),
        ]
        for d in [LANES] + [chans] * middle + [LANES]
    ]
    scratch = [
        packed, packed, packed, packed, packed, packed, packed, packed,
        V((utts, frames, LANES), bf16), V((MB, frames, LANES), f32), V((MB, frames, LANES), f32),
        V((MB, T, LANES), f32), V((MB, T, LANES), f32), V((MB, T, LANES), f32),
        V((MB, TH, LANES), bf16), V((middle + 1, MB, TH, chans), bf16),
        V((middle + 1, MB, T, chans), bf16),
        V((MB, T, chans), f32), V((MB, T, LANES), f32),
        V((MB, TH, chans), bf16), V((MB, TH, LANES), bf16),
        V((middle, taps, nz, PLANE, CORES, rows, chans), bf16),
        V((taps, nz, PLANE, CORES, rows, LANES), bf16),
        V((taps, nz, PLANE, CORES, rows, LANES), bf16),
        V((taps, nz, PLANE, CORES, rows, LANES), bf16),
        V((taps, nz, PLANE, CORES, rows, chans), bf16),
        landing,
        V((direct, 8, LANES), f32), V((direct, n_dp * CORES, 8, LANES), f32),
        V((rounds, 8, LANES), f32), V((rounds, PLANE * CORES, 8, LANES), f32),
        V((rounds, 8, LANES), f32), V((rounds, nz, 8, LANES), f32), V((8, LANES), f32),
        V((8, chans), f32), V((8, chans), f32), V((8, LANES), f32), V((8, LANES), f32), V((depth * MB, 8, chans), f32),
        V((8, LANES), f32), V((8, LANES), f32), pltpu.SMEM((utts,), jnp.int32),
        D((direct,)), D((direct,)),
        D((rounds,)), D((rounds,)), D((rounds,)), D((rounds,)), D((4,)), D((4,)),
    ] + [D((depth + 1,))] * 18
    body = functools.partial(kernel, n_dp, utts, frames, chans, mels, taps, middle)
    vmem = pl.BlockSpec(memory_space=pltpu.VMEM)
    smem = pl.BlockSpec(memory_space=pltpu.SMEM)
    out = pl.pallas_call(
        body,
        out_shape=out_shape,
        in_specs=[smem, smem] + [vmem] * 9,
        out_specs=(vmem,) * 9,
        scratch_shapes=scratch,
        compiler_params=pltpu.CompilerParams(
            collective_id=0, has_side_effects=True, vmem_limit_bytes=64 * 2**20
        ),
        name="postnet_step",
    )(
        lengths, regroup, mel, grad_post,
        w_first.reshape(taps, CORES, rows, mels),
        w_mid.reshape(middle, taps, CORES, rows, chans),
        w_last.reshape(taps, CORES, rows, mels),
        gains, shifts, gain_last[None, :], shift_last[None, :],
    )
    return (
        out[0], out[1],
        out[2].reshape(w_first.shape), out[3].reshape(w_mid.shape), out[4].reshape(w_last.shape),
        out[5], out[6], out[7][0], out[8][0],
    )


def shortened(value):

    def short(part):
        return part.astype(jnp.bfloat16) if part.dtype == jnp.float32 else part

    return jax.tree.map(short, value)


def shifted(hidden, offset):
    if offset == 0:
        return hidden
    frames = hidden.shape[1]
    reach = abs(offset)
    padded = jnp.pad(hidden, ((0, 0), (reach, reach), (0, 0)))
    return padded[:, reach + offset : reach + offset + frames]


def conv_forward(hidden, weight):
    centre = weight.shape[0] // 2
    running = jnp.einsum(
        "blc,cd->bld", shifted(hidden, -centre), weight[0], preferred_element_type=jnp.float32
    )
    for tap_index in range(1, weight.shape[0]):
        running = running + jnp.einsum(
            "blc,cd->bld",
            shifted(hidden, tap_index - centre),
            weight[tap_index],
            preferred_element_type=jnp.float32,
        )
    return running


def conv_backward(hidden, grad_values, weight):
    centre = weight.shape[0] // 2
    weight_grad = jnp.stack(
        [
            jnp.einsum(
                "blc,bld->cd",
                shifted(hidden, tap_index - centre),
                grad_values,
                preferred_element_type=jnp.float32,
            )
            for tap_index in range(weight.shape[0])
        ]
    )
    hidden_grad = jnp.einsum(
        "bld,cd->blc", shifted(grad_values, centre), weight[0], preferred_element_type=jnp.float32
    )
    for tap_index in range(1, weight.shape[0]):
        hidden_grad = hidden_grad + jnp.einsum(
            "bld,cd->blc",
            shifted(grad_values, centre - tap_index),
            weight[tap_index],
            preferred_element_type=jnp.float32,
        )
    return (weight_grad, hidden_grad)


def normalize(values, frame_mask, frame_count):
    first_sum, second_sum = lax.psum(
        (
            jnp.sum(values * frame_mask, axis=(0, 1)),
            jnp.sum(values * values * frame_mask, axis=(0, 1)),
        ),
        ("dp", "rep"),
    )
    centre = first_sum / frame_count
    spread = second_sum / frame_count - centre * centre
    scale_inv = lax.rsqrt(spread + 1e-05)
    return ((values - centre) * scale_inv, scale_inv)


def norm_backward(grad_out, normed, scale_inv, gain, frame_mask, frame_count):
    shift_grad, gain_grad = lax.psum(
        (jnp.sum(grad_out, axis=(0, 1)), jnp.sum(grad_out * normed, axis=(0, 1))), ("dp", "rep")
    )
    grad_values = (
        gain * scale_inv * (grad_out - shift_grad / frame_count - normed * gain_grad / frame_count)
    )
    return (frame_mask * grad_values, gain_grad, shift_grad)


def layer_list(fetched):
    middle = fetched[1].shape[0]
    return (
        [jnp.swapaxes(fetched[0], 1, 2)]
        + [fetched[1][layer] for layer in range(middle)]
        + [fetched[2]]
    )


def local(
    mel, grad_post, lengths, regroup, w_first, w_mid, w_last, gains, shifts, gain_last, shift_last
):
    devices_dp = lax.axis_size("dp")
    replicas = lax.axis_size("rep")
    dp_index = lax.axis_index("dp")
    rep_index = lax.axis_index("rep")
    group_size = regroup.shape[1]
    utt_dev = group_size // devices_dp
    utt_micro = utt_dev // MB
    frames_all = mel.shape[1] * devices_dp
    middle = w_mid.shape[0]
    offsets = (jnp.arange(replicas, dtype=jnp.int32) * group_size)[:, None]
    lens_order = lengths[(regroup + offsets).reshape(-1)].reshape(
        replicas, devices_dp, MB, utt_micro
    )
    counts = jnp.sum(lens_order, axis=(0, 1, 3)).astype(jnp.float32)
    own_lens = lax.dynamic_index_in_dim(
        lax.dynamic_index_in_dim(lens_order, rep_index, 0, False), dp_index, 0, False
    )
    frame_ids = jnp.arange(frames_all, dtype=jnp.int32)
    masks = (frame_ids[None, None, :] < own_lens[:, :, None]).astype(jnp.float32)[..., None]
    local_order = lax.dynamic_index_in_dim(regroup, rep_index, 0, False)
    moved_mel, moved_grad = (
        lax.all_to_all(mel[local_order], "dp", split_axis=0, concat_axis=1, tiled=True),
        lax.all_to_all(grad_post[local_order], "dp", split_axis=0, concat_axis=1, tiled=True),
    )
    gain_list = [gains[layer] for layer in range(middle + 1)] + [gain_last]
    shift_list = [shifts[layer] for layer in range(middle + 1)] + [shift_last]
    depth = middle + 2
    gain_grads = [jnp.zeros_like(entry) for entry in gain_list]
    shift_grads = [jnp.zeros_like(entry) for entry in shift_list]
    owned = (
        jnp.zeros(w_first.shape, jnp.float32),
        jnp.zeros(w_mid.shape, jnp.float32),
        jnp.zeros(w_last.shape, jnp.float32),
    )
    refined = []
    input_grads = []
    for micro_index in range(MB):
        mel_block = moved_mel[micro_index * utt_micro : (micro_index + 1) * utt_micro]
        grad_block = moved_grad[micro_index * utt_micro : (micro_index + 1) * utt_micro].astype(
            jnp.float32
        )
        frame_mask = masks[micro_index]
        frame_count = counts[micro_index]
        fetched = (
            lax.all_gather(w_first, "dp", axis=1, tiled=True),
            lax.all_gather(w_mid, "dp", axis=2, tiled=True),
            lax.all_gather(w_last, "dp", axis=1, tiled=True),
        )
        weights = layer_list(fetched)
        hidden = (mel_block.astype(jnp.float32) * frame_mask).astype(jnp.bfloat16)
        inputs = []
        kept = []
        for layer in range(depth):
            inputs.append(hidden)
            normed, scale_inv = normalize(
                conv_forward(hidden, weights[layer]), frame_mask, frame_count
            )
            kept.append((normed, scale_inv))
            activated = gain_list[layer] * normed + shift_list[layer]
            if layer < depth - 1:
                hidden = (frame_mask * jnp.tanh(activated)).astype(jnp.bfloat16)
            else:
                refined.append(
                    (mel_block.astype(jnp.float32) + frame_mask * activated).astype(jnp.bfloat16)
                )
        fetched = (
            lax.all_gather(w_first, "dp", axis=1, tiled=True),
            lax.all_gather(w_mid, "dp", axis=2, tiled=True),
            lax.all_gather(w_last, "dp", axis=1, tiled=True),
        )
        weights = layer_list(fetched)
        grad_out = frame_mask * grad_block
        weight_grads = [None] * depth
        for layer in reversed(range(depth)):
            normed, scale_inv = kept[layer]
            grad_values, gain_grad, shift_grad = norm_backward(
                grad_out, normed, scale_inv, gain_list[layer], frame_mask, frame_count
            )
            gain_grads[layer] = gain_grads[layer] + gain_grad
            shift_grads[layer] = shift_grads[layer] + shift_grad
            weight_grad, hidden_grad = conv_backward(
                inputs[layer], grad_values.astype(jnp.bfloat16), weights[layer]
            )
            weight_grads[layer] = weight_grad
            if layer > 0:
                before = kept[layer - 1]
                activated = jnp.tanh(gain_list[layer - 1] * before[0] + shift_list[layer - 1])
                grad_out = frame_mask * hidden_grad * (1.0 - activated * activated)
            else:
                input_grads.append((grad_block + frame_mask * hidden_grad).astype(jnp.bfloat16))
        local_grads = (
            jnp.swapaxes(weight_grads[0], 1, 2),
            jnp.stack(weight_grads[1 : depth - 1]),
            weight_grads[depth - 1],
        )
        pieces = (
            lax.psum_scatter(local_grads[0], "dp", scatter_dimension=1, tiled=True),
            lax.psum_scatter(local_grads[1], "dp", scatter_dimension=2, tiled=True),
            lax.psum_scatter(local_grads[2], "dp", scatter_dimension=1, tiled=True),
        )
        owned = tuple((total + piece for total, piece in zip(owned, pieces)))
    final_first, final_mid, final_last = jax.tree.map(
        lambda part: part.astype(jnp.float32), lax.psum(shortened(owned), "rep")
    )
    back_mel, back_grad = (
        lax.all_to_all(
            jnp.concatenate(refined, axis=0), "dp", split_axis=1, concat_axis=0, tiled=True
        ),
        lax.all_to_all(
            jnp.concatenate(input_grads, axis=0), "dp", split_axis=1, concat_axis=0, tiled=True
        ),
    )
    inverse = (
        jnp.zeros((group_size,), jnp.int32)
        .at[local_order]
        .set(jnp.arange(group_size, dtype=jnp.int32))
    )
    return (
        back_mel[inverse],
        back_grad[inverse],
        final_first,
        final_mid,
        final_last,
        jnp.stack(gain_grads[: depth - 1]),
        jnp.stack(shift_grads[: depth - 1]),
        gain_grads[depth - 1],
        shift_grads[depth - 1],
    )


def solution(mesh):
    in_specs = (
        P("rep", "dp", None),
        P("rep", "dp", None),
        P(),
        P(),
        P(None, "dp", None),
        P(None, None, "dp", None),
        P(None, "dp", None),
        P(),
        P(),
        P(),
        P(),
    )
    out_specs = (
        P("rep", "dp", None),
        P("rep", "dp", None),
        P(None, "dp", None),
        P(None, None, "dp", None),
        P(None, "dp", None),
        P(),
        P(),
        P(),
        P(),
    )
    step = local_kernel if mesh.shape["dp"] == SUB and mesh.shape["rep"] == CORES else local
    return jax.shard_map(step, mesh=mesh, in_specs=in_specs, out_specs=out_specs, check_vma=False)
```

```python
import functools

import jax
import jax.numpy as jnp
from jax import lax
from jax.experimental import pallas as pl
from jax.experimental.pallas import tpu as pltpu
from jax.sharding import PartitionSpec as P

MB = 2
PLANE = 4
CORES = 2
SUB = 16
LANES = 128
MESH = pl.DeviceIdType.MESH
bf16 = jnp.bfloat16
f32 = jnp.float32
EPS = 1e-05


def nn(a, b):
    return jnp.dot(a, b, preferred_element_type=f32)


def nt(a, b):
    return lax.dot_general(a, b, (((1,), (1,)), ((), ())), preferred_element_type=f32)


def tn(a, b):
    return lax.dot_general(a, b, (((0,), (0,)), ((), ())), preferred_element_type=f32)


def kernel(
    n_dp, utts, frames, chans, mels, taps, middle,
    len_s, reg_s, mel, gpost, wf, wm, wl, gains, shifts, gl, sl,
    o_mel, o_grad, o_wf, o_wm, o_wl, o_gains, o_shifts, o_gl, o_sl,
    mel_s, grd_s, bak_s, bak2_s, mel_r, grd_r, bak_r, bak2_r,
    whole, pad_m, pad_g, mel_p, grd_p, mask, h0, h, xh, z, zl, gz, gzl,
    W, WF, WL, GF, G1, rbufs,
    dr_s, dr_r, pl_s, pl_r, z_s, z_r, ar_t, a1, a2, a3, a4, invs, glp, slp, lens,
    drs_sem, drr_sem, pls_sem, plr_sem, zs_sem, zr_sem, a2a_s, a2a_r, gz_s, gz_r, gp_s, gp_r, gq_s, gq_r, gb_s, gb_r,
    r0_s, r0_r, r1_s, r1_r, r2_s, r2_r, r3_s, r3_r, ro_s, ro_r,
):
    nz = n_dp // PLANE
    total = n_dp * CORES
    T = n_dp * frames
    HALO = 2 * SUB
    MT = T // 2
    CL = chans // LANES
    ctile = 64
    dp = lax.axis_index("dp")
    rep = lax.axis_index("rep")
    zc = lax.div(dp, PLANE)
    s = lax.rem(dp, PLANE)
    sx = s + 1 - 2 * lax.rem(s, 2)
    sy = s + 2 - 4 * lax.div(s, 2)
    s1 = sx + rep * (sy - sx)
    s2 = sy + rep * (sx - sy)
    sd = 3 - s
    lin = dp * CORES + rep
    group = PLANE * CORES
    mine = s * CORES + rep
    other = 1 - rep
    sib = (dp, other)
    peer1 = (zc * PLANE + s1, rep)
    peer2 = (zc * PLANE + s2, rep)

    def send(src, dst, ss, rs, to):
        pltpu.make_async_remote_copy(
            src_ref=src, dst_ref=dst, send_sem=ss, recv_sem=rs, device_id=to, device_id_type=MESH
        ).start()

    def wait(ref, sem):
        pltpu.make_async_copy(ref, ref, sem).wait()

    W[:, :, zc, s] = wm[...]
    WF[:, zc, s] = jnp.zeros((taps, CORES) + WF.shape[4:], bf16)
    WL[:, zc, s] = jnp.zeros((taps, CORES) + WL.shape[4:], bf16)
    WF[:, zc, s, :, :, 0:mels] = wf[...]
    WL[:, zc, s, :, :, 0:mels] = wl[...]

    barrier = pltpu.get_barrier_semaphore()
    for i in range(1, total):
        to = lax.rem(lin + i, total)
        pl.semaphore_signal(
            barrier, inc=1, device_id=(lax.div(to, CORES), lax.rem(to, CORES)), device_id_type=MESH
        )

    lane = lax.broadcasted_iota(jnp.int32, (frames, LANES), 1)
    lane_b = lax.broadcasted_iota(jnp.int32, (SUB, LANES), 1)
    half = LANES // 2
    tail = mels - half
    parts = frames // SUB

    def pack(dst, j, vs):
        low = jnp.where(lane < half, vs[0], pltpu.roll(vs[1], half, 1))
        rest = jnp.zeros((SUB, LANES), f32)
        for m in range(MB):
            for r in range(parts):
                at = (m * parts + r) * tail
                piece = vs[m][r * SUB : (r + 1) * SUB, :]
                moved = pltpu.roll(piece, (at - half) % LANES, 1) if at != half else piece
                rest = jnp.where((lane_b >= at) & (lane_b < at + tail), moved, rest)
        dst[j, 0:frames, :] = low.astype(bf16)
        dst[j, frames : frames + SUB, :] = rest.astype(bf16)

    def unpack(src, j):
        low = src[j, 0:frames, :].astype(f32)
        rest = src[j, frames : frames + SUB, :].astype(f32)
        vs = []
        for m in range(MB):
            pieces = []
            for r in range(parts):
                shift = (half - (m * parts + r) * tail) % LANES
                pieces.append(pltpu.roll(rest, shift, 1) if shift else rest)
            high = jnp.where(lane < mels, jnp.concatenate(pieces, axis=0), 0.0)
            vs.append(jnp.where(lane < half, pltpu.roll(low, half, 1) if m else low, high))
        return vs

    pad_m[...] = jnp.zeros(pad_m.shape, f32)
    pad_g[...] = jnp.zeros(pad_g.shape, f32)

    def pack_pair(src, pad, dst):
        @pl.loop(0, n_dp)
        def _(j):
            for m in range(MB):
                pad[m, :, 0:mels] = src[reg_s[rep, j * MB + m]].astype(f32)
            pack(dst, j, [pad[m] for m in range(MB)])

    pl.semaphore_wait(barrier, total - 1)

    def chunk(c):
        if c == 0:
            return WF
        if c == middle + 1:
            return WL
        return W.at[c - 1]

    units = []
    for layer in range(middle + 2):
        cuts = (0, 2, taps) if layer == 1 else (0, taps)
        units += [(layer, k0, k1) for k0, k1 in zip(cuts[:-1], cuts[1:])]

    def parts_of(c):
        return [
            (u, chunk(c).at[pl.ds(k0, k1 - k0)])
            for u, (layer, k0, k1) in enumerate(units)
            if layer == c
        ]

    def three(w):
        return w.at[:, pl.ds(0, nz - 1), 0, 0]

    def g0u(u, w):
        for i in range(1, nz):
            to = lax.rem(zc + i, nz) * PLANE + s
            piece = w.at[:, zc, s, rep]
            send(piece, piece, gz_s.at[u], gz_r.at[u], (to, rep))

    def g1u(u, w):
        wait(three(w), gz_r.at[u])
        col = w.at[:, :, s, rep]
        send(col, col, gp_s.at[u], gp_r.at[u], peer1)
        send(col, col, gq_s.at[u], gq_r.at[u], peer2)
        send(col, col, gb_s.at[u], gb_r.at[u], sib)

    def g2u(u, w):
        wait(w.at[:, :, 0, 0], gp_r.at[u])
        col = w.at[:, :, s1, rep]
        send(col, col, gq_s.at[u], gq_r.at[u], peer2)
        send(col, col, gb_s.at[u], gb_r.at[u], sib)

    def g3u(u, w):
        wait(w.at[:, :, pl.ds(0, 2), 0], gq_r.at[u])
        for q in (s2, sd):
            col = w.at[:, :, q, rep]
            send(col, col, gb_s.at[u], gb_r.at[u], sib)

    def g4u(u, w):
        wait(w.at[:, :, :, 0], gb_r.at[u])

    def gdrainu(u, w):
        wait(three(w), gz_s.at[u])
        wait(w.at[:, :, 0, 0], gp_s.at[u])
        wait(w.at[:, :, pl.ds(0, 2), 0], gq_s.at[u])
        wait(w.at[:, :, :, 0], gb_s.at[u])

    def each(fn):
        def run(c, only=None):
            for i, (u, w) in enumerate(parts_of(c)):
                if only is None or i == only:
                    fn(u, w)

        return run

    g0, g1, g2, g3, g4, gdrain = [each(f) for f in (g0u, g1u, g2u, g3u, g4u, gdrainu)]

    def deal(src, dst, which):
        for i in range(1, n_dp):
            to = lax.rem(dp + i, n_dp)
            send(src.at[to], dst.at[dp], a2a_s.at[which], a2a_r.at[which], (to, rep))
        dst[dp] = src[dp]

    def dealt(dst, which):
        wait(dst.at[pl.ds(0, n_dp - 1)], a2a_r.at[which])

    def spread(src, dst):
        for j in range(n_dp):
            for m, v in enumerate(unpack(src, j)):
                dst.at[m][pl.ds(j, frames, stride=SUB), :] = v

    def collect(src, dst):
        for j in range(n_dp):
            pack(dst, j, [src.at[m][pl.ds(j, frames, stride=SUB), :] for m in range(MB)])

    def restore(src, out):
        for j in range(n_dp):
            for m, v in enumerate(unpack(src, j)):
                whole[j * MB + m] = v.astype(bf16)

        @pl.loop(0, utts)
        def _(u):
            out[u] = whole[lens[u], :, 0:mels]

    all_rounds = (2 * (middle + 2) - 1) * MB
    exposed = [(middle + 2) * MB + m for m in range(MB)]
    exposed += [(middle + 2 + middle) * MB + m for m in range(MB)]
    straight = list(range((middle + 2) * MB)) + exposed
    stepped = [r for r in range(all_rounds) if r not in straight]

    def ar_go(rd, vs):
        n = 8 // len(vs)
        plain = rd in straight
        rd = straight.index(rd) if plain else stepped.index(rd)
        if plain:
            src, dst, slot = dr_s.at[rd], dr_r.at[rd], lin
        else:
            src, dst, slot = pl_s.at[rd], pl_r.at[rd], mine
        for e, v in enumerate(vs):
            for i in range(n):
                if (i + 1) * LANES <= v.shape[1]:
                    row = v[:, i * LANES : (i + 1) * LANES]
                else:
                    row = jnp.zeros((1, LANES), f32)
                at = e * n + i
                src[at : at + 1, :] = row
                dst[slot, at : at + 1, :] = row
        if plain:
            for i in range(1, total):
                to = lax.rem(lin + i, total)
                send(
                    src, dst.at[lin], drs_sem.at[rd], drr_sem.at[rd],
                    (lax.div(to, CORES), lax.rem(to, CORES)),
                )
            return
        for i in range(1, group):
            to = lax.rem(mine + i, group)
            send(
                src, dst.at[mine], pls_sem.at[rd], plr_sem.at[rd],
                (zc * PLANE + lax.div(to, CORES), lax.rem(to, CORES)),
            )

    def ar_mid(rd):
        if rd in straight:
            return
        rd = stepped.index(rd)
        wait(pl_r.at[rd, pl.ds(0, group - 1)], plr_sem.at[rd])
        acc = pl_r[rd, 0]
        for i in range(1, group):
            acc = acc + pl_r[rd, i]
        z_s[rd] = acc
        z_r[rd, zc] = acc
        for i in range(1, nz):
            to = lax.rem(zc + i, nz) * PLANE + s
            send(z_s.at[rd], z_r.at[rd, zc], zs_sem.at[rd], zr_sem.at[rd], (to, rep))

    def ar_get(rd, n):
        if rd in straight:
            rd = straight.index(rd)
            wait(dr_r.at[rd, pl.ds(0, total - 1)], drr_sem.at[rd])
            acc = dr_r[rd, 0]
            for i in range(1, total):
                acc = acc + dr_r[rd, i]
        else:
            rd = stepped.index(rd)
            wait(z_r.at[rd, pl.ds(0, nz - 1)], zr_sem.at[rd])
            acc = z_r[rd, 0]
            for i in range(1, nz):
                acc = acc + z_r[rd, i]
        ar_t[...] = acc
        q = CL if n == CL else 2
        return [
            jnp.concatenate([ar_t[e * q + i : e * q + i + 1, :] for i in range(n)], axis=1)
            for e in range(8 // q)
        ]

    def fold(v):
        return jnp.sum(v.reshape(v.shape[0] // 8, 8, v.shape[1]), axis=0)

    def wide(mk, d):
        return jnp.concatenate([mk] * (d // LANES), axis=1) if d > LANES else mk

    def clear(d):
        a1[:, 0:d] = jnp.zeros((8, d), f32)
        a2[:, 0:d] = jnp.zeros((8, d), f32)
        if d == LANES:
            a3[...] = jnp.zeros((8, d), f32)
            a4[...] = jnp.zeros((8, d), f32)

    def ar_acc(rd, d, before=None):
        if before is not None:
            ar_mid(before)
        accs = (a1, a2, a3, a4) if d == LANES else (a1, a2)
        ar_go(rd, [jnp.sum(v[:, 0:d], axis=0, keepdims=True) for v in accs])

    def halo(ref):
        d = ref.shape[1]
        row = lax.rem(lax.broadcasted_iota(jnp.int32, (HALO, d), 0), SUB)
        low = pltpu.roll(ref[T : T + HALO, :].astype(f32), 1, 0)
        ref[0:HALO, :] = jnp.where(row == 0, 0.0, low).astype(bf16)
        high = pltpu.roll(ref[HALO : 2 * HALO, :].astype(f32), HALO - 1, 0)
        ref[T + HALO : T + 2 * HALO, :] = jnp.where(row == SUB - 1, 0.0, high).astype(bf16)

    cnt = []
    own = []
    for m in range(MB):

        def body(j, c, m=m):
            for r in range(CORES):
                c = c + len_s[r * utts + reg_s[r, j * MB + m]]
            return c

        cnt.append(lax.fori_loop(0, n_dp, body, jnp.int32(0)).astype(f32))
        own.append(len_s[rep * utts + reg_s[rep, dp * MB + m]])

    last = middle + 1

    def mean_inv(rd, m, n):
        v1, v2 = ar_get(rd, n)
        mean = v1 / cnt[m]
        var = v2 / cnt[m] - mean * mean
        inv = lax.rsqrt(var + EPS)
        invs[rd, 0:1, 0 : n * LANES] = inv
        return mean, inv

    pairs = [tuple(range(k, min(k + 2, taps))) for k in range(0, taps, 2)]

    def joined(vs):
        return jnp.concatenate(vs, axis=1) if len(vs) > 1 else vs[0]

    def conv(layer, m):
        rd = layer * MB + m
        d = LANES if layer == last else chans
        dst = zl if layer == last else z
        clear(d)

        @pl.loop(0, T // MT)
        def _(t):
            base = pl.multiple_of(t * MT, MT)
            acc = None
            if layer == 0:
                for ks in pairs:
                    prod = nt(
                        joined([h0[m, pl.ds(base + SUB * k, MT), :] for k in ks]),
                        joined([WF[k].reshape(chans, LANES) for k in ks]),
                    )
                    acc = prod if acc is None else acc + prod
            else:
                for k in range(taps):
                    rows = pl.ds(base + SUB * k, MT)
                    if layer == last:
                        prod = nn(h[layer - 1, m, rows, :], WL[k].reshape(chans, LANES))
                    else:
                        prod = nn(h[layer - 1, m, rows, :], W[layer - 1, k].reshape(chans, chans))
                    acc = prod if acc is None else acc + prod
            dst[m, pl.ds(base, MT), :] = acc
            zm = acc * wide(mask[m, pl.ds(base, MT), :], d)
            a1[:, 0:d] += fold(zm)
            a2[:, 0:d] += fold(zm * acc)
            if layer == last:
                gy = mask[m, pl.ds(base, MT), :] * grd_p[m, pl.ds(base, MT), :]
                a3[...] += fold(gy)
                a4[...] += fold(gy * acc)

        ar_acc(rd, d, rd - m if m else None)

    def norm(layer, m):
        mean, inv = mean_inv(layer * MB + m, m, CL)
        g = gains[layer : layer + 1, :]
        b = shifts[layer : layer + 1, :]

        @pl.loop(0, T // ctile)
        def _(i):
            base = pl.multiple_of(i * ctile, ctile)
            rows = pl.ds(base, ctile)
            xv = (z[m, rows, :] - mean) * inv
            hv = wide(mask[m, rows, :], chans) * jnp.tanh(g * xv + b)
            xh[layer, m, rows, :] = xv.astype(bf16)
            h[layer, m, pl.ds(base + HALO, ctile), :] = hv.astype(bf16)

        halo(h.at[layer, m])

    def grad_tail(layer, m, base, acc):
        g = gains[layer : layer + 1, :]
        b = shifts[layer : layer + 1, :]
        rows = pl.ds(base, MT)
        xv = xh[layer, m, rows, :].astype(f32)
        th = jnp.tanh(g * xv + b)
        gy = wide(mask[m, rows, :], chans) * acc * (1.0 - th * th)
        z[m, rows, :] = gy
        a1[...] += fold(gy)
        a2[...] += fold(gy * xv)

    def bround(layer, m):
        return (last + 1 + layer) * MB + m

    def coefs(layer, m, n, g, og, os):
        v1, v2 = ar_get(bround(layer, m), n)
        og(v2, m > 0)
        os(v1, m > 0)
        a = g * invs[layer * MB + m, 0:1, 0 : n * LANES]
        return a, a * v1 / cnt[m], a * v2 / cnt[m]

    def grad_z(layer, m):
        def og(v, add):
            o_gains[layer : layer + 1, :] = v + o_gains[layer : layer + 1, :] if add else v

        def os(v, add):
            o_shifts[layer : layer + 1, :] = v + o_shifts[layer : layer + 1, :] if add else v

        a, c1, c2 = coefs(layer, m, CL, gains[layer : layer + 1, :], og, os)

        @pl.loop(0, T // ctile)
        def _(i):
            base = pl.multiple_of(i * ctile, ctile)
            rows = pl.ds(base, ctile)
            v = a * z[m, rows, :] - c1 - c2 * xh[layer, m, rows, :].astype(f32)
            gz[m, pl.ds(base + HALO, ctile), :] = (wide(mask[m, rows, :], chans) * v).astype(bf16)

        halo(gz.at[m])

    def grad_h(layer, m):
        clear(chans)

        @pl.loop(0, T // MT)
        def _(t):
            base = pl.multiple_of(t * MT, MT)
            acc = None
            if layer == last:
                for ks in pairs:
                    prod = nt(
                        joined([gzl[m, pl.ds(base + SUB * (taps - 1 - k), MT), :] for k in ks]),
                        joined([WL[k].reshape(chans, LANES) for k in ks]),
                    )
                    acc = prod if acc is None else acc + prod
            else:
                for k in range(taps):
                    rows = pl.ds(base + SUB * (taps - 1 - k), MT)
                    prod = nt(gz[m, rows, :], W[layer - 1, k].reshape(chans, chans))
                    acc = prod if acc is None else acc + prod
            grad_tail(layer - 1, m, base, acc)

        ar_acc(bround(layer - 1, m), chans, bround(layer - 1, 0) if m else None)

    def gchunk(layer):
        return GF if layer == 0 else G1 if layer == 1 else chunk(layer)

    def wgrad(layer, split=0, between=()):
        gdrain(layer)
        w = gchunk(layer)

        def narrow(ks):
            acc = None
            for m in range(MB):
                if layer == 0:
                    right = joined([h0[m, pl.ds(SUB * k, T), :] for k in ks])
                    prod = tn(gz[m, HALO : HALO + T, :], right)
                else:
                    right = joined([gzl[m, pl.ds(SUB * (taps - 1 - k), T), :] for k in ks])
                    prod = tn(h[layer - 1, m, HALO : HALO + T, :], right)
                acc = prod if acc is None else acc + prod
            for i, k in enumerate(ks):
                v = acc[:, i * LANES : (i + 1) * LANES]
                w[k] = v.astype(bf16).reshape(w.shape[1:])

        def one(k):
            rows = pl.ds(pl.multiple_of(SUB * (taps - 1 - k), SUB), T)
            acc = tn(h[layer - 1, 0, HALO : HALO + T, :], gz[0, rows, :])
            for m in range(1, MB):
                acc = acc + tn(h[layer - 1, m, HALO : HALO + T, :], gz[m, rows, :])
            w[k] = acc.astype(bf16).reshape(w.shape[1:])

        if layer in (0, last):
            for ks in pairs:
                narrow(ks)
        else:
            if split:
                pl.loop(0, split)(one)
                for fn, arg in between:
                    fn(arg)
            pl.loop(split, taps)(one)
        send(w.at[:, :, :, other], rbuf(layer)[0], r0_s.at[layer], r0_r.at[layer], sib)

    def rbuf(layer):
        return rbufs[layer]

    def total_of(a, b):
        return (a.astype(f32) + b.astype(f32)).astype(bf16)

    def ra(layer):
        w = gchunk(layer)
        r0, r1 = rbuf(layer)[0:2]
        wait(r0, r0_r.at[layer])
        for k in range(taps):
            r0[k] = total_of(r0[k], w[k, :, :, rep])
        for slot, q in ((1, sd), (0, s2)):
            send(r0.at[:, :, q], r1.at[slot], r1_s.at[layer], r1_r.at[layer], peer2)

    def rb(layer):
        r0, r1, r2 = rbuf(layer)[0:3]
        wait(r1, r1_r.at[layer])
        for slot, q in ((1, s1), (0, s)):
            for k in range(taps):
                r1[slot, k] = total_of(r1[slot, k], r0[k, :, q])
        send(r1.at[1], r2, r2_s.at[layer], r2_r.at[layer], peer1)

    def rc(layer):
        r1, r2, r3 = rbuf(layer)[1:4]
        wait(r2, r2_r.at[layer])
        for k in range(taps):
            r2[k] = total_of(r2[k], r1[0, k])
        for i in range(1, nz):
            zt = lax.rem(zc + i, nz)
            send(
                r2.at[:, zt], r3.at[i - 1], r3_s.at[layer], r3_r.at[layer],
                (zt * PLANE + s, rep),
            )

    def outs(layer):
        return o_wf if layer == 0 else o_wl if layer == last else o_wm.at[layer - 1]

    def rd_(layer):
        r2, r3 = rbuf(layer)[2:4]
        fs, fr = rbuf(layer)[4:6]
        wait(r3, r3_r.at[layer])
        out = outs(layer)
        for k in range(taps):
            v = r2[k, zc].astype(f32)
            for i in range(nz - 1):
                v = v + r3[i, k].astype(f32)
            fs[k] = v
            out[k, rep] = v[:, 0 : out.shape[3]]
        send(fs, fr, ro_s.at[layer], ro_r.at[layer], sib)

    def rdrain(layer):
        r0, r1, r2, r3, fs, fr = rbuf(layer)
        out = outs(layer)
        wait(fr, ro_r.at[layer])
        for k in range(taps):
            out[k, other] = fr[k][:, 0 : out.shape[3]]
        wait(fs, ro_s.at[layer])
        wait(r0, r0_s.at[layer])
        wait(r1, r1_s.at[layer])
        wait(r2, r2_s.at[layer])
        wait(r3, r3_s.at[layer])

    g0(0)
    g0(1)
    pack_pair(mel, pad_m, mel_s)
    deal(mel_s, mel_r, 0)
    g0(2)
    glp[...] = jnp.zeros(glp.shape, f32)
    slp[...] = jnp.zeros(slp.shape, f32)
    glp[0:1, 0:mels] = gl[...]
    slp[0:1, 0:mels] = sl[...]
    for m in range(MB):

        @pl.loop(0, T // ctile)
        def _(i):
            base = pl.multiple_of(i * ctile, ctile)
            r = base + lax.broadcasted_iota(jnp.int32, (ctile, LANES), 0)
            t = lax.rem(r, SUB) * frames + lax.div(r, SUB)
            mask[m, pl.ds(base, ctile), :] = jnp.where(t < own[m], 1.0, 0.0)

    g1(0)
    g1(1, 0)
    g2(0)
    g1(1, 1)
    g3(0)
    g2(1, 0)

    @pl.loop(0, utts)
    def _(u):
        at = jnp.int32(0)
        for k in range(utts):
            at = jnp.where(reg_s[rep, k] == u, k, at)
        lens[u] = at

    pack_pair(gpost, pad_g, grd_s)
    dealt(mel_r, 0)
    spread(mel_r, mel_p)
    for m in range(MB):
        h0[m, HALO : HALO + T, :] = (mel_p[m] * mask[m]).astype(bf16)
        halo(h0.at[m])
        if m == 0:
            g4(0)
        if m == 0:
            g2(1, 1)
            g3(1, 0)
        conv(0, m)
    g1(2)
    g0(3)
    for layer in range(1, last + 1):
        ar_mid((layer - 1) * MB + 1)
        g3(layer, 1 if layer == 1 else None)
        g4(layer)
        for m in range(MB):
            norm(layer - 1, m)
            if layer == last and m == 0:
                dealt(grd_r, 1)
                spread(grd_r, grd_p)
            conv(layer, m)
            if m == 0:
                if layer + 1 <= last:
                    g2(layer + 1)
            else:
                if layer + 2 <= last:
                    g1(layer + 2)
                if layer + 3 <= last:
                    g0(layer + 3)
                if layer == 2:
                    deal(grd_s, grd_r, 1)

    ar_mid(last * MB + 1)
    g_last = glp[0:1, :]
    b_last = slp[0:1, :]
    ct = 64
    for m in range(MB):
        tot = ar_get(last * MB + m, 1)
        mean = tot[0] / cnt[m]
        var = tot[1] / cnt[m] - mean * mean
        inv = lax.rsqrt(var + EPS)
        v1 = tot[2]
        v2 = inv * (tot[3] - mean * v1)
        if m == 0:
            o_gl[...] = v2[:, 0:mels]
            o_sl[...] = v1[:, 0:mels]
        else:
            o_gl[...] = o_gl[...] + v2[:, 0:mels]
            o_sl[...] = o_sl[...] + v1[:, 0:mels]
        a = g_last * inv
        c1 = a * v1 / cnt[m]
        c2 = a * v2 / cnt[m]

        @pl.loop(0, T // ct)
        def _(i):
            base = pl.multiple_of(i * ct, ct)
            rows = pl.ds(base, ct)
            mk = mask[m, rows, :]
            xv = (zl[m, rows, :] - mean) * inv
            mel_p[m, rows, :] = mel_p[m, rows, :] + mk * (g_last * xv + b_last)
            v = a * grd_p[m, rows, :] - c1 - c2 * xv
            gzl[m, pl.ds(base + HALO, ct), :] = (mk * v).astype(bf16)

        halo(gzl.at[m])
        grad_h(last, m)
    wgrad(last)
    collect(mel_p, bak_s)
    ar_mid(bround(middle, 1))
    deal(bak_s, bak_r, 2)
    for layer in range(middle, 1, -1):
        for m in range(MB):
            grad_z(layer, m)
            grad_h(layer, m)
            if m == 0:
                ra(layer + 1)
        mid = (ar_mid, bround(layer - 1, 1))
        if layer + 1 == last:
            rb(layer + 1)
            wgrad(layer, 3, (mid, (rc, layer + 1)))
            rd_(layer + 1)
        else:
            wgrad(layer, 3, (mid, (rb, layer + 1)))
    for m in range(MB):
        grad_z(1, m)
    wgrad(1, 2, ((rc, 3), (ra, 2)) if middle > 2 else ())
    grad_h(1, 0)
    rb(2)
    rd_(3)
    grad_h(1, 1)
    ra(1)
    dealt(bak_r, 2)
    restore(bak_r, o_mel)
    ar_mid(bround(0, 1))
    rc(2)
    for m in range(MB):
        grad_z(0, m)
    wgrad(0)
    for m in range(MB):

        @pl.loop(0, T // MT)
        def _(t):
            base = pl.multiple_of(t * MT, MT)
            acc = None
            for k in range(taps):
                rows = pl.ds(base + SUB * (taps - 1 - k), MT)
                part = nn(gz[m, rows, :], WF[k].reshape(chans, LANES))
                acc = part if acc is None else acc + part
            rows = pl.ds(base, MT)
            grd_p[m, rows, :] = grd_p[m, rows, :] + mask[m, rows, :] * acc

    rb(1)
    collect(grd_p, bak2_s)
    deal(bak2_s, bak2_r, 3)
    ra(0)
    rd_(2)
    rc(1)
    rb(0)
    rc(0)
    dealt(bak2_r, 3)
    restore(bak2_r, o_grad)
    rd_(1)
    rd_(0)
    for layer in reversed(range(last + 1)):
        rdrain(layer)
    wait(mel_r.at[pl.ds(0, n_dp - 1)], a2a_s.at[0])
    wait(grd_r.at[pl.ds(0, n_dp - 1)], a2a_s.at[1])
    wait(bak_r.at[pl.ds(0, n_dp - 1)], a2a_s.at[2])
    wait(bak2_r.at[pl.ds(0, n_dp - 1)], a2a_s.at[3])

    @pl.loop(0, len(straight))
    def _(r):
        wait(dr_r.at[r, pl.ds(0, total - 1)], drs_sem.at[r])

    @pl.loop(0, len(stepped))
    def _(r):
        wait(pl_r.at[r, pl.ds(0, group - 1)], pls_sem.at[r])
        wait(z_r.at[r, pl.ds(0, nz - 1)], zs_sem.at[r])


def local_kernel(
    mel, grad_post, lengths, regroup, w_first, w_mid, w_last, gains, shifts, gain_last, shift_last
):
    n_dp = lax.axis_size("dp")
    nz = n_dp // PLANE
    utts, frames, mels = mel.shape
    middle, taps, shard, chans = w_mid.shape
    depth = middle + 2
    T = n_dp * frames
    TH = T + 4 * SUB
    rows = shard // CORES
    direct = (depth + 2) * MB
    rounds = (depth - 3) * MB
    V = pltpu.VMEM
    D = pltpu.SemaphoreType.DMA
    S = jax.ShapeDtypeStruct
    out_shape = (
        S(mel.shape, bf16),
        S(mel.shape, bf16),
        S((taps, CORES, rows, mels), f32),
        S((middle, taps, CORES, rows, chans), f32),
        S((taps, CORES, rows, mels), f32),
        S(gains.shape, f32),
        S(gains.shape, f32),
        S((1, mels), f32),
        S((1, mels), f32),
    )
    packed = V((n_dp, frames + SUB, LANES), bf16)
    landing = [
        [
            V((taps, nz, PLANE, rows, d), bf16),
            V((2, taps, nz, rows, d), bf16),
            V((taps, nz, rows, d), bf16),
            V((nz - 1, taps, rows, d), bf16),
            V((taps, rows, d), f32),
            V((taps, rows, d), f32),
        ]
        for d in [LANES] + [chans] * middle + [LANES]
    ]
    scratch = [
        packed, packed, packed, packed, packed, packed, packed, packed,
        V((utts, frames, LANES), bf16), V((MB, frames, LANES), f32), V((MB, frames, LANES), f32),
        V((MB, T, LANES), f32), V((MB, T, LANES), f32), V((MB, T, LANES), f32),
        V((MB, TH, LANES), bf16), V((middle + 1, MB, TH, chans), bf16),
        V((middle + 1, MB, T, chans), bf16),
        V((MB, T, chans), f32), V((MB, T, LANES), f32),
        V((MB, TH, chans), bf16), V((MB, TH, LANES), bf16),
        V((middle, taps, nz, PLANE, CORES, rows, chans), bf16),
        V((taps, nz, PLANE, CORES, rows, LANES), bf16),
        V((taps, nz, PLANE, CORES, rows, LANES), bf16),
        V((taps, nz, PLANE, CORES, rows, LANES), bf16),
        V((taps, nz, PLANE, CORES, rows, chans), bf16),
        landing,
        V((direct, 8, LANES), f32), V((direct, n_dp * CORES, 8, LANES), f32),
        V((rounds, 8, LANES), f32), V((rounds, PLANE * CORES, 8, LANES), f32),
        V((rounds, 8, LANES), f32), V((rounds, nz, 8, LANES), f32), V((8, LANES), f32),
        V((8, chans), f32), V((8, chans), f32), V((8, LANES), f32), V((8, LANES), f32), V((depth * MB, 8, chans), f32),
        V((8, LANES), f32), V((8, LANES), f32), pltpu.SMEM((utts,), jnp.int32),
        D((direct,)), D((direct,)),
        D((rounds,)), D((rounds,)), D((rounds,)), D((rounds,)), D((4,)), D((4,)),
    ] + [D((depth + 1,))] * 18
    body = functools.partial(kernel, n_dp, utts, frames, chans, mels, taps, middle)
    vmem = pl.BlockSpec(memory_space=pltpu.VMEM)
    smem = pl.BlockSpec(memory_space=pltpu.SMEM)
    out = pl.pallas_call(
        body,
        out_shape=out_shape,
        in_specs=[smem, smem] + [vmem] * 9,
        out_specs=(vmem,) * 9,
        scratch_shapes=scratch,
        compiler_params=pltpu.CompilerParams(
            collective_id=0, has_side_effects=True, vmem_limit_bytes=64 * 2**20
        ),
        name="postnet_step",
    )(
        lengths, regroup, mel, grad_post,
        w_first.reshape(taps, CORES, rows, mels),
        w_mid.reshape(middle, taps, CORES, rows, chans),
        w_last.reshape(taps, CORES, rows, mels),
        gains, shifts, gain_last[None, :], shift_last[None, :],
    )
    return (
        out[0], out[1],
        out[2].reshape(w_first.shape), out[3].reshape(w_mid.shape), out[4].reshape(w_last.shape),
        out[5], out[6], out[7][0], out[8][0],
    )


def shortened(value):

    def short(part):
        return part.astype(jnp.bfloat16) if part.dtype == jnp.float32 else part

    return jax.tree.map(short, value)


def shifted(hidden, offset):
    if offset == 0:
        return hidden
    frames = hidden.shape[1]
    reach = abs(offset)
    padded = jnp.pad(hidden, ((0, 0), (reach, reach), (0, 0)))
    return padded[:, reach + offset : reach + offset + frames]


def conv_forward(hidden, weight):
    centre = weight.shape[0] // 2
    running = jnp.einsum(
        "blc,cd->bld", shifted(hidden, -centre), weight[0], preferred_element_type=jnp.float32
    )
    for tap_index in range(1, weight.shape[0]):
        running = running + jnp.einsum(
            "blc,cd->bld",
            shifted(hidden, tap_index - centre),
            weight[tap_index],
            preferred_element_type=jnp.float32,
        )
    return running


def conv_backward(hidden, grad_values, weight):
    centre = weight.shape[0] // 2
    weight_grad = jnp.stack(
        [
            jnp.einsum(
                "blc,bld->cd",
                shifted(hidden, tap_index - centre),
                grad_values,
                preferred_element_type=jnp.float32,
            )
            for tap_index in range(weight.shape[0])
        ]
    )
    hidden_grad = jnp.einsum(
        "bld,cd->blc", shifted(grad_values, centre), weight[0], preferred_element_type=jnp.float32
    )
    for tap_index in range(1, weight.shape[0]):
        hidden_grad = hidden_grad + jnp.einsum(
            "bld,cd->blc",
            shifted(grad_values, centre - tap_index),
            weight[tap_index],
            preferred_element_type=jnp.float32,
        )
    return (weight_grad, hidden_grad)


def normalize(values, frame_mask, frame_count):
    first_sum, second_sum = lax.psum(
        (
            jnp.sum(values * frame_mask, axis=(0, 1)),
            jnp.sum(values * values * frame_mask, axis=(0, 1)),
        ),
        ("dp", "rep"),
    )
    centre = first_sum / frame_count
    spread = second_sum / frame_count - centre * centre
    scale_inv = lax.rsqrt(spread + 1e-05)
    return ((values - centre) * scale_inv, scale_inv)


def norm_backward(grad_out, normed, scale_inv, gain, frame_mask, frame_count):
    shift_grad, gain_grad = lax.psum(
        (jnp.sum(grad_out, axis=(0, 1)), jnp.sum(grad_out * normed, axis=(0, 1))), ("dp", "rep")
    )
    grad_values = (
        gain * scale_inv * (grad_out - shift_grad / frame_count - normed * gain_grad / frame_count)
    )
    return (frame_mask * grad_values, gain_grad, shift_grad)


def layer_list(fetched):
    middle = fetched[1].shape[0]
    return (
        [jnp.swapaxes(fetched[0], 1, 2)]
        + [fetched[1][layer] for layer in range(middle)]
        + [fetched[2]]
    )


def local(
    mel, grad_post, lengths, regroup, w_first, w_mid, w_last, gains, shifts, gain_last, shift_last
):
    devices_dp = lax.axis_size("dp")
    replicas = lax.axis_size("rep")
    dp_index = lax.axis_index("dp")
    rep_index = lax.axis_index("rep")
    group_size = regroup.shape[1]
    utt_dev = group_size // devices_dp
    utt_micro = utt_dev // MB
    frames_all = mel.shape[1] * devices_dp
    middle = w_mid.shape[0]
    offsets = (jnp.arange(replicas, dtype=jnp.int32) * group_size)[:, None]
    lens_order = lengths[(regroup + offsets).reshape(-1)].reshape(
        replicas, devices_dp, MB, utt_micro
    )
    counts = jnp.sum(lens_order, axis=(0, 1, 3)).astype(jnp.float32)
    own_lens = lax.dynamic_index_in_dim(
        lax.dynamic_index_in_dim(lens_order, rep_index, 0, False), dp_index, 0, False
    )
    frame_ids = jnp.arange(frames_all, dtype=jnp.int32)
    masks = (frame_ids[None, None, :] < own_lens[:, :, None]).astype(jnp.float32)[..., None]
    local_order = lax.dynamic_index_in_dim(regroup, rep_index, 0, False)
    moved_mel, moved_grad = (
        lax.all_to_all(mel[local_order], "dp", split_axis=0, concat_axis=1, tiled=True),
        lax.all_to_all(grad_post[local_order], "dp", split_axis=0, concat_axis=1, tiled=True),
    )
    gain_list = [gains[layer] for layer in range(middle + 1)] + [gain_last]
    shift_list = [shifts[layer] for layer in range(middle + 1)] + [shift_last]
    depth = middle + 2
    gain_grads = [jnp.zeros_like(entry) for entry in gain_list]
    shift_grads = [jnp.zeros_like(entry) for entry in shift_list]
    owned = (
        jnp.zeros(w_first.shape, jnp.float32),
        jnp.zeros(w_mid.shape, jnp.float32),
        jnp.zeros(w_last.shape, jnp.float32),
    )
    refined = []
    input_grads = []
    for micro_index in range(MB):
        mel_block = moved_mel[micro_index * utt_micro : (micro_index + 1) * utt_micro]
        grad_block = moved_grad[micro_index * utt_micro : (micro_index + 1) * utt_micro].astype(
            jnp.float32
        )
        frame_mask = masks[micro_index]
        frame_count = counts[micro_index]
        fetched = (
            lax.all_gather(w_first, "dp", axis=1, tiled=True),
            lax.all_gather(w_mid, "dp", axis=2, tiled=True),
            lax.all_gather(w_last, "dp", axis=1, tiled=True),
        )
        weights = layer_list(fetched)
        hidden = (mel_block.astype(jnp.float32) * frame_mask).astype(jnp.bfloat16)
        inputs = []
        kept = []
        for layer in range(depth):
            inputs.append(hidden)
            normed, scale_inv = normalize(
                conv_forward(hidden, weights[layer]), frame_mask, frame_count
            )
            kept.append((normed, scale_inv))
            activated = gain_list[layer] * normed + shift_list[layer]
            if layer < depth - 1:
                hidden = (frame_mask * jnp.tanh(activated)).astype(jnp.bfloat16)
            else:
                refined.append(
                    (mel_block.astype(jnp.float32) + frame_mask * activated).astype(jnp.bfloat16)
                )
        fetched = (
            lax.all_gather(w_first, "dp", axis=1, tiled=True),
            lax.all_gather(w_mid, "dp", axis=2, tiled=True),
            lax.all_gather(w_last, "dp", axis=1, tiled=True),
        )
        weights = layer_list(fetched)
        grad_out = frame_mask * grad_block
        weight_grads = [None] * depth
        for layer in reversed(range(depth)):
            normed, scale_inv = kept[layer]
            grad_values, gain_grad, shift_grad = norm_backward(
                grad_out, normed, scale_inv, gain_list[layer], frame_mask, frame_count
            )
            gain_grads[layer] = gain_grads[layer] + gain_grad
            shift_grads[layer] = shift_grads[layer] + shift_grad
            weight_grad, hidden_grad = conv_backward(
                inputs[layer], grad_values.astype(jnp.bfloat16), weights[layer]
            )
            weight_grads[layer] = weight_grad
            if layer > 0:
                before = kept[layer - 1]
                activated = jnp.tanh(gain_list[layer - 1] * before[0] + shift_list[layer - 1])
                grad_out = frame_mask * hidden_grad * (1.0 - activated * activated)
            else:
                input_grads.append((grad_block + frame_mask * hidden_grad).astype(jnp.bfloat16))
        local_grads = (
            jnp.swapaxes(weight_grads[0], 1, 2),
            jnp.stack(weight_grads[1 : depth - 1]),
            weight_grads[depth - 1],
        )
        pieces = (
            lax.psum_scatter(local_grads[0], "dp", scatter_dimension=1, tiled=True),
            lax.psum_scatter(local_grads[1], "dp", scatter_dimension=2, tiled=True),
            lax.psum_scatter(local_grads[2], "dp", scatter_dimension=1, tiled=True),
        )
        owned = tuple((total + piece for total, piece in zip(owned, pieces)))
    final_first, final_mid, final_last = jax.tree.map(
        lambda part: part.astype(jnp.float32), lax.psum(shortened(owned), "rep")
    )
    back_mel, back_grad = (
        lax.all_to_all(
            jnp.concatenate(refined, axis=0), "dp", split_axis=1, concat_axis=0, tiled=True
        ),
        lax.all_to_all(
            jnp.concatenate(input_grads, axis=0), "dp", split_axis=1, concat_axis=0, tiled=True
        ),
    )
    inverse = (
        jnp.zeros((group_size,), jnp.int32)
        .at[local_order]
        .set(jnp.arange(group_size, dtype=jnp.int32))
    )
    return (
        back_mel[inverse],
        back_grad[inverse],
        final_first,
        final_mid,
        final_last,
        jnp.stack(gain_grads[: depth - 1]),
        jnp.stack(shift_grads[: depth - 1]),
        gain_grads[depth - 1],
        shift_grads[depth - 1],
    )


def solution(mesh):
    in_specs = (
        P("rep", "dp", None),
        P("rep", "dp", None),
        P(),
        P(),
        P(None, "dp", None),
        P(None, None, "dp", None),
        P(None, "dp", None),
        P(),
        P(),
        P(),
        P(),
    )
    out_specs = (
        P("rep", "dp", None),
        P("rep", "dp", None),
        P(None, "dp", None),
        P(None, None, "dp", None),
        P(None, "dp", None),
        P(),
        P(),
        P(),
        P(),
    )
    step = local_kernel if mesh.shape["dp"] == SUB and mesh.shape["rep"] == CORES else local
    return jax.shard_map(step, mesh=mesh, in_specs=in_specs, out_specs=out_specs, check_vma=False)
```
